128 devices in a mesh: dp: 16 (over x, z_lo, core), ctx: 8 (over y, z_hi).
Axes of the slice: x: 4, y: 4, z: 4 (z_hi: 2, z_lo: 2; z = z_hi * 2 + z_lo), core: 2. Of those that a mesh axis runs over, the one named last changes fastest.
Arguments:
- queries: bfloat16 [16, 1024, 2048], P('dp', 'ctx'), may hold values from -8 to 8
- keys: bfloat16 [16, 1024, 128], P('dp', 'ctx'), may hold values from -8 to 8
- values: bfloat16 [16, 1024, 128], P('dp', 'ctx'), may hold values from -24 to 24
- expert_ids: int32 [16, 1024, 8], P('dp', 'ctx'), may hold values from 0 to 127, all different within a row; in each aligned block of 128 rows (0 to 127, 128 to 255, ..., all dimensions but the last counted through in order) at most 10 rows name the same one
- router_scores: float32 [16, 1024, 8], P('dp', 'ctx'), may hold values from 0.25 to 5
- gate_weight: bfloat16 [128, 2048, 768], P(('dp', 'ctx')), may hold values from -0.125 to 0.125
- up_weight: bfloat16 [128, 2048, 768], P(('dp', 'ctx')), may hold values from -0.125 to 0.125
- down_weight: bfloat16 [128, 768, 2048], P(('dp', 'ctx')), may hold values from -0.21875 to 0.21875
- out_grad: bfloat16 [16, 1024, 2048], P('dp', 'ctx'), may hold values from -6 to 6
Outputs:
- moe_out: bfloat16 [16, 1024, 2048], P('dp', 'ctx')
- query_grad: bfloat16 [16, 1024, 2048], P('dp', 'ctx')
- key_grad: bfloat16 [16, 1024, 128], P('dp', 'ctx')
- value_grad: bfloat16 [16, 1024, 128], P('dp', 'ctx')
- score_grad: float32 [16, 1024, 8], P('dp', 'ctx')
The draws below stay inside these ranges and needn't reach their ends.
Inputs may be any that keep to these rules, and one draw needn't show every extreme that they name: `expert_ids`: the 8 experts of a token are distinct. Among the 128 tokens of one device no expert is picked more than 10 times, and in every draw some expert is picked exactly 10 times by some device's tokens.
All inputs are finite; a program needn't handle non-finite values.
Results may differ from the reference program's by a relative error of at most 0.038.
Values may be sent and summed in bfloat16 or wider, within the bound.
A program may use at most 192 MiB of HBM per device.

```python
import math
import jax
import jax.numpy as jnp
import numpy as np
from jax import lax

D = 2048
QH = 32
KVH = 2
HD = 64
GROUP = 16
FF = 768
TOPK = 8
TOK_DEV = 128
LENGTH = 1024
SEQS = 16
EXPERTS = 128
CAP = 10
N_DP = 16
N_CTX = 8


def draw_queries(key, part):
    own_key = jax.random.fold_in(key, 3)
    return jnp.clip(jax.random.normal(own_key, (SEQS, LENGTH, QH * HD), jnp.float32), -8.0, 8.0).astype(jnp.bfloat16)


def draw_keys(key, part):
    own_key = jax.random.fold_in(key, 5)
    return jnp.clip(jax.random.normal(own_key, (SEQS, LENGTH, KVH * HD), jnp.float32), -8.0, 8.0).astype(jnp.bfloat16)


def draw_values(key, part):
    own_key = jax.random.fold_in(key, 7)
    key_cols, key_rows, key_base = jax.random.split(own_key, 3)
    row_scale = jnp.exp(jax.random.uniform(key_rows, (SEQS, LENGTH, 1), jnp.float32, math.log(0.7), math.log(1.4)))
    column_scale = jnp.exp(jax.random.uniform(key_cols, (KVH * HD,), jnp.float32, math.log(0.4), math.log(2.5)))
    drawn = jnp.clip(jax.random.normal(key_base, (SEQS, LENGTH, KVH * HD), jnp.float32), -4.0, 4.0)
    return (drawn * column_scale[None, None, :] * row_scale).astype(jnp.bfloat16)


def block_scale(key, dims, pieces, low, top_value):
    level, own = 1.0, jax.random.fold_in(key, 6)
    for axis_at, blocks in pieces:
        steps = jnp.exp(jax.random.uniform(jax.random.fold_in(own, axis_at), (blocks,), jnp.float32, low / len(pieces), top_value / len(pieces)))
        level = level * jnp.repeat(steps, dims[axis_at] // blocks).reshape([-1 if axis == axis_at else 1 for axis in range(len(dims))])
    return level


def assign_block(key, own, number, rows, amount, top, bound, lean):
    sequence = jax.random.permutation(key, amount)
    heavy_load, common = load_shares(amount, rows * top, bound, lean, True), load_shares(amount, rows * top, bound, lean, False)
    places = jnp.arange(amount)

    def named(tallies, offset_by):
        used = int((tallies > 0).sum())
        fixed = max(1, used // 4)
        moved = fixed + (places - fixed + offset_by * (used - fixed)) % max(1, amount - fixed)
        return jnp.zeros((amount,), jnp.int32).at[sequence[jnp.where(places < fixed, places, moved)]].set(jnp.asarray(tallies, jnp.int32))

    tallies = jnp.where(number % 4 == 0, named(heavy_load, number // 4), named(common, number - number // 4 - 1))
    mixed = jax.random.permutation(jax.random.fold_in(own, 3), amount)
    giver, receiver = mixed[0:amount // 2 * 2:2], mixed[1:amount // 2 * 2:2]
    margin = jnp.minimum(tallies[giver] - 1, bound - tallies[receiver]) // 2
    margin = jnp.where((giver == sequence[0]) | (receiver == sequence[0]) | (tallies[receiver] == 0), 0, jnp.maximum(margin, 0))
    moved = jax.random.randint(jax.random.fold_in(own, 4), (amount // 2,), 0, 1 << 20) % (margin + 1)
    tallies = tallies.at[giver].add(-moved).at[receiver].add(moved)
    members = jnp.searchsorted(jnp.cumsum(tallies), jnp.arange(rows * top), side="right").astype(jnp.int32)
    table = members.reshape(top, rows).T
    table = table[jax.random.permutation(jax.random.fold_in(own, 1), rows)]
    offset_by = jax.random.randint(jax.random.fold_in(own, 2), (rows, 1), 0, top)
    return jnp.take_along_axis(table, (jnp.arange(top)[None, :] + offset_by) % top, axis=1)


def load_shares(count, total, most, slope, full):
    loads = [(1 << 20) // math.isqrt(rank ** slope) + 1 for rank in range(1, count + 1)]
    largest = most if full else min(most, max(-(-total // count), total * loads[0] // sum(loads)))
    least = 1 if total - largest >= count - 1 else 0
    counts, rest = [largest] + [least] * (count - 1), total - largest - least * (count - 1)
    while rest > 0:
        free = [i for i in range(1, count) if counts[i] < largest] or [i for i in range(1, count) if counts[i] < most]
        pool, remaining = sum([loads[i] for i in free]), rest
        for i in free:
            extra = min(most - counts[i], max(1, remaining * loads[i] // pool), rest)
            counts[i] = counts[i] + extra
            rest = rest - extra
    return np.array(counts)


def centred(key, dims, deviation, most, cuts=(), kind=jnp.bfloat16):
    gain = block_scale(key, dims, cuts, -0.22, 0.18) if cuts else 1.0
    result = jax.random.normal(key, dims, jnp.float32) * deviation * gain
    return jnp.minimum(jnp.maximum(result, -most), most).astype(kind)


def setup_inputs(seed: int = 0) -> dict:
    key_of = jax.random.split(jax.random.key(seed), 10)
    queries = draw_queries(jax.random.fold_in(key_of[9], 71), 0)
    keys = draw_keys(jax.random.fold_in(key_of[9], 71), 0)
    values = draw_values(jax.random.fold_in(key_of[9], 71), 0)
    expert_ids_keys = jax.random.split(jax.random.fold_in(key_of[3], 1), SEQS * LENGTH // TOK_DEV)
    expert_ids_turns = jax.random.permutation(jax.random.fold_in(key_of[3], 3), SEQS * LENGTH // TOK_DEV)
    expert_ids = jax.vmap(lambda own, number: assign_block(jax.random.fold_in(key_of[3], 2), own, number, TOK_DEV, EXPERTS, TOPK, CAP, 2))(expert_ids_keys, expert_ids_turns).reshape((SEQS, LENGTH, TOPK))
    router_scores = jnp.clip(jnp.exp(math.log(5.0) - 2.9957323 * jax.random.uniform(key_of[4], (SEQS, LENGTH, TOPK), jnp.float32) ** block_scale(key_of[4], (SEQS, LENGTH, TOPK), ((0, 16), (1, 8)), -0.2, 0.2)), 0.25, 5.0)
    gate_weight = centred(key_of[5], (EXPERTS, D, FF), D ** -0.5, 0.125, ((0, 128),))
    up_weight = centred(key_of[6], (EXPERTS, D, FF), D ** -0.5, 0.125, ((0, 128),))
    down_weight = centred(key_of[7], (EXPERTS, FF, D), FF ** -0.5, 0.21875, ((0, 128),))
    out_grad = centred(key_of[8], (SEQS, LENGTH, D), 1.0, 6.0, ((0, 16), (1, 8)))
    return dict(queries=queries, keys=keys, values=values, expert_ids=expert_ids, router_scores=router_scores, gate_weight=gate_weight, up_weight=up_weight, down_weight=down_weight, out_grad=out_grad)


EPSILON = 1e-06
NEGATIVE = -1e+30

def causal_allowed():
    position = jnp.arange(LENGTH, dtype=jnp.int32)
    return position[None, :] <= position[:, None]

def head_scores(query_head, key_head):
    scores = jnp.dot(query_head, key_head.T, preferred_element_type=jnp.float32) * HD ** (-0.5)
    return jnp.where(causal_allowed(), scores, NEGATIVE)

def head_forward(operands):
    query_head, key_head, value_head = operands
    allowed = causal_allowed()
    scores = head_scores(query_head, key_head)
    row_max = lax.optimization_barrier(jnp.max(scores, axis=1, keepdims=True))
    exp_scores = jnp.where(allowed, jnp.exp(scores - row_max), 0.0)
    row_sum = lax.optimization_barrier(jnp.sum(exp_scores, axis=1, keepdims=True))
    soft_weights = (exp_scores / row_sum).astype(jnp.bfloat16)
    head_out = jnp.dot(soft_weights, value_head, preferred_element_type=jnp.float32)
    return (head_out, (row_max + jnp.log(row_sum))[:, 0])

def head_backward(operands):
    query_head, key_head, value_head, out_head, grad_head, log_total = operands
    allowed = causal_allowed()
    scores = head_scores(query_head, key_head)
    soft_weights = jnp.where(allowed, jnp.exp(scores - log_total[:, None]), 0.0)
    value_part = jnp.dot(soft_weights.astype(jnp.bfloat16).T, grad_head, preferred_element_type=jnp.float32)
    prob_grad = jnp.dot(grad_head, value_head.T, preferred_element_type=jnp.float32)
    row_delta = lax.optimization_barrier(jnp.sum(grad_head.astype(jnp.float32) * out_head.astype(jnp.float32), axis=1, keepdims=True))
    score_grads = (soft_weights * (prob_grad - row_delta) * HD ** (-0.5)).astype(jnp.bfloat16)
    query_part = jnp.dot(score_grads, key_head, preferred_element_type=jnp.float32)
    key_part = jnp.dot(score_grads.T, query_head, preferred_element_type=jnp.float32)
    return (query_part, key_part, value_part)

def split_heads(matrix, heads):
    return matrix.reshape(LENGTH, heads, HD).transpose(1, 0, 2)

def join_heads(stack):
    return stack.transpose(1, 0, 2).reshape(LENGTH, stack.shape[0] * HD)

def attend(operands):
    query_seq, key_seq, value_seq = operands
    query_heads = split_heads(query_seq, QH)
    key_heads = jnp.repeat(split_heads(key_seq, KVH), GROUP, axis=0)
    value_heads = jnp.repeat(split_heads(value_seq, KVH), GROUP, axis=0)
    head_out, log_total = lax.map(head_forward, (query_heads, key_heads, value_heads))
    return (join_heads(head_out).astype(jnp.bfloat16), log_total)

def attend_backward(operands):
    query_seq, key_seq, value_seq, out_seq, grad_seq, log_total = operands
    query_heads = split_heads(query_seq, QH)
    key_heads = jnp.repeat(split_heads(key_seq, KVH), GROUP, axis=0)
    value_heads = jnp.repeat(split_heads(value_seq, KVH), GROUP, axis=0)
    out_heads = split_heads(out_seq, QH)
    grad_heads = split_heads(grad_seq, QH)
    query_part, key_part, value_part = lax.map(head_backward, (query_heads, key_heads, value_heads, out_heads, grad_heads, log_total))
    query_grad = join_heads(query_part).astype(jnp.bfloat16)
    key_grad = join_heads(key_part.reshape(KVH, GROUP, LENGTH, HD).sum(axis=1)).astype(jnp.bfloat16)
    value_grad = join_heads(value_part.reshape(KVH, GROUP, LENGTH, HD).sum(axis=1)).astype(jnp.bfloat16)
    return (query_grad, key_grad, value_grad)

def routing_table(expert_ids):
    devices = N_DP * N_CTX
    picks = expert_ids.reshape(devices, TOK_DEV * TOPK)
    onehot = (picks[:, :, None] == jnp.arange(EXPERTS, dtype=jnp.int32)[None, None, :]).astype(jnp.int32)
    slot_index = lax.optimization_barrier(jnp.sum(jnp.cumsum(onehot, axis=1) * onehot, axis=2)) - 1
    source = jnp.arange(devices, dtype=jnp.int32)[:, None]
    placed = picks * (devices * CAP) + source * CAP + slot_index
    pick_count = SEQS * LENGTH * TOPK
    table = jnp.full((EXPERTS * devices * CAP,), pick_count, jnp.int32)
    table = table.at[placed.reshape(-1)].set(jnp.arange(pick_count, dtype=jnp.int32))
    return table.reshape(EXPERTS, devices * CAP)

def reference(queries, keys, values, expert_ids, router_scores, gate_weight, up_weight, down_weight, out_grad):
    attn_out, log_total = lax.map(attend, (queries, keys, values))
    token_count = SEQS * LENGTH
    pick_count = token_count * TOPK
    attn_wide = attn_out.reshape(token_count, D).astype(jnp.float32)
    inv_rms = lax.rsqrt(lax.optimization_barrier(jnp.mean(attn_wide * attn_wide, axis=1, keepdims=True)) + EPSILON)
    normed = (attn_wide * inv_rms).astype(jnp.bfloat16)
    scores_flat = router_scores.reshape(token_count, TOPK)
    score_total = lax.optimization_barrier(jnp.sum(scores_flat, axis=1, keepdims=True))
    mixing = scores_flat / score_total
    grad_flat = out_grad.reshape(token_count, D)
    table = routing_table(expert_ids)
    normed_pad = jnp.concatenate([normed, jnp.zeros((1, D), jnp.bfloat16)])
    grad_pad = jnp.concatenate([grad_flat, jnp.zeros((1, D), jnp.bfloat16)])
    mixing_pad = jnp.concatenate([mixing.reshape(-1), jnp.zeros((1,), jnp.float32)])

    def expert_step(running, operands):
        mixed_sum, normed_sum, weight_sum = running
        picks, w_gate, w_up, w_down = operands
        tokens = picks // TOPK
        flat_rows = normed_pad[tokens]
        gate_act = jnp.dot(flat_rows, w_gate, preferred_element_type=jnp.float32)
        up_act = jnp.dot(flat_rows, w_up, preferred_element_type=jnp.float32)
        sigmoid_gate = jax.nn.sigmoid(gate_act)
        hidden = (gate_act * sigmoid_gate * up_act).astype(jnp.bfloat16)
        expert_out = jnp.dot(hidden, w_down, preferred_element_type=jnp.float32).astype(jnp.bfloat16)
        share = mixing_pad[picks][:, None]
        grad_rows = grad_pad[tokens]
        weight_part = lax.optimization_barrier(jnp.sum(grad_rows.astype(jnp.float32) * expert_out.astype(jnp.float32), axis=1))
        sent_grad = (share * grad_rows.astype(jnp.float32)).astype(jnp.bfloat16)
        hidden_grad = jnp.dot(sent_grad, w_down.T, preferred_element_type=jnp.float32)
        gate_grad = (hidden_grad * up_act * sigmoid_gate * (1.0 + gate_act * (1.0 - sigmoid_gate))).astype(jnp.bfloat16)
        up_grad = (hidden_grad * gate_act * sigmoid_gate).astype(jnp.bfloat16)
        row_grad = (jnp.dot(gate_grad, w_gate.T, preferred_element_type=jnp.float32) + jnp.dot(up_grad, w_up.T, preferred_element_type=jnp.float32)).astype(jnp.bfloat16)
        mixed_sum = mixed_sum.at[tokens].add(share * expert_out.astype(jnp.float32))
        normed_sum = normed_sum.at[tokens].add(row_grad.astype(jnp.float32))
        weight_sum = weight_sum.at[picks].add(weight_part)
        return ((mixed_sum, normed_sum, weight_sum), None)
    start_state = (jnp.zeros((token_count + 1, D), jnp.float32), jnp.zeros((token_count + 1, D), jnp.float32), jnp.zeros((pick_count + 1,), jnp.float32))
    final_state, unused = lax.scan(expert_step, start_state, (table, gate_weight, up_weight, down_weight))
    mixed_sum, normed_sum, weight_sum = final_state
    moe_out = mixed_sum[:token_count].astype(jnp.bfloat16).reshape(SEQS, LENGTH, D)
    weight_grad = weight_sum[:pick_count].reshape(token_count, TOPK)
    score_grad = (weight_grad - lax.optimization_barrier(jnp.sum(mixing * weight_grad, axis=1, keepdims=True))) / score_total
    normed_grad = normed_sum[:token_count]
    attn_grad = (inv_rms * normed_grad - inv_rms ** 3 * attn_wide * lax.optimization_barrier(jnp.mean(normed_grad * attn_wide, axis=1, keepdims=True))).astype(jnp.bfloat16)
    query_grad, key_grad, value_grad = lax.map(attend_backward, (queries, keys, values, attn_out, attn_grad.reshape(SEQS, LENGTH, D), log_total))
    return (moe_out, query_grad, key_grad, value_grad, score_grad.reshape(SEQS, LENGTH, TOPK))
```

```python
import functools

import jax
import jax.numpy as jnp
from jax import lax
from jax.experimental import pallas as pl
from jax.experimental.pallas import tpu as pltpu
from jax.sharding import PartitionSpec as P

KVH = 2
HD = 64
GROUP = 16
TOPK = 8


EPSILON = 1e-06
NEGATIVE = -1e30


MESH = pl.DeviceIdType.MESH
CHUNK_ROWS = 16


def offset_target(step, x, y, z, core, sign):
    inner = step % 64
    a, b, c = inner // 16, (inner // 4) % 4, inner % 4
    dx = c
    dy = (c + b) % 4
    dz = (c + a + 2 * b) % 4
    tx = (x + sign * dx + 4) % 4
    ty = (y + sign * dy + 4) % 4
    tz = (z + sign * dz + 4) % 4
    tcore = (core + step // 64) % 2
    return tx * 4 + (tz % 2) * 2 + tcore, ty * 2 + tz // 2


def exchange_kernel(count, src, dst, send_sem, recv_sem, own_sem):
    dp, ctx = lax.axis_index("dp"), lax.axis_index("ctx")
    x, core = dp // 4, dp % 2
    y, z = ctx // 2, (dp // 2) % 2 + 2 * (ctx % 2)
    sign = 1 - 2 * core
    me = dp * 8 + ctx
    barrier = pltpu.get_barrier_semaphore()

    def greet(step, carry):
        tdp, tctx = offset_target(step, x, y, z, core, sign)
        pl.semaphore_signal(barrier, inc=1, device_id=(tdp, tctx), device_id_type=MESH)
        return carry

    lax.fori_loop(1, count, greet, 0)
    pl.semaphore_wait(barrier, count - 1)
    own = pltpu.make_async_copy(src.at[me], dst.at[me], own_sem)
    own.start()

    def send(step, carry):
        tdp, tctx = offset_target(step, x, y, z, core, sign)
        pltpu.make_async_remote_copy(
            src_ref=src.at[tdp * 8 + tctx],
            dst_ref=dst.at[me],
            send_sem=send_sem,
            recv_sem=recv_sem,
            device_id=(tdp, tctx),
            device_id_type=MESH,
        ).start()
        return carry

    lax.fori_loop(1, count, send, 0)
    tdp, tctx = offset_target(1, x, y, z, core, sign)
    everything = pltpu.make_async_remote_copy(
        src_ref=src.at[pl.ds(0, count - 1)],
        dst_ref=dst.at[pl.ds(0, count - 1)],
        send_sem=send_sem,
        recv_sem=recv_sem,
        device_id=(tdp, tctx),
        device_id_type=MESH,
    )
    everything.wait()
    own.wait()


def exchange(rows, number):
    count = rows.shape[0]
    size = rows.shape[1] * rows.shape[2]
    flat = rows.reshape(count, CHUNK_ROWS, size // CHUNK_ROWS)
    out = pl.pallas_call(
        functools.partial(exchange_kernel, count),
        out_shape=jax.ShapeDtypeStruct(flat.shape, flat.dtype),
        in_specs=[pl.BlockSpec(memory_space=pl.ANY)],
        out_specs=pl.BlockSpec(memory_space=pl.ANY),
        scratch_shapes=[pltpu.SemaphoreType.DMA] * 3,
        compiler_params=pltpu.CompilerParams(collective_id=number, has_side_effects=True),
        name="exchange_%d" % number,
    )(flat)
    return out.reshape(rows.shape)


def shards(
    queries, keys, values, expert_ids, router_scores, gate_weight, up_weight, down_weight, out_grad
):
    rows_here = queries.shape[1]
    model_width = queries.shape[2]
    pair_width = keys.shape[2]
    score_scale = HD ** (-0.5)
    local_queries = queries[0]
    query_pos = lax.axis_index("ctx") * rows_here + jnp.arange(rows_here, dtype=jnp.int32)
    query_sets = [
        local_queries[:, head_set * GROUP * HD : (head_set + 1) * GROUP * HD].reshape(
            rows_here, GROUP, HD
        )
        for head_set in range(KVH)
    ]
    running_max = jnp.full((GROUP * KVH, rows_here), NEGATIVE, jnp.float32)
    weighted = jnp.zeros((rows_here, model_width), jnp.float32)
    block_keys = lax.all_gather(keys, "ctx", axis=1, tiled=True)[0]
    block_values = lax.all_gather(values, "ctx", axis=1, tiled=True)[0]
    block_rows = block_keys.shape[0]
    key_pos = jnp.arange(block_rows, dtype=jnp.int32)
    allowed = (key_pos[None, :] <= query_pos[:, None])[None]
    new_maxes = []
    new_sums = []
    new_weighted = []
    for fold_head_set in range(KVH):
        fold_head_cols = slice(fold_head_set * HD, (fold_head_set + 1) * HD)
        fold_scores = (
            jnp.einsum(
                "thd,sd->hts",
                query_sets[fold_head_set],
                block_keys[:, fold_head_cols],
                preferred_element_type=jnp.float32,
            )
            * score_scale
        )
        fold_scores = jnp.where(allowed, fold_scores, NEGATIVE)
        old_max = running_max[fold_head_set * GROUP : (fold_head_set + 1) * GROUP]
        new_max = jnp.maximum(old_max, jnp.max(fold_scores, axis=2))
        exp_scores = jnp.where(allowed, jnp.exp(fold_scores - new_max[:, :, None]), 0.0)
        shrink = jnp.exp(old_max - new_max)
        new_maxes.append(new_max)
        new_sums.append(jnp.sum(exp_scores, axis=2))
        update = jnp.einsum(
            "hts,sd->thd",
            exp_scores.astype(jnp.bfloat16),
            block_values[:, fold_head_cols],
            preferred_element_type=jnp.float32,
        )
        previous = weighted[
            :, fold_head_set * GROUP * HD : (fold_head_set + 1) * GROUP * HD
        ].reshape(rows_here, GROUP, HD)
        new_weighted.append(
            (previous * shrink.T[:, :, None] + update).reshape(rows_here, GROUP * HD)
        )
    running_max = jnp.concatenate(new_maxes)
    running_sum = jnp.concatenate(new_sums)
    weighted = jnp.concatenate(new_weighted, axis=1)
    all_keys, all_values = (
        lax.all_gather(keys, "ctx", axis=1, tiled=True),
        lax.all_gather(values, "ctx", axis=1, tiled=True),
    )
    attn_out = (
        (weighted.reshape(rows_here, GROUP * KVH, HD) / running_sum.T[:, :, None])
        .reshape(rows_here, model_width)
        .astype(jnp.bfloat16)
    )
    log_total = running_max + jnp.log(running_sum)
    attn_wide = attn_out.astype(jnp.float32)
    inv_rms = lax.rsqrt(jnp.mean(attn_wide * attn_wide, axis=1, keepdims=True) + EPSILON)
    normed = (attn_wide * inv_rms).astype(jnp.bfloat16)
    dp_count = lax.axis_size("dp")
    ctx_count = lax.axis_size("ctx")
    experts = dp_count * ctx_count
    capacity = 10 * rows_here * TOPK // (8 * experts)
    expert_picks = expert_ids[0].reshape(-1)
    pick_count = expert_picks.shape[0]
    onehot = (expert_picks[:, None] == jnp.arange(experts, dtype=jnp.int32)[None, :]).astype(
        jnp.int32
    )
    slot_index = jnp.sum(jnp.cumsum(onehot, axis=0) * onehot, axis=1) - 1
    placed = expert_picks * capacity + slot_index
    slot_pick = (
        jnp.full((experts * capacity,), pick_count, jnp.int32)
        .at[placed]
        .set(jnp.arange(pick_count, dtype=jnp.int32))
    )
    slot_token = slot_pick // TOPK
    normed_pad = jnp.concatenate([normed, jnp.zeros((1, model_width), jnp.bfloat16)])
    outgoing = normed_pad[slot_token].reshape(experts, capacity, model_width)
    w_gate = gate_weight[0]
    w_up = up_weight[0]
    w_down = down_weight[0]
    arrived_rows = exchange(outgoing, 0)
    sources = arrived_rows.shape[0]
    slots = arrived_rows.shape[1]
    flat_rows = arrived_rows.reshape(sources * slots, model_width)
    expert_gate_act = jnp.dot(flat_rows, w_gate, preferred_element_type=jnp.float32)
    expert_up_act = jnp.dot(flat_rows, w_up, preferred_element_type=jnp.float32)
    hidden = (expert_gate_act * jax.nn.sigmoid(expert_gate_act) * expert_up_act).astype(
        jnp.bfloat16
    )
    produced = jnp.dot(hidden, w_down, preferred_element_type=jnp.float32).astype(jnp.bfloat16)
    produced, gate_act, up_act = (
        produced.reshape(sources, slots, model_width),
        expert_gate_act.reshape(sources, slots, -1),
        expert_up_act.reshape(sources, slots, -1),
    )
    returned = exchange(produced, 1)
    pick_out = returned.reshape(experts * capacity, model_width)[placed].reshape(
        rows_here, TOPK, model_width
    )
    raw_scores = router_scores[0]
    score_total = jnp.sum(raw_scores, axis=1, keepdims=True)
    mixing = raw_scores / score_total
    mixed = jnp.sum(mixing[:, :, None] * pick_out.astype(jnp.float32), axis=1)
    moe_out = mixed.astype(jnp.bfloat16)[None]
    grad_rows = out_grad[0]
    weight_grad = jnp.einsum("td,tkd->tk", grad_rows, pick_out, preferred_element_type=jnp.float32)
    score_grad = (weight_grad - jnp.sum(mixing * weight_grad, axis=1, keepdims=True)) / score_total
    mixing_pad = jnp.concatenate([mixing.reshape(-1), jnp.zeros((1,), jnp.float32)])
    grad_pad = jnp.concatenate([grad_rows, jnp.zeros((1, model_width), jnp.bfloat16)])
    grad_sent = (
        (mixing_pad[slot_pick][:, None] * grad_pad[slot_token].astype(jnp.float32))
        .astype(jnp.bfloat16)
        .reshape(experts, capacity, model_width)
    )
    arrived_grad = exchange(grad_sent, 2)
    flat_grad = arrived_grad.reshape(-1, model_width)
    gate_flat = gate_act.reshape(flat_grad.shape[0], -1)
    up_flat = up_act.reshape(flat_grad.shape[0], -1)
    hidden_grad = jnp.dot(flat_grad, w_down.T, preferred_element_type=jnp.float32)
    sigmoid_gate = jax.nn.sigmoid(gate_flat)
    gate_grad = (
        hidden_grad * up_flat * sigmoid_gate * (1.0 + gate_flat * (1.0 - sigmoid_gate))
    ).astype(jnp.bfloat16)
    up_grad = (hidden_grad * gate_flat * sigmoid_gate).astype(jnp.bfloat16)
    row_grad = jnp.dot(gate_grad, w_gate.T, preferred_element_type=jnp.float32) + jnp.dot(
        up_grad, w_up.T, preferred_element_type=jnp.float32
    )
    returned_grad = exchange(row_grad.astype(jnp.bfloat16).reshape(arrived_grad.shape), 3)
    normed_grad = jnp.sum(
        returned_grad.reshape(experts * capacity, model_width)[placed]
        .reshape(rows_here, TOPK, model_width)
        .astype(jnp.float32),
        axis=1,
    )
    attn_grad = (
        inv_rms * normed_grad
        - inv_rms**3 * attn_wide * jnp.mean(normed_grad * attn_wide, axis=1, keepdims=True)
    ).astype(jnp.bfloat16)
    full_keys = all_keys[0]
    full_values = all_values[0]
    full_pos = jnp.arange(full_keys.shape[0], dtype=jnp.int32)
    allowed_full = (full_pos[None, :] <= query_pos[:, None])[None]
    query_parts, score_sets, weight_sets, grad_sets = ([], [], [], [])
    for head_set in range(KVH):
        head_cols = slice(head_set * HD, (head_set + 1) * HD)
        group_cols = slice(head_set * GROUP * HD, (head_set + 1) * GROUP * HD)
        key_set = full_keys[:, head_cols]
        scores = (
            jnp.einsum(
                "thd,sd->hts", query_sets[head_set], key_set, preferred_element_type=jnp.float32
            )
            * score_scale
        )
        soft_weights = jnp.where(
            allowed_full,
            jnp.exp(scores - log_total[head_set * GROUP : (head_set + 1) * GROUP][:, :, None]),
            0.0,
        )
        grad_set = attn_grad[:, group_cols].reshape(rows_here, GROUP, HD)
        out_set = attn_out[:, group_cols].reshape(rows_here, GROUP, HD)
        row_delta = jnp.sum(grad_set.astype(jnp.float32) * out_set.astype(jnp.float32), axis=2).T
        prob_grad = jnp.einsum(
            "thd,sd->hts", grad_set, full_values[:, head_cols], preferred_element_type=jnp.float32
        )
        score_grads = (soft_weights * (prob_grad - row_delta[:, :, None]) * score_scale).astype(
            jnp.bfloat16
        )
        query_parts.append(
            jnp.einsum(
                "hts,sd->thd", score_grads, key_set, preferred_element_type=jnp.float32
            ).reshape(rows_here, GROUP * HD)
        )
        score_sets.append(score_grads)
        weight_sets.append(soft_weights.astype(jnp.bfloat16))
        grad_sets.append(grad_set)
    query_grad = jnp.concatenate(query_parts, axis=1).astype(jnp.bfloat16)[None]
    key_parts = []
    value_parts = []
    for head_set in range(KVH):
        score_slice = score_sets[head_set]
        weight_slice = weight_sets[head_set]
        key_parts.append(
            jnp.einsum(
                "hts,thd->sd", score_slice, query_sets[head_set], preferred_element_type=jnp.float32
            )
        )
        value_parts.append(
            jnp.einsum(
                "hts,thd->sd", weight_slice, grad_sets[head_set], preferred_element_type=jnp.float32
            )
        )
    pair_grad = lax.psum_scatter(
        jnp.concatenate(key_parts + value_parts, axis=1), "ctx", scatter_dimension=0, tiled=True
    )
    key_grad = pair_grad[:, :pair_width].astype(jnp.bfloat16)[None]
    value_grad = pair_grad[:, pair_width:].astype(jnp.bfloat16)[None]
    return (moe_out, query_grad, key_grad, value_grad, score_grad[None])


def solution(mesh):
    placed = (
        P("dp", "ctx", None),
        P("dp", "ctx", None),
        P("dp", "ctx", None),
        P("dp", "ctx", None),
        P("dp", "ctx", None),
        P(("dp", "ctx"), None, None),
        P(("dp", "ctx"), None, None),
        P(("dp", "ctx"), None, None),
        P("dp", "ctx", None),
    )
    return jax.shard_map(
        shards,
        mesh=mesh,
        in_specs=placed,
        out_specs=(
            P("dp", "ctx", None),
            P("dp", "ctx", None),
            P("dp", "ctx", None),
            P("dp", "ctx", None),
            P("dp", "ctx", None),
        ),
        check_vma=False,
    )
```

```python
import functools

import jax
import jax.numpy as jnp
from jax import lax
from jax.experimental import pallas as pl
from jax.experimental.pallas import tpu as pltpu
from jax.sharding import PartitionSpec as P

HD = 64
EPSILON = 1e-06
NEGATIVE = -1e30
MESH = pl.DeviceIdType.MESH
F32 = jnp.float32
BF16 = jnp.bfloat16

ROWS = 16
MAIN = 1024
SPILL = 256
CHUNK = MAIN + SPILL
BLOCK = 16
PAIR = 128


def dot(a, b):
    return lax.dot_general(a, b, (((1,), (0,)), ((), ())), preferred_element_type=F32)


def dot_nt(a, b):
    return lax.dot_general(a, b, (((1,), (1,)), ((), ())), preferred_element_type=F32)


def iota(shape, dim):
    return lax.broadcasted_iota(jnp.int32, shape, dim)


def torus_partner(step, x, y, z, core, sign):
    inner = step % 64
    a, b, c = inner // 16, (inner // 4) % 4, inner % 4
    dx = c
    dy = (c + b) % 4
    dz = (c + a + 2 * b) % 4
    tx = (x + sign * dx + 4) % 4
    ty = (y + sign * dy + 4) % 4
    tz = (z + sign * dz + 4) % 4
    tcore = (core + step // 64) % 2
    return tx * 4 + (tz % 2) * 2 + tcore, ty * 2 + tz // 2


def partners(n_dp, n_ctx):
    dp, ctx = lax.axis_index("dp"), lax.axis_index("ctx")
    count = n_dp * n_ctx
    if (n_dp, n_ctx) == (16, 8):
        x, core = dp // 4, dp % 2
        y, z = ctx // 2, (dp // 2) % 2 + 2 * (ctx % 2)
        sign = 1 - 2 * core

        def target(step):
            return torus_partner(step, x, y, z, core, sign)

        def source(step):
            other = 1 - 2 * (step // 64)
            return torus_partner(step, x, y, z, core, -sign * other)

        return target, source
    me = dp * n_ctx + ctx

    def target(step):
        t = (me + step) % count
        return t // n_ctx, t % n_ctx

    def source(step):
        t = (me - step + count) % count
        return t // n_ctx, t % n_ctx

    return target, source


def layer_kernel(
    n_dp,
    n_ctx,
    group,
    ids,
    raw,
    queries,
    keys,
    values,
    out_grad,
    gate_hbm,
    up_hbm,
    down_hbm,
    moe_out,
    query_grad,
    key_grad,
    value_grad,
    score_grad,
    w_gate,
    w_up,
    w_down,
    grad_out,
    grad_in,
    row_out,
    row_in,
    back_rows,
    back_outs,
    canon_x,
    canon_g,
    halves,
    rank_et,
    mix_main,
    mix_spill,
    all_keys,
    all_values,
    key_dup,
    value_dup,
    key_dup_t,
    value_dup_t,
    bias,
    attn,
    log_total,
    wide,
    pick_et,
    key_acc,
    value_acc,
    pair_part,
    pair_in,
    w_sem,
    kv_send,
    kv_recv,
    g_send,
    g_recv,
    x_send,
    x_recv,
    r_send,
    r_recv,
    y_send,
    y_recv,
    p_send,
    p_recv,
):
    count = n_dp * n_ctx
    groups = count // group
    tokens = queries.shape[0]
    width = queries.shape[1]
    pairs = width // PAIR
    per_kv = pairs // 2
    length = n_ctx * tokens
    dp, ctx = lax.axis_index("dp"), lax.axis_index("ctx")
    me = dp * n_ctx + ctx
    target, source = partners(n_dp, n_ctx)
    neighbour = target(1)

    weight_copies = [
        pltpu.make_async_copy(src, dst, w_sem.at[n])
        for n, (src, dst) in enumerate(((gate_hbm, w_gate), (up_hbm, w_up), (down_hbm, w_down)))
    ]
    for copy in weight_copies:
        copy.start()

    barrier = pltpu.get_barrier_semaphore()

    def greet(step, carry):
        pl.semaphore_signal(barrier, inc=1, device_id=target(step), device_id_type=MESH)
        return carry

    lax.fori_loop(1, count, greet, 0)

    expert_row = iota((count, tokens), 0)
    scores_t = raw[...]
    total_t = jnp.sum(scores_t, axis=0, keepdims=True)
    mixing_t = scores_t / total_t
    named = jnp.zeros((count, tokens), F32)
    mix_et = jnp.zeros((count, tokens), F32)
    for k in range(ids.shape[0]):
        hit = expert_row == ids[k : k + 1, :]
        named = named + jnp.where(hit, 1.0, 0.0)
        mix_et = mix_et + jnp.where(hit, mixing_t[k : k + 1, :], 0.0)
    before = jnp.where(iota((tokens, tokens), 0) < iota((tokens, tokens), 1), 1.0, 0.0)
    rank = dot(named.astype(BF16), before.astype(BF16))
    rank = jnp.where(named > 0.0, rank, -1.0)
    rank_et[...] = rank

    spread = jnp.where(
        iota((count, count * ROWS), 0) == iota((count, count * ROWS), 1) // ROWS, 1.0, 0.0
    ).astype(BF16)
    lane_row = iota((tokens, count * ROWS), 1) % ROWS
    rank_wide = dot(rank.T.astype(BF16), spread)
    mix_wide = dot(mix_et.T.astype(BF16), spread)
    slot_main = (lane_row % 8).astype(F32)
    slot_spill = (8 + lane_row % 2).astype(F32)
    main_mix = jnp.where(rank_wide == slot_main, mix_wide, 0.0)
    mix_main[0:tokens, :] = jnp.where(lane_row < 8, main_mix, 0.0).astype(BF16)
    mix_main[tokens:, :] = jnp.where(lane_row >= 8, main_mix, 0.0).astype(BF16)
    mix_spill[...] = jnp.where(rank_wide == slot_spill, mix_wide, 0.0).astype(BF16)

    p_out, p_in = iota((256, 256), 0), iota((256, 256), 1)
    to_blocks = jnp.where(
        (p_out // 32 == (p_in % 16) // 2)
        & ((p_out % 32) // 2 == p_in // 16)
        & (p_out % 2 == p_in % 2),
        1.0,
        0.0,
    ).astype(BF16)
    to_chunks = jnp.where(
        (p_in // 32 == (p_out % 16) // 2)
        & ((p_in % 32) // 2 == p_out // 16)
        & (p_out % 2 == p_in % 2),
        1.0,
        0.0,
    ).astype(BF16)
    repeat_main = jnp.where(iota((256, BLOCK), 0) // ROWS == iota((256, BLOCK), 1), 1.0, 0.0).astype(BF16)
    repeat_spill = jnp.where(iota((32, BLOCK), 0) // 2 == iota((32, BLOCK), 1), 1.0, 0.0).astype(BF16)

    def ranks_of(block):
        rows = rank_et[pl.ds(pl.multiple_of(block * BLOCK, BLOCK), BLOCK), :]
        return rows.astype(BF16)

    def pack_rows(dst):
        def body(block, carry):
            ranks = ranks_of(block)
            wide_rank = dot(repeat_main, ranks)
            row = iota((256, tokens), 0) % ROWS
            hit = wide_rank == (row % 8).astype(F32)
            left = jnp.where(hit & (row < 8), 1.0, 0.0).astype(BF16)
            right = jnp.where(hit & (row >= 8), 1.0, 0.0).astype(BF16)
            first = pl.ds(pl.multiple_of(block * BLOCK, BLOCK), BLOCK)
            main = dot(jnp.concatenate([left, right], axis=1), halves[...])
            dst[first, :, 0:MAIN] = main.astype(BF16).reshape(BLOCK, ROWS, MAIN)
            spill_rank = dot(repeat_spill, ranks)
            spill_slot = (8 + iota((32, tokens), 0) % 2).astype(F32)
            spill_hit = jnp.where(spill_rank == spill_slot, 1.0, 0.0).astype(BF16)
            rows = [
                dot(spill_hit, halves[0:tokens, :]).astype(BF16),
                dot(spill_hit, halves[tokens:, :]).astype(BF16),
            ]
            dst[first, :, MAIN:] = spill_to_chunk(rows)
            return carry

        lax.fori_loop(0, count // BLOCK, body, 0)

    def spill_to_chunk(rows):
        stacked = jnp.concatenate(
            [part[:, c * SPILL : (c + 1) * SPILL] for part in rows for c in range(4)], axis=0
        )
        return dot(to_chunks, stacked).astype(BF16).reshape(BLOCK, ROWS, SPILL)

    def send_out(src, dst, send_sem, recv_sem):
        own = pltpu.make_async_copy(src.at[me], dst.at[0], recv_sem.at[0])
        own.start()

        def body(step, carry):
            tdp, tctx = target(step)
            pltpu.make_async_remote_copy(
                src_ref=src.at[tdp * n_ctx + tctx],
                dst_ref=dst.at[step],
                send_sem=send_sem,
                recv_sem=recv_sem.at[step // group],
                device_id=(tdp, tctx),
                device_id_type=MESH,
            ).start()
            return carry

        lax.fori_loop(1, count, body, 0)

    def send_back(src, dst, send_sem, recv_sem, lo, hi):
        def body(step, carry):
            pltpu.make_async_remote_copy(
                src_ref=src.at[step],
                dst_ref=dst.at[me],
                send_sem=send_sem,
                recv_sem=recv_sem,
                device_id=source(step),
                device_id_type=MESH,
            ).start()
            return carry

        lax.fori_loop(lo, hi, body, 0)

    def bytes_of(ref, amount, sem_a, sem_b):
        part = ref.at[pl.ds(0, amount)]
        return pltpu.make_async_remote_copy(
            src_ref=part,
            dst_ref=part,
            send_sem=sem_a,
            recv_sem=sem_b,
            device_id=neighbour,
            device_id_type=MESH,
        )

    halves[0:tokens, :] = out_grad[:, 0:MAIN]
    halves[tokens:, :] = out_grad[:, MAIN:]
    pack_rows(grad_out)

    pl.semaphore_wait(barrier, count - 1)
    here = pl.ds(pl.multiple_of(ctx * tokens, tokens), tokens)
    all_keys[here, :] = keys[...]
    all_values[here, :] = values[...]

    def send_pair(j, carry):
        peer = (dp, (ctx + j) % n_ctx)
        for n, (src, dst) in enumerate(((keys, all_keys), (values, all_values))):
            pltpu.make_async_remote_copy(
                src_ref=src,
                dst_ref=dst.at[here],
                send_sem=kv_send.at[n],
                recv_sem=kv_recv.at[n],
                device_id=peer,
                device_id_type=MESH,
            ).start()
        return carry

    lax.fori_loop(1, n_ctx, send_pair, 0)
    send_out(grad_out, grad_in, g_send, g_recv)

    key_at = iota((length, 2 * tokens), 0)
    query_at = ctx * tokens + iota((length, 2 * tokens), 1) % tokens
    bias[...] = jnp.where(key_at <= query_at, 0.0, NEGATIVE)
    for n, ref in enumerate((all_keys, all_values)):
        pair_wait = bytes_of(ref, (n_ctx - 1) * tokens, kv_send.at[n], kv_recv.at[n])
        pair_wait.wait()
    for g in range(2):
        select = jnp.where(
            iota((PAIR, PAIR), 0) == g * HD + iota((PAIR, PAIR), 1) % HD, 1.0, 0.0
        ).astype(BF16)
        select_t = jnp.where(
            iota((PAIR, PAIR), 1) == g * HD + iota((PAIR, PAIR), 0) % HD, 1.0, 0.0
        ).astype(BF16)
        key_dup[g] = dot(all_keys[...], select).astype(BF16)
        value_dup[g] = dot(all_values[...], select).astype(BF16)
        key_dup_t[g] = dot_nt(select_t, all_keys[...]).astype(BF16)
        value_dup_t[g] = dot_nt(select_t, all_values[...]).astype(BF16)

    low = iota((tokens, PAIR), 1) < HD

    def two_heads(rows):
        return jnp.concatenate(
            [jnp.where(low, rows, 0.0), jnp.where(low, 0.0, rows)], axis=0
        ).astype(BF16)

    def join_heads(both_t):
        both = both_t.T
        return jnp.where(low, both[0:tokens], both[tokens:])

    def columns(p):
        return pl.ds(pl.multiple_of(p * PAIR, PAIR), PAIR)

    scale = HD**-0.5

    def forward(p, carry):
        g = p // per_kv
        query = two_heads(queries[:, columns(p)].astype(F32) * scale)
        scores = dot_nt(key_dup[g], query) + bias[...]
        top = jnp.max(scores, axis=0, keepdims=True)
        weights = jnp.exp(scores - top)
        total = jnp.sum(weights, axis=0, keepdims=True)
        out_t = dot(value_dup_t[g], weights.astype(BF16)) / total
        attn[:, columns(p)] = join_heads(out_t).astype(BF16)
        log_total[p] = top + jnp.log(total)
        return carry

    lax.fori_loop(0, pairs, forward, 0)

    attn_wide = attn[...].astype(F32)
    inv_rms = lax.rsqrt(jnp.mean(attn_wide * attn_wide, axis=1, keepdims=True) + EPSILON)
    normed = (attn_wide * inv_rms).astype(BF16)
    halves[0:tokens, :] = normed[:, 0:MAIN]
    halves[tokens:, :] = normed[:, MAIN:]
    pack_rows(row_out)
    send_out(row_out, row_in, x_send, x_recv)
    for copy in weight_copies:
        copy.wait()

    main_rows = group * 8

    def unpack(buf, start, canon):
        def body(j, carry):
            both = buf[pl.ds(start + 2 * j, 2), :, 0:MAIN].astype(F32)
            at = pl.ds(pl.multiple_of(j * 16, 16), 16)
            for h in range(2):
                part = jnp.concatenate(
                    [both[0, 8 * h : 8 * h + 8], both[1, 8 * h : 8 * h + 8]], axis=0
                )
                canon[at, h * MAIN : (h + 1) * MAIN] = part.astype(BF16)
            return carry

        lax.fori_loop(0, group // 2, body, 0)
        for b in range(group // BLOCK):
            spill = buf[pl.ds(start + b * BLOCK, BLOCK), :, MAIN:].reshape(256, SPILL)
            moved = dot(to_blocks, spill).astype(BF16)
            for c in range(8):
                canon[
                    main_rows + 32 * b : main_rows + 32 * (b + 1), c * SPILL : (c + 1) * SPILL
                ] = moved[32 * c : 32 * (c + 1)]

    def repack(canon, buf, start):
        def body(j, carry):
            both = canon[pl.ds(pl.multiple_of(j * 16, 16), 16), :].astype(F32)
            for s in range(2):
                part = jnp.concatenate(
                    [both[8 * s : 8 * s + 8, 0:MAIN], both[8 * s : 8 * s + 8, MAIN:]], axis=0
                )
                buf[start + 2 * j + s, :, 0:MAIN] = part.astype(BF16)
            return carry

        lax.fori_loop(0, group // 2, body, 0)
        for b in range(group // BLOCK):
            rows = canon[main_rows + 32 * b : main_rows + 32 * (b + 1), :]
            buf[pl.ds(start + b * BLOCK, BLOCK), :, MAIN:] = spill_to_chunk(
                [rows[:, 0:MAIN], rows[:, MAIN:]]
            )

    def expert(n, carry):
        start = n * group
        bytes_of(grad_in, group, g_send, g_recv.at[n]).wait_recv()
        bytes_of(row_in, group, x_send, x_recv.at[n]).wait_recv()
        unpack(row_in, start, canon_x)
        unpack(grad_in, start, canon_g)
        gate_act = dot(canon_x[...], w_gate[...])
        up_act = dot(canon_x[...], w_up[...])
        sigmoid = jax.nn.sigmoid(gate_act)
        silu = gate_act * sigmoid
        hidden = (silu * up_act).astype(BF16)
        hidden_grad = dot_nt(canon_g[...], w_down[...])
        gate_grad = (hidden_grad * up_act * sigmoid * (1.0 + gate_act * (1.0 - sigmoid))).astype(BF16)
        up_grad = (hidden_grad * silu).astype(BF16)
        canon_x[...] = (dot_nt(gate_grad, w_gate[...]) + dot_nt(up_grad, w_up[...])).astype(BF16)
        repack(canon_x, row_in, start)
        send_back(row_in, back_rows, r_send, r_recv, jnp.maximum(start, 1), start + group)
        canon_g[...] = dot(hidden, w_down[...]).astype(BF16)
        repack(canon_g, grad_in, start)
        return carry

    lax.fori_loop(0, groups, expert, 0)
    pltpu.make_async_copy(row_in.at[0], back_rows.at[me], r_recv).start()
    pltpu.make_async_copy(grad_in.at[0], back_outs.at[me], y_recv).start()
    send_back(grad_in, back_outs, y_send, y_recv, 1, count)

    def combine(buf):
        for n in range(4):
            cols = slice(n * 256, (n + 1) * 256)
            part = dot(mix_main[...], buf[:, :, cols].reshape(count * ROWS, 256))
            wide[:, n * 256 : (n + 1) * 256] = part[0:tokens]
            wide[:, MAIN + n * 256 : MAIN + (n + 1) * 256] = part[tokens:]
        spill = buf[:, :, MAIN:].reshape(count * ROWS, SPILL)
        block_of = (iota((tokens, count * ROWS), 1) % ROWS) // 2
        for c in range(8):
            picked = jnp.where(block_of == c, mix_spill[...].astype(F32), 0.0).astype(BF16)
            wide[:, c * SPILL : (c + 1) * SPILL] += dot(picked, spill)

    bytes_of(back_rows, count, r_send, r_recv).wait_recv()
    combine(back_rows)
    normed_grad = wide[...]
    attn_again = attn[...].astype(F32)
    inv = lax.rsqrt(jnp.mean(attn_again * attn_again, axis=1, keepdims=True) + EPSILON)
    shared = jnp.mean(normed_grad * attn_again, axis=1, keepdims=True)
    wide[...] = inv * normed_grad - inv * inv * inv * attn_again * shared

    key_acc[...] = jnp.zeros_like(key_acc)
    value_acc[...] = jnp.zeros_like(value_acc)

    def backward(p, carry):
        g = p // per_kv
        query = two_heads(queries[:, columns(p)].astype(F32) * scale)
        grad = wide[:, columns(p)].astype(BF16).astype(F32)
        grads = two_heads(grad)
        product_t = (grad * attn[:, columns(p)].astype(F32)).T
        delta = jnp.concatenate(
            [
                jnp.sum(product_t[0:HD], axis=0, keepdims=True),
                jnp.sum(product_t[HD:], axis=0, keepdims=True),
            ],
            axis=1,
        )
        scores = dot_nt(key_dup[g], query) + bias[...]
        weights = jnp.exp(scores - log_total[p])
        prob_grad = dot_nt(value_dup[g], grads)
        score_grads = (weights * (prob_grad - delta)).astype(BF16)
        query_t = dot(key_dup_t[g], score_grads) * scale
        query_grad[:, columns(p)] = join_heads(query_t).astype(BF16)
        key_acc[g] += dot(score_grads, query)
        value_acc[g] += dot(weights.astype(BF16), grads)
        return carry

    lax.fori_loop(0, pairs, backward, 0)

    low_long = iota((length, PAIR), 1) < HD
    for n, acc in enumerate((key_acc, value_acc)):
        first = acc[0] + pltpu.roll(acc[0], HD, 1)
        second = acc[1] + pltpu.roll(acc[1], HD, 1)
        pair_part[:, n * PAIR : (n + 1) * PAIR] = jnp.where(low_long, first, second)

    def send_part(j, carry):
        peer = (ctx + j) % n_ctx
        pltpu.make_async_remote_copy(
            src_ref=pair_part.at[pl.ds(pl.multiple_of(peer * tokens, tokens), tokens)],
            dst_ref=pair_in.at[j],
            send_sem=p_send,
            recv_sem=p_recv,
            device_id=(dp, peer),
            device_id_type=MESH,
        ).start()
        return carry

    lax.fori_loop(1, n_ctx, send_part, 0)

    bytes_of(back_outs, count, y_send, y_recv).wait_recv()
    combine(back_outs)
    moe_out[...] = wide[...].astype(BF16)

    def weigh(block, carry):
        first = pl.ds(pl.multiple_of(block * BLOCK, BLOCK), BLOCK)
        sent = grad_out[first].reshape(256, CHUNK).astype(F32)
        got = back_outs[first].reshape(256, CHUNK).astype(F32)
        product = sent * got
        main = jnp.sum(product[:, 0:MAIN], axis=1, keepdims=True)
        spill = jnp.sum(product[:, MAIN:], axis=1, keepdims=True)
        ranks = dot(repeat_main, ranks_of(block))
        row = iota((256, tokens), 0) % ROWS
        found = jnp.where(ranks == (row % 8).astype(F32), main, 0.0) + jnp.where(
            ranks == (8 + row % 2).astype(F32), spill, 0.0
        )
        pick_et[first, :] = jnp.sum(found.reshape(BLOCK, ROWS, tokens), axis=1)
        return carry

    lax.fori_loop(0, count // BLOCK, weigh, 0)
    dots = pick_et[...]
    weight_grad = jnp.concatenate(
        [
            jnp.sum(
                jnp.where(iota((count, tokens), 0) == ids[k : k + 1, :], dots, 0.0),
                axis=0,
                keepdims=True,
            )
            for k in range(ids.shape[0])
        ],
        axis=0,
    )
    score_again = raw[...]
    sum_again = jnp.sum(score_again, axis=0, keepdims=True)
    mixing_again = score_again / sum_again
    score_grad[...] = (
        weight_grad - jnp.sum(mixing_again * weight_grad, axis=0, keepdims=True)
    ) / sum_again

    parts_wait = bytes_of(pair_in, n_ctx - 1, p_send, p_recv)
    parts_wait.wait()
    pair_sum = pair_part[here, :]
    for j in range(1, n_ctx):
        pair_sum = pair_sum + pair_in[j]
    key_grad[...] = pair_sum[:, 0:PAIR].astype(BF16)
    value_grad[...] = pair_sum[:, PAIR:].astype(BF16)

    for ref, sem_s, sem_r in (
        (grad_out, g_send, g_recv.at[0]),
        (row_out, x_send, x_recv.at[0]),
        (row_in, r_send, r_recv),
        (grad_in, y_send, y_recv),
    ):
        bytes_of(ref, count - 1, sem_s, sem_r).wait_send()


def shards(
    n_dp,
    n_ctx,
    queries,
    keys,
    values,
    expert_ids,
    router_scores,
    gate_weight,
    up_weight,
    down_weight,
    out_grad,
):
    count = n_dp * n_ctx
    group = max(BLOCK, count // 4)
    groups = count // group
    tokens, width = queries.shape[1:]
    pair_width = keys.shape[2]
    top = expert_ids.shape[2]
    hidden = gate_weight.shape[2]
    length = n_ctx * tokens
    pairs = width // PAIR
    chunk_buf = pltpu.VMEM((count, ROWS, CHUNK), BF16)
    dma = pltpu.SemaphoreType.DMA
    vmem = pl.BlockSpec(memory_space=pltpu.VMEM)
    hbm = pl.BlockSpec(memory_space=pl.ANY)
    canon = pltpu.VMEM((group * 10, width), BF16)
    outs = pl.pallas_call(
        functools.partial(layer_kernel, n_dp, n_ctx, group),
        out_shape=(
            jax.ShapeDtypeStruct((tokens, width), BF16),
            jax.ShapeDtypeStruct((tokens, width), BF16),
            jax.ShapeDtypeStruct((tokens, pair_width), BF16),
            jax.ShapeDtypeStruct((tokens, pair_width), BF16),
            jax.ShapeDtypeStruct((top, tokens), F32),
        ),
        in_specs=[vmem] * 6 + [hbm] * 3,
        out_specs=[vmem] * 5,
        scratch_shapes=[
            pltpu.VMEM((width, hidden), BF16),
            pltpu.VMEM((width, hidden), BF16),
            pltpu.VMEM((hidden, width), BF16),
            chunk_buf,
            chunk_buf,
            chunk_buf,
            chunk_buf,
            chunk_buf,
            chunk_buf,
            canon,
            canon,
            pltpu.VMEM((2 * tokens, MAIN), BF16),
            pltpu.VMEM((count, tokens), F32),
            pltpu.VMEM((2 * tokens, count * ROWS), BF16),
            pltpu.VMEM((tokens, count * ROWS), BF16),
            pltpu.VMEM((length, pair_width), BF16),
            pltpu.VMEM((length, pair_width), BF16),
            pltpu.VMEM((2, length, PAIR), BF16),
            pltpu.VMEM((2, length, PAIR), BF16),
            pltpu.VMEM((2, PAIR, length), BF16),
            pltpu.VMEM((2, PAIR, length), BF16),
            pltpu.VMEM((length, 2 * tokens), F32),
            pltpu.VMEM((tokens, width), BF16),
            pltpu.VMEM((pairs, 1, 2 * tokens), F32),
            pltpu.VMEM((tokens, width), F32),
            pltpu.VMEM((count, tokens), F32),
            pltpu.VMEM((2, length, PAIR), F32),
            pltpu.VMEM((2, length, PAIR), F32),
            pltpu.VMEM((length, 2 * PAIR), F32),
            pltpu.VMEM((n_ctx, tokens, 2 * PAIR), F32),
            dma((3,)),
            dma((2,)),
            dma((2,)),
            dma,
            dma((groups,)),
            dma,
            dma((groups,)),
            dma,
            dma,
            dma,
            dma,
            dma,
            dma,
        ],
        compiler_params=pltpu.CompilerParams(
            collective_id=0, has_side_effects=True, vmem_limit_bytes=63 * 2**20
        ),
        name="layer",
    )(
        expert_ids[0].T,
        router_scores[0].T,
        queries[0],
        keys[0],
        values[0],
        out_grad[0],
        gate_weight[0],
        up_weight[0],
        down_weight[0],
    )
    moe_out, query_grad, key_grad, value_grad, score_grad = outs
    return (
        moe_out[None],
        query_grad[None],
        key_grad[None],
        value_grad[None],
        score_grad.T[None],
    )


def solution(mesh):
    split = P("dp", "ctx", None)
    whole = P(("dp", "ctx"), None, None)
    return jax.shard_map(
        functools.partial(shards, mesh.shape["dp"], mesh.shape["ctx"]),
        mesh=mesh,
        in_specs=(split, split, split, split, split, whole, whole, whole, split),
        out_specs=(split,) * 5,
        check_vma=False,
    )
```

```python
import functools

import jax
import jax.numpy as jnp
from jax import lax
from jax.experimental import pallas as pl
from jax.experimental.pallas import tpu as pltpu
from jax.sharding import PartitionSpec as P

HD = 64
EPSILON = 1e-06
NEGATIVE = -1e30
MESH = pl.DeviceIdType.MESH
F32 = jnp.float32
BF16 = jnp.bfloat16

ROWS = 16
MAIN = 1024
SPILL = 256
CHUNK = MAIN + SPILL
BLOCK = 16
PAIR = 128


def dot(a, b):
    return lax.dot_general(a, b, (((1,), (0,)), ((), ())), preferred_element_type=F32)


def dot_nt(a, b):
    return lax.dot_general(a, b, (((1,), (1,)), ((), ())), preferred_element_type=F32)


def iota(shape, dim):
    return lax.broadcasted_iota(jnp.int32, shape, dim)


def quo(a, n):
    return lax.shift_right_logical(a, jnp.int32(n.bit_length() - 1)) if a.ndim else a // n


def rem(a, n):
    return jnp.bitwise_and(a, n - 1) if a.ndim else a % n


def torus_partner(step, x, y, z, core, sign):
    inner = rem(step, 64)
    a, b, c = quo(inner, 16), rem(quo(inner, 4), 4), rem(inner, 4)
    dx = c
    dy = rem(c + b, 4)
    dz = rem(c + a + 2 * b, 4)
    tx = rem(x + sign * dx + 4, 4)
    ty = rem(y + sign * dy + 4, 4)
    tz = rem(z + sign * dz + 4, 4)
    tcore = rem(core + quo(step, 64), 2)
    return tx * 4 + rem(tz, 2) * 2 + tcore, ty * 2 + quo(tz, 2)


def partners(n_dp, n_ctx):
    dp, ctx = lax.axis_index("dp"), lax.axis_index("ctx")
    count = n_dp * n_ctx
    if (n_dp, n_ctx) == (16, 8):
        x, core = dp // 4, dp % 2
        y, z = ctx // 2, (dp // 2) % 2 + 2 * (ctx % 2)
        sign = 1 - 2 * core

        def target(step):
            step = jnp.asarray(step, jnp.int32)
            return torus_partner(step, x, y, z, core, sign)

        def source(step):
            step = jnp.asarray(step, jnp.int32)
            other = 1 - 2 * (step // 64)
            return torus_partner(step, x, y, z, core, -sign * other)

        return target, source
    me = dp * n_ctx + ctx

    def target(step):
        step = jnp.asarray(step, jnp.int32)
        t = rem(me + step, count)
        return quo(t, n_ctx), rem(t, n_ctx)

    def source(step):
        t = (me - step + count) % count
        return t // n_ctx, t % n_ctx

    return target, source


def layer_kernel(
    n_dp,
    n_ctx,
    group,
    ids,
    raw,
    queries,
    keys,
    values,
    out_grad,
    gate_hbm,
    up_hbm,
    down_hbm,
    moe_out,
    query_grad,
    key_grad,
    value_grad,
    score_grad,
    w_gate,
    w_up,
    w_down,
    grad_out,
    grad_in,
    row_out,
    row_in,
    back_rows,
    back_outs,
    canon_x,
    canon_g,
    halves,
    rank_et,
    mix_main,
    mix_spill,
    all_keys,
    all_values,
    key_dup,
    value_dup,
    key_dup_t,
    value_dup_t,
    bias,
    attn,
    log_total,
    wide,
    pick_et,
    key_acc,
    value_acc,
    pair_part,
    pair_in,
    w_sem,
    kv_send,
    kv_recv,
    g_send,
    g_recv,
    x_send,
    x_recv,
    r_send,
    r_recv,
    y_send,
    y_recv,
    p_send,
    p_recv,
):
    count = n_dp * n_ctx
    groups = count // group
    tokens = queries.shape[0]
    width = queries.shape[1]
    pairs = width // PAIR
    per_kv = pairs // 2
    length = n_ctx * tokens
    dp, ctx = lax.axis_index("dp"), lax.axis_index("ctx")
    me = dp * n_ctx + ctx
    target, source = partners(n_dp, n_ctx)
    neighbour = target(1)

    weight_copies = [
        pltpu.make_async_copy(src, dst, w_sem.at[n])
        for n, (src, dst) in enumerate(((gate_hbm, w_gate), (up_hbm, w_up), (down_hbm, w_down)))
    ]
    all_keys[...] = jnp.zeros_like(all_keys)
    all_values[...] = jnp.zeros_like(all_values)

    barrier = pltpu.get_barrier_semaphore()

    def greet(step, carry):
        pl.semaphore_signal(barrier, inc=1, device_id=target(step), device_id_type=MESH)
        return carry

    lax.fori_loop(1, count, greet, 0)

    tdp_row, tctx_row = target(iota((count, tokens), 0))
    expert_row = (tdp_row * n_ctx + tctx_row).astype(F32)
    ids_t = ids[...].astype(F32)
    named = jnp.zeros((count, tokens), F32)
    for k in range(ids_t.shape[0]):
        named = named + jnp.where(expert_row == ids_t[k : k + 1, :], 1.0, 0.0)
    before = jnp.where(iota((tokens, tokens), 0) < iota((tokens, tokens), 1), 1.0, 0.0)
    rank = dot(named.astype(BF16), before.astype(BF16))
    rank_et[...] = jnp.where(named > 0.0, rank, -1.0)

    p_out, p_in = iota((256, 256), 0), iota((256, 256), 1)
    to_blocks = jnp.where(
        (quo(p_out, 32) == quo(rem(p_in, 16), 2))
        & (quo(rem(p_out, 32), 2) == quo(p_in, 16))
        & (rem(p_out, 2) == rem(p_in, 2)),
        1.0,
        0.0,
    ).astype(BF16)
    to_chunks = jnp.where(
        (quo(p_in, 32) == quo(rem(p_out, 16), 2))
        & (quo(rem(p_in, 32), 2) == quo(p_out, 16))
        & (rem(p_out, 2) == rem(p_in, 2)),
        1.0,
        0.0,
    ).astype(BF16)
    repeat_main = jnp.where(
        quo(iota((256, BLOCK), 0), ROWS) == iota((256, BLOCK), 1), 1.0, 0.0
    ).astype(BF16)
    repeat_spill = jnp.where(quo(iota((32, BLOCK), 0), 2) == iota((32, BLOCK), 1), 1.0, 0.0).astype(
        BF16
    )
    block_row = rem(iota((256, tokens), 0), ROWS)
    main_slot = rem(block_row, 8).astype(F32)
    spill_slot = (8 + rem(block_row, 2)).astype(F32)
    spill_row_slot = (8 + rem(iota((32, tokens), 0), 2)).astype(F32)

    def ranks_of(block):
        rows = rank_et[pl.ds(pl.multiple_of(block * BLOCK, BLOCK), BLOCK), :]
        return rows.astype(BF16)

    def pack_block(dst, block):
        ranks = ranks_of(block)
        hit = dot(repeat_main, ranks) == main_slot
        left = jnp.where(hit & (block_row < 8), 1.0, 0.0).astype(BF16)
        right = jnp.where(hit & (block_row >= 8), 1.0, 0.0).astype(BF16)
        first = pl.ds(pl.multiple_of(block * BLOCK, BLOCK), BLOCK)
        main = dot(jnp.concatenate([left, right], axis=1), halves[...])
        dst[first, :, 0:MAIN] = main.astype(BF16).reshape(BLOCK, ROWS, MAIN)
        spill_hit = jnp.where(dot(repeat_spill, ranks) == spill_row_slot, 1.0, 0.0).astype(BF16)
        rows = [
            dot(spill_hit, halves[0:tokens, :]).astype(BF16),
            dot(spill_hit, halves[tokens:, :]).astype(BF16),
        ]
        dst[first, :, MAIN:] = spill_to_chunk(rows)

    def spill_to_chunk(rows):
        stacked = jnp.concatenate(
            [part[:, c * SPILL : (c + 1) * SPILL] for part in rows for c in range(4)], axis=0
        )
        return dot(to_chunks, stacked).astype(BF16).reshape(BLOCK, ROWS, SPILL)

    def send_out(src, dst, send_sem, recv_sem):
        def send(step, carry):
            pltpu.make_async_remote_copy(
                src_ref=src.at[step],
                dst_ref=dst.at[step],
                send_sem=send_sem,
                recv_sem=recv_sem.at[step // group],
                device_id=target(step),
                device_id_type=MESH,
            ).start()
            return carry

        def body(block, carry):
            pack_block(src, block)
            lax.fori_loop(jnp.maximum(block * BLOCK, 1), (block + 1) * BLOCK, send, 0)
            return carry

        lax.fori_loop(0, count // BLOCK, body, 0)
        pltpu.make_async_copy(src.at[0], dst.at[0], recv_sem.at[0]).start()

    def send_back(src, dst, send_sem, recv_sem, lo, hi):
        def body(step, carry):
            pltpu.make_async_remote_copy(
                src_ref=src.at[step],
                dst_ref=dst.at[step],
                send_sem=send_sem,
                recv_sem=recv_sem.at[step // group],
                device_id=source(step),
                device_id_type=MESH,
            ).start()
            return carry

        lax.fori_loop(lo, hi, body, 0)

    def bytes_of(ref, amount, sem_a, sem_b):
        part = ref.at[pl.ds(0, amount)]
        return pltpu.make_async_remote_copy(
            src_ref=part,
            dst_ref=part,
            send_sem=sem_a,
            recv_sem=sem_b,
            device_id=neighbour,
            device_id_type=MESH,
        )

    pl.semaphore_wait(barrier, count - 1)
    here = pl.ds(pl.multiple_of(ctx * tokens, tokens), tokens)
    pair_copies = ((keys, all_keys), (values, all_values))

    def pair_copy(n, peer, at):
        return pltpu.make_async_remote_copy(
            src_ref=pair_copies[n][0],
            dst_ref=pair_copies[n][1].at[pl.ds(pl.multiple_of(at * tokens, tokens), tokens)],
            send_sem=kv_send.at[n, peer],
            recv_sem=kv_recv.at[n, at],
            device_id=(dp, peer),
            device_id_type=MESH,
        )

    def send_pair(peer, carry):
        for n in range(2):
            pair_copy(n, peer, ctx).start()
        return carry

    lax.fori_loop(ctx + 1, n_ctx, send_pair, 0)
    halves[0:tokens, :] = out_grad[:, 0:MAIN]
    halves[tokens:, :] = out_grad[:, MAIN:]
    send_out(grad_out, grad_in, g_send, g_recv)
    for copy in weight_copies:
        copy.start()

    all_keys[here, :] = keys[...]
    all_values[here, :] = values[...]
    key_at = iota((length, 2 * tokens), 0)
    query_at = ctx * tokens + rem(iota((length, 2 * tokens), 1), tokens)
    bias[...] = jnp.where(key_at <= query_at, 0.0, NEGATIVE)

    def wait_pair(at, carry):
        for n in range(2):
            pair_copy(n, at, at).wait_recv()
        return carry

    lax.fori_loop(0, ctx, wait_pair, 0)
    for g in range(2):
        select = jnp.where(
            iota((PAIR, PAIR), 0) == g * HD + rem(iota((PAIR, PAIR), 1), HD), 1.0, 0.0
        ).astype(BF16)
        select_t = jnp.where(
            iota((PAIR, PAIR), 1) == g * HD + rem(iota((PAIR, PAIR), 0), HD), 1.0, 0.0
        ).astype(BF16)
        key_dup[g] = dot(all_keys[...], select).astype(BF16)
        value_dup[g] = dot(all_values[...], select).astype(BF16)
        key_dup_t[g] = dot_nt(select_t, all_keys[...]).astype(BF16)
        value_dup_t[g] = dot_nt(select_t, all_values[...]).astype(BF16)

    low = iota((tokens, PAIR), 1) < HD

    def two_heads(rows):
        return jnp.concatenate(
            [jnp.where(low, rows, 0.0), jnp.where(low, 0.0, rows)], axis=0
        ).astype(BF16)

    def join_heads(both_t):
        both = both_t.T
        return jnp.where(low, both[0:tokens], both[tokens:])

    def columns(p):
        return pl.ds(pl.multiple_of(p * PAIR, PAIR), PAIR)

    scale = HD**-0.5

    def forward(p, carry):
        g = p // per_kv
        query = two_heads(queries[:, columns(p)].astype(F32) * scale)
        scores = dot_nt(key_dup[g], query) + bias[...]
        top = jnp.max(scores, axis=0, keepdims=True)
        weights = jnp.exp(scores - top)
        total = jnp.sum(weights, axis=0, keepdims=True)
        out_t = dot(value_dup_t[g], weights.astype(BF16)) / total
        attn[:, columns(p)] = join_heads(out_t).astype(BF16)
        log_total[p] = top + jnp.log(total)
        return carry

    lax.fori_loop(0, pairs, forward, 0)

    attn_wide = attn[...].astype(F32)
    inv_rms = lax.rsqrt(jnp.mean(attn_wide * attn_wide, axis=1, keepdims=True) + EPSILON)
    normed = (attn_wide * inv_rms).astype(BF16)
    halves[0:tokens, :] = normed[:, 0:MAIN]
    halves[tokens:, :] = normed[:, MAIN:]
    send_out(row_out, row_in, x_send, x_recv)

    scores_t = raw[...]
    total_t = jnp.sum(scores_t, axis=0, keepdims=True)
    mixing_t = scores_t / total_t
    mix_et = jnp.zeros((count, tokens), F32)
    for k in range(ids_t.shape[0]):
        mix_et = mix_et + jnp.where(expert_row == ids_t[k : k + 1, :], mixing_t[k : k + 1, :], 0.0)
    wide_shape = (count, count * ROWS)
    spread = jnp.where(iota(wide_shape, 0) == quo(iota(wide_shape, 1), ROWS), 1.0, 0.0).astype(BF16)
    lane_row = rem(iota((tokens, count * ROWS), 1), ROWS)
    rank_wide = dot(rank_et[...].T.astype(BF16), spread)
    mix_wide = dot(mix_et.T.astype(BF16), spread)
    main_mix = jnp.where(rank_wide == rem(lane_row, 8).astype(F32), mix_wide, 0.0)
    mix_main[0:tokens, :] = jnp.where(lane_row < 8, main_mix, 0.0).astype(BF16)
    mix_main[tokens:, :] = jnp.where(lane_row >= 8, main_mix, 0.0).astype(BF16)
    spill_mix = jnp.where(rank_wide == (8 + rem(lane_row, 2)).astype(F32), mix_wide, 0.0)
    mix_spill[...] = spill_mix.astype(BF16)
    for copy in weight_copies:
        copy.wait()

    main_rows = group * 8

    def unpack(buf, start, canon):
        def body(j, carry):
            both = buf[pl.ds(start + 2 * j, 2), :, 0:MAIN].astype(F32)
            at = pl.ds(pl.multiple_of(j * 16, 16), 16)
            for h in range(2):
                part = jnp.concatenate(
                    [both[0, 8 * h : 8 * h + 8], both[1, 8 * h : 8 * h + 8]], axis=0
                )
                canon[at, h * MAIN : (h + 1) * MAIN] = part.astype(BF16)
            return carry

        lax.fori_loop(0, group // 2, body, 0)
        for b in range(group // BLOCK):
            spill = buf[pl.ds(start + b * BLOCK, BLOCK), :, MAIN:].reshape(256, SPILL)
            moved = dot(to_blocks, spill).astype(BF16)
            for c in range(8):
                canon[
                    main_rows + 32 * b : main_rows + 32 * (b + 1), c * SPILL : (c + 1) * SPILL
                ] = moved[32 * c : 32 * (c + 1)]

    def repack(canon, buf, start):
        def body(j, carry):
            both = canon[pl.ds(pl.multiple_of(j * 16, 16), 16), :].astype(F32)
            for s in range(2):
                part = jnp.concatenate(
                    [both[8 * s : 8 * s + 8, 0:MAIN], both[8 * s : 8 * s + 8, MAIN:]], axis=0
                )
                buf[start + 2 * j + s, :, 0:MAIN] = part.astype(BF16)
            return carry

        lax.fori_loop(0, group // 2, body, 0)
        for b in range(group // BLOCK):
            rows = canon[main_rows + 32 * b : main_rows + 32 * (b + 1), :]
            buf[pl.ds(start + b * BLOCK, BLOCK), :, MAIN:] = spill_to_chunk(
                [rows[:, 0:MAIN], rows[:, MAIN:]]
            )

    def expert(n, carry):
        start = n * group
        bytes_of(grad_in, group, g_send, g_recv.at[n]).wait_recv()
        bytes_of(row_in, group, x_send, x_recv.at[n]).wait_recv()
        unpack(row_in, start, canon_x)
        unpack(grad_in, start, canon_g)
        gate_act = dot(canon_x[...], w_gate[...])
        up_act = dot(canon_x[...], w_up[...])
        sigmoid = jax.nn.sigmoid(gate_act)
        silu = gate_act * sigmoid
        hidden = (silu * up_act).astype(BF16)
        hidden_grad = dot_nt(canon_g[...], w_down[...])
        gate_grad = (hidden_grad * up_act * sigmoid * (1.0 + gate_act * (1.0 - sigmoid))).astype(BF16)
        up_grad = (hidden_grad * silu).astype(BF16)
        canon_x[...] = (dot_nt(gate_grad, w_gate[...]) + dot_nt(up_grad, w_up[...])).astype(BF16)
        repack(canon_x, row_in, start)
        send_back(row_in, back_rows, r_send, r_recv, jnp.maximum(start, 1), start + group)
        canon_g[...] = dot(hidden, w_down[...]).astype(BF16)
        repack(canon_g, grad_in, start)
        return carry

    lax.fori_loop(0, groups, expert, 0)
    pltpu.make_async_copy(row_in.at[0], back_rows.at[0], r_recv.at[0]).start()
    pltpu.make_async_copy(grad_in.at[0], back_outs.at[0], y_recv.at[0]).start()
    send_back(grad_in, back_outs, y_send, y_recv, 1, count)

    def combine(buf, n):
        mine = pl.ds(pl.multiple_of(n * group, group), group)
        lanes = pl.ds(pl.multiple_of(n * group * ROWS, group * ROWS), group * ROWS)
        for c in range(4):
            rows = buf[mine, :, c * 256 : (c + 1) * 256].reshape(group * ROWS, 256)
            part = dot(mix_main[:, lanes], rows)
            wide[:, c * 256 : (c + 1) * 256] += part[0:tokens]
            wide[:, MAIN + c * 256 : MAIN + (c + 1) * 256] += part[tokens:]
        spill = buf[mine, :, MAIN:].reshape(group * ROWS, SPILL)
        spill_mix = mix_spill[:, lanes].astype(F32)
        column_block = quo(rem(iota((tokens, group * ROWS), 1), ROWS), 2)
        for c in range(8):
            picked = jnp.where(column_block == c, spill_mix, 0.0).astype(BF16)
            wide[:, c * SPILL : (c + 1) * SPILL] += dot(picked, spill)

    wide[...] = jnp.zeros_like(wide)

    def take_rows(n, carry):
        bytes_of(back_rows, group, r_send, r_recv.at[n]).wait_recv()
        combine(back_rows, n)
        return carry

    lax.fori_loop(0, groups, take_rows, 0)
    normed_grad = wide[...]
    attn_again = attn[...].astype(F32)
    inv = lax.rsqrt(jnp.mean(attn_again * attn_again, axis=1, keepdims=True) + EPSILON)
    shared = jnp.mean(normed_grad * attn_again, axis=1, keepdims=True)
    wide[...] = inv * normed_grad - inv * inv * inv * attn_again * shared

    key_acc[...] = jnp.zeros_like(key_acc)
    value_acc[...] = jnp.zeros_like(value_acc)

    def backward(p, carry):
        g = p // per_kv
        query = two_heads(queries[:, columns(p)].astype(F32) * scale)
        grad = wide[:, columns(p)].astype(BF16).astype(F32)
        grads = two_heads(grad)
        product_t = (grad * attn[:, columns(p)].astype(F32)).T
        delta = jnp.concatenate(
            [
                jnp.sum(product_t[0:HD], axis=0, keepdims=True),
                jnp.sum(product_t[HD:], axis=0, keepdims=True),
            ],
            axis=1,
        )
        scores = dot_nt(key_dup[g], query) + bias[...]
        weights = jnp.exp(scores - log_total[p])
        prob_grad = dot_nt(value_dup[g], grads)
        score_grads = (weights * (prob_grad - delta)).astype(BF16)
        query_t = dot(key_dup_t[g], score_grads) * scale
        query_grad[:, columns(p)] = join_heads(query_t).astype(BF16)
        key_acc[g] += dot(score_grads, query)
        value_acc[g] += dot(weights.astype(BF16), grads)
        return carry

    lax.fori_loop(0, pairs, backward, 0)

    low_long = iota((length, PAIR), 1) < HD
    for n, acc in enumerate((key_acc, value_acc)):
        first = acc[0] + pltpu.roll(acc[0], HD, 1)
        second = acc[1] + pltpu.roll(acc[1], HD, 1)
        pair_part[:, n * PAIR : (n + 1) * PAIR] = jnp.where(low_long, first, second).astype(BF16)

    def part_copy(peer, distance):
        return pltpu.make_async_remote_copy(
            src_ref=pair_part.at[pl.ds(pl.multiple_of(peer * tokens, tokens), tokens)],
            dst_ref=pair_in.at[distance],
            send_sem=p_send.at[distance],
            recv_sem=p_recv.at[distance],
            device_id=(dp, peer),
            device_id_type=MESH,
        )

    def send_part(peer, carry):
        part_copy(peer, ctx - peer).start()
        return carry

    lax.fori_loop(0, ctx, send_part, 0)

    wide[...] = jnp.zeros_like(wide)

    def weigh(block):
        first = pl.ds(pl.multiple_of(block * BLOCK, BLOCK), BLOCK)
        sent = grad_out[first].reshape(256, CHUNK).astype(F32)
        got = back_outs[first].reshape(256, CHUNK).astype(F32)
        product = sent * got
        main = jnp.sum(product[:, 0:MAIN], axis=1, keepdims=True)
        spill = jnp.sum(product[:, MAIN:], axis=1, keepdims=True)
        ranks = dot(repeat_main, ranks_of(block))
        found = jnp.where(ranks == main_slot, main, 0.0) + jnp.where(
            ranks == spill_slot, spill, 0.0
        )
        pick_et[first, :] = jnp.sum(found.reshape(BLOCK, ROWS, tokens), axis=1)

    def take_outs(n, carry):
        bytes_of(back_outs, group, y_send, y_recv.at[n]).wait_recv()
        combine(back_outs, n)
        for b in range(group // BLOCK):
            weigh(n * (group // BLOCK) + b)
        return carry

    lax.fori_loop(0, groups, take_outs, 0)
    moe_out[...] = wide[...].astype(BF16)
    dots = pick_et[...]
    weight_grad = jnp.concatenate(
        [
            jnp.sum(
                jnp.where(expert_row == ids_t[k : k + 1, :], dots, 0.0), axis=0, keepdims=True
            )
            for k in range(ids_t.shape[0])
        ],
        axis=0,
    )
    score_grad[...] = (
        weight_grad - jnp.sum(mixing_t * weight_grad, axis=0, keepdims=True)
    ) / total_t

    def add_part(distance, total):
        part_copy(0, distance).wait_recv()
        return total + pair_in[distance].astype(F32)

    pair_sum = lax.fori_loop(1, n_ctx - ctx, add_part, pair_part[here, :].astype(F32))
    key_grad[...] = pair_sum[:, 0:PAIR].astype(BF16)
    value_grad[...] = pair_sum[:, PAIR:].astype(BF16)

    for ref, sem_s, sem_r in (
        (grad_out, g_send, g_recv.at[0]),
        (row_out, x_send, x_recv.at[0]),
        (row_in, r_send, r_recv.at[0]),
        (grad_in, y_send, y_recv.at[0]),
    ):
        bytes_of(ref, count - 1, sem_s, sem_r).wait_send()

    def sent_pair(peer, carry):
        for n in range(2):
            pair_copy(n, peer, ctx).wait_send()
        return carry

    lax.fori_loop(ctx + 1, n_ctx, sent_pair, 0)

    def sent_part(peer, carry):
        part_copy(peer, ctx - peer).wait_send()
        return carry

    lax.fori_loop(0, ctx, sent_part, 0)


def settle_kernel(*refs):
    half = len(refs) // 2
    copies = [
        pltpu.make_async_copy(refs[n], refs[half + n], refs[-1].at[n]) for n in range(half)
    ]
    for copy in copies:
        copy.start()
    for copy in copies:
        copy.wait()


def settle(arrays):
    hbm = pl.BlockSpec(memory_space=pltpu.HBM)
    return pl.pallas_call(
        settle_kernel,
        out_shape=tuple(jax.ShapeDtypeStruct(a.shape, a.dtype) for a in arrays),
        in_specs=[hbm] * len(arrays),
        out_specs=[hbm] * len(arrays),
        scratch_shapes=[pltpu.SemaphoreType.DMA((len(arrays),))],
        compiler_params=pltpu.CompilerParams(vmem_limit_bytes=62 * 2**20),
        name="settle",
    )(*arrays)


def shards(
    n_dp,
    n_ctx,
    queries,
    keys,
    values,
    expert_ids,
    router_scores,
    gate_weight,
    up_weight,
    down_weight,
    out_grad,
):
    count = n_dp * n_ctx
    group = max(BLOCK, count // 4)
    groups = count // group
    tokens, width = queries.shape[1:]
    pair_width = keys.shape[2]
    top = expert_ids.shape[2]
    hidden = gate_weight.shape[2]
    length = n_ctx * tokens
    pairs = width // PAIR
    chunk_buf = pltpu.VMEM((count, ROWS, CHUNK), BF16)
    dma = pltpu.SemaphoreType.DMA
    vmem = pl.BlockSpec(memory_space=pltpu.VMEM)
    hbm = pl.BlockSpec(memory_space=pl.ANY)
    canon = pltpu.VMEM((group * 10, width), BF16)
    outs = pl.pallas_call(
        functools.partial(layer_kernel, n_dp, n_ctx, group),
        out_shape=(
            jax.ShapeDtypeStruct((tokens, width), BF16),
            jax.ShapeDtypeStruct((tokens, width), BF16),
            jax.ShapeDtypeStruct((tokens, pair_width), BF16),
            jax.ShapeDtypeStruct((tokens, pair_width), BF16),
            jax.ShapeDtypeStruct((top, tokens), F32),
        ),
        in_specs=[vmem] * 6 + [hbm] * 3,
        out_specs=[vmem] * 5,
        scratch_shapes=[
            pltpu.VMEM((width, hidden), BF16),
            pltpu.VMEM((width, hidden), BF16),
            pltpu.VMEM((hidden, width), BF16),
            chunk_buf,
            chunk_buf,
            chunk_buf,
            chunk_buf,
            chunk_buf,
            chunk_buf,
            canon,
            canon,
            pltpu.VMEM((2 * tokens, MAIN), BF16),
            pltpu.VMEM((count, tokens), F32),
            pltpu.VMEM((2 * tokens, count * ROWS), BF16),
            pltpu.VMEM((tokens, count * ROWS), BF16),
            pltpu.VMEM((length, pair_width), BF16),
            pltpu.VMEM((length, pair_width), BF16),
            pltpu.VMEM((2, length, PAIR), BF16),
            pltpu.VMEM((2, length, PAIR), BF16),
            pltpu.VMEM((2, PAIR, length), BF16),
            pltpu.VMEM((2, PAIR, length), BF16),
            pltpu.VMEM((length, 2 * tokens), F32),
            pltpu.VMEM((tokens, width), BF16),
            pltpu.VMEM((pairs, 1, 2 * tokens), F32),
            pltpu.VMEM((tokens, width), F32),
            pltpu.VMEM((count, tokens), F32),
            pltpu.VMEM((2, length, PAIR), F32),
            pltpu.VMEM((2, length, PAIR), F32),
            pltpu.VMEM((length, 2 * PAIR), BF16),
            pltpu.VMEM((n_ctx, tokens, 2 * PAIR), BF16),
            dma((3,)),
            dma((2, n_ctx)),
            dma((2, n_ctx)),
            dma,
            dma((groups,)),
            dma,
            dma((groups,)),
            dma,
            dma((groups,)),
            dma,
            dma((groups,)),
            dma((n_ctx,)),
            dma((n_ctx,)),
        ],
        compiler_params=pltpu.CompilerParams(
            collective_id=0, has_side_effects=True, vmem_limit_bytes=63 * 2**20
        ),
        name="layer",
    )(
        expert_ids[0].T,
        router_scores[0].T,
        queries[0],
        keys[0],
        values[0],
        out_grad[0],
        gate_weight[0],
        up_weight[0],
        down_weight[0],
    )
    moe_out, query_grad, key_grad, value_grad, score_grad = settle(outs)
    return (
        moe_out[None],
        query_grad[None],
        key_grad[None],
        value_grad[None],
        score_grad.T[None],
    )


def solution(mesh):
    split = P("dp", "ctx", None)
    whole = P(("dp", "ctx"), None, None)
    return jax.shard_map(
        functools.partial(shards, mesh.shape["dp"], mesh.shape["ctx"]),
        mesh=mesh,
        in_specs=(split, split, split, split, split, whole, whole, whole, split),
        out_specs=(split,) * 5,
        check_vma=False,
    )
```

```python
import functools

import jax
import jax.numpy as jnp
from jax import lax
from jax.experimental import pallas as pl
from jax.experimental.pallas import tpu as pltpu
from jax.sharding import PartitionSpec as P

HD = 64
EPSILON = 1e-06
NEGATIVE = -1e30
MESH = pl.DeviceIdType.MESH
F32 = jnp.float32
BF16 = jnp.bfloat16

ROWS = 16
MAIN = 1024
SPILL = 256
CHUNK = MAIN + SPILL
BLOCK = 16
PAIR = 128


def dot(a, b):
    return lax.dot_general(a, b, (((1,), (0,)), ((), ())), preferred_element_type=F32)


def dot_nt(a, b):
    return lax.dot_general(a, b, (((1,), (1,)), ((), ())), preferred_element_type=F32)


def iota(shape, dim):
    return lax.broadcasted_iota(jnp.int32, shape, dim)


def quo(a, n):
    return lax.shift_right_logical(a, jnp.int32(n.bit_length() - 1)) if a.ndim else a // n


def rem(a, n):
    return jnp.bitwise_and(a, n - 1) if a.ndim else a % n


def torus_partner(step, x, y, z, core, sign):
    inner = rem(step, 64)
    a, b, c = quo(inner, 16), rem(quo(inner, 4), 4), rem(inner, 4)
    dx = c
    dy = rem(c + b, 4)
    dz = rem(c + a + 2 * b, 4)
    tx = rem(x + sign * dx + 4, 4)
    ty = rem(y + sign * dy + 4, 4)
    tz = rem(z + sign * dz + 4, 4)
    tcore = rem(core + quo(step, 64), 2)
    return tx * 4 + rem(tz, 2) * 2 + tcore, ty * 2 + quo(tz, 2)


def partners(n_dp, n_ctx):
    dp, ctx = lax.axis_index("dp"), lax.axis_index("ctx")
    count = n_dp * n_ctx
    if (n_dp, n_ctx) == (16, 8):
        x, core = dp // 4, dp % 2
        y, z = ctx // 2, (dp // 2) % 2 + 2 * (ctx % 2)
        sign = 1 - 2 * core

        def target(step):
            step = jnp.asarray(step, jnp.int32)
            return torus_partner(step, x, y, z, core, sign)

        def source(step):
            step = jnp.asarray(step, jnp.int32)
            other = 1 - 2 * (step // 64)
            return torus_partner(step, x, y, z, core, -sign * other)

        return target, source
    me = dp * n_ctx + ctx

    def target(step):
        step = jnp.asarray(step, jnp.int32)
        t = rem(me + step, count)
        return quo(t, n_ctx), rem(t, n_ctx)

    def source(step):
        t = (me - step + count) % count
        return t // n_ctx, t % n_ctx

    return target, source


def layer_kernel(
    n_dp,
    n_ctx,
    group,
    ids,
    raw,
    queries,
    keys,
    values,
    out_grad,
    gate_hbm,
    up_hbm,
    down_hbm,
    moe_out,
    query_grad,
    key_grad,
    value_grad,
    score_grad,
    w_gate,
    w_up,
    w_down,
    grad_out,
    grad_in,
    row_out,
    row_in,
    back_rows,
    back_outs,
    canon_x,
    canon_g,
    halves,
    rank_et,
    mix_main,
    mix_spill,
    all_keys,
    all_values,
    key_dup,
    value_dup,
    key_dup_t,
    value_dup_t,
    bias,
    attn,
    log_total,
    wide,
    pick_et,
    key_acc,
    value_acc,
    pair_part,
    pair_in,
    w_sem,
    kv_send,
    kv_recv,
    g_send,
    g_recv,
    x_send,
    x_recv,
    r_send,
    r_recv,
    y_send,
    y_recv,
    p_send,
    p_recv,
):
    count = n_dp * n_ctx
    groups = count // group
    tokens = queries.shape[0]
    width = queries.shape[1]
    pairs = width // PAIR
    per_kv = pairs // 2
    length = n_ctx * tokens
    dp, ctx = lax.axis_index("dp"), lax.axis_index("ctx")
    me = dp * n_ctx + ctx
    target, source = partners(n_dp, n_ctx)
    neighbour = target(1)

    weight_copies = [
        pltpu.make_async_copy(src, dst, w_sem.at[n])
        for n, (src, dst) in enumerate(((gate_hbm, w_gate), (up_hbm, w_up), (down_hbm, w_down)))
    ]
    all_keys[...] = jnp.zeros_like(all_keys)
    all_values[...] = jnp.zeros_like(all_values)

    barrier = pltpu.get_barrier_semaphore()

    def greet(step, carry):
        pl.semaphore_signal(barrier, inc=1, device_id=target(step), device_id_type=MESH)
        return carry

    lax.fori_loop(1, count, greet, 0)

    tdp_row, tctx_row = target(iota((count, tokens), 0))
    expert_row = (tdp_row * n_ctx + tctx_row).astype(F32)
    ids_t = ids[...].astype(F32)
    named = jnp.zeros((count, tokens), F32)
    for k in range(ids_t.shape[0]):
        named = named + jnp.where(expert_row == ids_t[k : k + 1, :], 1.0, 0.0)
    before = jnp.where(iota((tokens, tokens), 0) < iota((tokens, tokens), 1), 1.0, 0.0)
    rank = dot(named.astype(BF16), before.astype(BF16))
    rank_et[...] = jnp.where(named > 0.0, rank, -1.0)

    p_out, p_in = iota((256, 256), 0), iota((256, 256), 1)
    to_blocks = jnp.where(
        (quo(p_out, 32) == quo(rem(p_in, 16), 2))
        & (quo(rem(p_out, 32), 2) == quo(p_in, 16))
        & (rem(p_out, 2) == rem(p_in, 2)),
        1.0,
        0.0,
    ).astype(BF16)
    to_chunks = jnp.where(
        (quo(p_in, 32) == quo(rem(p_out, 16), 2))
        & (quo(rem(p_in, 32), 2) == quo(p_out, 16))
        & (rem(p_out, 2) == rem(p_in, 2)),
        1.0,
        0.0,
    ).astype(BF16)
    repeat_main = jnp.where(
        quo(iota((256, BLOCK), 0), ROWS) == iota((256, BLOCK), 1), 1.0, 0.0
    ).astype(BF16)
    repeat_spill = jnp.where(quo(iota((32, BLOCK), 0), 2) == iota((32, BLOCK), 1), 1.0, 0.0).astype(
        BF16
    )
    block_row = rem(iota((256, tokens), 0), ROWS)
    main_slot = rem(block_row, 8).astype(F32)
    spill_slot = (8 + rem(block_row, 2)).astype(F32)
    spill_row_slot = (8 + rem(iota((32, tokens), 0), 2)).astype(F32)

    def ranks_of(block):
        rows = rank_et[pl.ds(pl.multiple_of(block * BLOCK, BLOCK), BLOCK), :]
        return rows.astype(BF16)

    def pack_block(dst, block):
        ranks = ranks_of(block)
        hit = dot(repeat_main, ranks) == main_slot
        left = jnp.where(hit & (block_row < 8), 1.0, 0.0).astype(BF16)
        right = jnp.where(hit & (block_row >= 8), 1.0, 0.0).astype(BF16)
        first = pl.ds(pl.multiple_of(block * BLOCK, BLOCK), BLOCK)
        main = dot(jnp.concatenate([left, right], axis=1), halves[...])
        dst[first, :, 0:MAIN] = main.astype(BF16).reshape(BLOCK, ROWS, MAIN)
        spill_hit = jnp.where(dot(repeat_spill, ranks) == spill_row_slot, 1.0, 0.0).astype(BF16)
        rows = [
            dot(spill_hit, halves[0:tokens, :]).astype(BF16),
            dot(spill_hit, halves[tokens:, :]).astype(BF16),
        ]
        dst[first, :, MAIN:] = spill_to_chunk(rows)

    def spill_to_chunk(rows):
        stacked = jnp.concatenate(
            [part[:, c * SPILL : (c + 1) * SPILL] for part in rows for c in range(4)], axis=0
        )
        return dot(to_chunks, stacked).astype(BF16).reshape(BLOCK, ROWS, SPILL)

    def send_out(src, dst, send_sem, recv_sem, held=None):
        def send(step, carry):
            pltpu.make_async_remote_copy(
                src_ref=src.at[step],
                dst_ref=dst.at[step],
                send_sem=send_sem,
                recv_sem=recv_sem.at[step // group],
                device_id=target(step),
                device_id_type=MESH,
            ).start()
            return carry

        def body(block, carry):
            pack_block(src, block)
            if not held:
                lax.fori_loop(jnp.maximum(block * BLOCK, 1), (block + 1) * BLOCK, send, 0)
            return carry

        lax.fori_loop(0, count // BLOCK, body, 0)
        if held:
            held()
            lax.fori_loop(1, count, send, 0)
        pltpu.make_async_copy(src.at[0], dst.at[0], recv_sem.at[0]).start()

    def send_back(src, dst, send_sem, recv_sem, lo, hi):
        def body(step, carry):
            pltpu.make_async_remote_copy(
                src_ref=src.at[step],
                dst_ref=dst.at[step],
                send_sem=send_sem,
                recv_sem=recv_sem.at[step // group],
                device_id=source(step),
                device_id_type=MESH,
            ).start()
            return carry

        lax.fori_loop(lo, hi, body, 0)

    def bytes_of(ref, amount, sem_a, sem_b):
        part = ref.at[pl.ds(0, amount)]
        return pltpu.make_async_remote_copy(
            src_ref=part,
            dst_ref=part,
            send_sem=sem_a,
            recv_sem=sem_b,
            device_id=neighbour,
            device_id_type=MESH,
        )

    pl.semaphore_wait(barrier, count - 1)
    here = pl.ds(pl.multiple_of(ctx * tokens, tokens), tokens)
    pair_copies = ((keys, all_keys), (values, all_values))

    def pair_copy(n, peer, at):
        return pltpu.make_async_remote_copy(
            src_ref=pair_copies[n][0],
            dst_ref=pair_copies[n][1].at[pl.ds(pl.multiple_of(at * tokens, tokens), tokens)],
            send_sem=kv_send.at[n, peer],
            recv_sem=kv_recv.at[n, at],
            device_id=(dp, peer),
            device_id_type=MESH,
        )

    def send_pair(peer, carry):
        for n in range(2):
            pair_copy(n, peer, ctx).start()
        return carry

    lax.fori_loop(ctx + 1, n_ctx, send_pair, 0)
    halves[0:tokens, :] = out_grad[:, 0:MAIN]
    halves[tokens:, :] = out_grad[:, MAIN:]
    send_out(grad_out, grad_in, g_send, g_recv)
    for copy in weight_copies:
        copy.start()

    all_keys[here, :] = keys[...]
    all_values[here, :] = values[...]
    key_at = iota((length, 2 * tokens), 0)
    query_at = ctx * tokens + rem(iota((length, 2 * tokens), 1), tokens)
    bias[...] = jnp.where(key_at <= query_at, 0.0, NEGATIVE)

    def wait_pair(at, carry):
        for n in range(2):
            pair_copy(n, at, at).wait_recv()
        return carry

    lax.fori_loop(0, ctx, wait_pair, 0)
    for g in range(2):
        select = jnp.where(
            iota((PAIR, PAIR), 0) == g * HD + rem(iota((PAIR, PAIR), 1), HD), 1.0, 0.0
        ).astype(BF16)
        select_t = jnp.where(
            iota((PAIR, PAIR), 1) == g * HD + rem(iota((PAIR, PAIR), 0), HD), 1.0, 0.0
        ).astype(BF16)
        key_dup[g] = dot(all_keys[...], select).astype(BF16)
        value_dup[g] = dot(all_values[...], select).astype(BF16)
        key_dup_t[g] = dot_nt(select_t, all_keys[...]).astype(BF16)
        value_dup_t[g] = dot_nt(select_t, all_values[...]).astype(BF16)

    low = iota((tokens, PAIR), 1) < HD

    def two_heads(rows):
        return jnp.concatenate(
            [jnp.where(low, rows, 0.0), jnp.where(low, 0.0, rows)], axis=0
        ).astype(BF16)

    def join_heads(both_t):
        both = both_t.T
        return jnp.where(low, both[0:tokens], both[tokens:])

    def columns(p):
        return pl.ds(pl.multiple_of(p * PAIR, PAIR), PAIR)

    scale = HD**-0.5

    def forward(p, carry):
        g = p // per_kv
        query = two_heads(queries[:, columns(p)].astype(F32) * scale)
        scores = dot_nt(key_dup[g], query) + bias[...]
        top = jnp.max(scores, axis=0, keepdims=True)
        weights = jnp.exp(scores - top)
        total = jnp.sum(weights, axis=0, keepdims=True)
        out_t = dot(value_dup_t[g], weights.astype(BF16)) / total
        attn[:, columns(p)] = join_heads(out_t).astype(BF16)
        log_total[p] = top + jnp.log(total)
        return carry

    lax.fori_loop(0, pairs, forward, 0)

    attn_wide = attn[...].astype(F32)
    inv_rms = lax.rsqrt(jnp.mean(attn_wide * attn_wide, axis=1, keepdims=True) + EPSILON)
    normed = (attn_wide * inv_rms).astype(BF16)
    halves[0:tokens, :] = normed[:, 0:MAIN]
    halves[tokens:, :] = normed[:, MAIN:]

    def grads_here():
        for n in range(groups):
            bytes_of(grad_in, group, g_send, g_recv.at[n]).wait_recv()

    send_out(row_out, row_in, x_send, x_recv, grads_here)

    scores_t = raw[...]
    total_t = jnp.sum(scores_t, axis=0, keepdims=True)
    mixing_t = scores_t / total_t
    mix_et = jnp.zeros((count, tokens), F32)
    for k in range(ids_t.shape[0]):
        mix_et = mix_et + jnp.where(expert_row == ids_t[k : k + 1, :], mixing_t[k : k + 1, :], 0.0)
    wide_shape = (count, count * ROWS)
    spread = jnp.where(iota(wide_shape, 0) == quo(iota(wide_shape, 1), ROWS), 1.0, 0.0).astype(BF16)
    lane_row = rem(iota((tokens, count * ROWS), 1), ROWS)
    rank_wide = dot(rank_et[...].T.astype(BF16), spread)
    mix_wide = dot(mix_et.T.astype(BF16), spread)
    main_mix = jnp.where(rank_wide == rem(lane_row, 8).astype(F32), mix_wide, 0.0)
    mix_main[0:tokens, :] = jnp.where(lane_row < 8, main_mix, 0.0).astype(BF16)
    mix_main[tokens:, :] = jnp.where(lane_row >= 8, main_mix, 0.0).astype(BF16)
    spill_mix = jnp.where(rank_wide == (8 + rem(lane_row, 2)).astype(F32), mix_wide, 0.0)
    mix_spill[...] = spill_mix.astype(BF16)
    for copy in weight_copies:
        copy.wait()

    main_rows = group * 8

    def unpack(buf, start, canon):
        def body(j, carry):
            both = buf[pl.ds(start + 2 * j, 2), :, 0:MAIN].astype(F32)
            at = pl.ds(pl.multiple_of(j * 16, 16), 16)
            for h in range(2):
                part = jnp.concatenate(
                    [both[0, 8 * h : 8 * h + 8], both[1, 8 * h : 8 * h + 8]], axis=0
                )
                canon[at, h * MAIN : (h + 1) * MAIN] = part.astype(BF16)
            return carry

        lax.fori_loop(0, group // 2, body, 0)
        for b in range(group // BLOCK):
            spill = buf[pl.ds(start + b * BLOCK, BLOCK), :, MAIN:].reshape(256, SPILL)
            moved = dot(to_blocks, spill).astype(BF16)
            for c in range(8):
                canon[
                    main_rows + 32 * b : main_rows + 32 * (b + 1), c * SPILL : (c + 1) * SPILL
                ] = moved[32 * c : 32 * (c + 1)]

    def repack(canon, buf, start):
        def body(j, carry):
            both = canon[pl.ds(pl.multiple_of(j * 16, 16), 16), :].astype(F32)
            for s in range(2):
                part = jnp.concatenate(
                    [both[8 * s : 8 * s + 8, 0:MAIN], both[8 * s : 8 * s + 8, MAIN:]], axis=0
                )
                buf[start + 2 * j + s, :, 0:MAIN] = part.astype(BF16)
            return carry

        lax.fori_loop(0, group // 2, body, 0)
        for b in range(group // BLOCK):
            rows = canon[main_rows + 32 * b : main_rows + 32 * (b + 1), :]
            buf[pl.ds(start + b * BLOCK, BLOCK), :, MAIN:] = spill_to_chunk(
                [rows[:, 0:MAIN], rows[:, MAIN:]]
            )

    def expert(n, carry):
        start = n * group
        bytes_of(row_in, group, x_send, x_recv.at[n]).wait_recv()

        @pl.when(n == groups - 1)
        def _():
            send_back(row_in, back_rows, r_send, r_recv, 1, start)

        unpack(row_in, start, canon_x)
        unpack(grad_in, start, canon_g)
        gate_act = dot(canon_x[...], w_gate[...])
        up_act = dot(canon_x[...], w_up[...])
        sigmoid = jax.nn.sigmoid(gate_act)
        silu = gate_act * sigmoid
        hidden = (silu * up_act).astype(BF16)
        hidden_grad = dot_nt(canon_g[...], w_down[...])
        gate_grad = (hidden_grad * up_act * sigmoid * (1.0 + gate_act * (1.0 - sigmoid))).astype(BF16)
        up_grad = (hidden_grad * silu).astype(BF16)
        canon_x[...] = (dot_nt(gate_grad, w_gate[...]) + dot_nt(up_grad, w_up[...])).astype(BF16)
        repack(canon_x, row_in, start)

        @pl.when(n == groups - 1)
        def _():
            send_back(row_in, back_rows, r_send, r_recv, jnp.maximum(start, 1), start + group)

        canon_g[...] = dot(hidden, w_down[...]).astype(BF16)
        repack(canon_g, grad_in, start)
        return carry

    lax.fori_loop(0, groups, expert, 0)
    pltpu.make_async_copy(row_in.at[0], back_rows.at[0], r_recv.at[0]).start()

    def combine(buf, n):
        mine = pl.ds(pl.multiple_of(n * group, group), group)
        lanes = pl.ds(pl.multiple_of(n * group * ROWS, group * ROWS), group * ROWS)
        for c in range(4):
            rows = buf[mine, :, c * 256 : (c + 1) * 256].reshape(group * ROWS, 256)
            part = dot(mix_main[:, lanes], rows)
            wide[:, c * 256 : (c + 1) * 256] += part[0:tokens]
            wide[:, MAIN + c * 256 : MAIN + (c + 1) * 256] += part[tokens:]
        spill = buf[mine, :, MAIN:].reshape(group * ROWS, SPILL)
        spill_mix = mix_spill[:, lanes].astype(F32)
        column_block = quo(rem(iota((tokens, group * ROWS), 1), ROWS), 2)
        for c in range(8):
            picked = jnp.where(column_block == c, spill_mix, 0.0).astype(BF16)
            wide[:, c * SPILL : (c + 1) * SPILL] += dot(picked, spill)

    wide[...] = jnp.zeros_like(wide)

    def take_rows(n, carry):
        bytes_of(back_rows, group, r_send, r_recv.at[n]).wait_recv()
        combine(back_rows, n)
        return carry

    lax.fori_loop(0, groups, take_rows, 0)
    pltpu.make_async_copy(grad_in.at[0], back_outs.at[0], y_recv.at[0]).start()
    send_back(grad_in, back_outs, y_send, y_recv, 1, count)
    normed_grad = wide[...]
    attn_again = attn[...].astype(F32)
    inv = lax.rsqrt(jnp.mean(attn_again * attn_again, axis=1, keepdims=True) + EPSILON)
    shared = jnp.mean(normed_grad * attn_again, axis=1, keepdims=True)
    wide[...] = inv * normed_grad - inv * inv * inv * attn_again * shared

    key_acc[...] = jnp.zeros_like(key_acc)
    value_acc[...] = jnp.zeros_like(value_acc)

    def backward(p, carry):
        g = p // per_kv
        query = two_heads(queries[:, columns(p)].astype(F32) * scale)
        grad = wide[:, columns(p)].astype(BF16).astype(F32)
        grads = two_heads(grad)
        product_t = (grad * attn[:, columns(p)].astype(F32)).T
        delta = jnp.concatenate(
            [
                jnp.sum(product_t[0:HD], axis=0, keepdims=True),
                jnp.sum(product_t[HD:], axis=0, keepdims=True),
            ],
            axis=1,
        )
        scores = dot_nt(key_dup[g], query) + bias[...]
        weights = jnp.exp(scores - log_total[p])
        prob_grad = dot_nt(value_dup[g], grads)
        score_grads = (weights * (prob_grad - delta)).astype(BF16)
        query_t = dot(key_dup_t[g], score_grads) * scale
        query_grad[:, columns(p)] = join_heads(query_t).astype(BF16)
        key_acc[g] += dot(score_grads, query)
        value_acc[g] += dot(weights.astype(BF16), grads)
        return carry

    lax.fori_loop(0, pairs, backward, 0)

    low_long = iota((length, PAIR), 1) < HD
    for n, acc in enumerate((key_acc, value_acc)):
        first = acc[0] + pltpu.roll(acc[0], HD, 1)
        second = acc[1] + pltpu.roll(acc[1], HD, 1)
        pair_part[:, n * PAIR : (n + 1) * PAIR] = jnp.where(low_long, first, second).astype(BF16)

    def part_copy(peer, distance):
        return pltpu.make_async_remote_copy(
            src_ref=pair_part.at[pl.ds(pl.multiple_of(peer * tokens, tokens), tokens)],
            dst_ref=pair_in.at[distance],
            send_sem=p_send.at[distance],
            recv_sem=p_recv.at[distance],
            device_id=(dp, peer),
            device_id_type=MESH,
        )

    def send_part(peer, carry):
        part_copy(peer, ctx - peer).start()
        return carry

    lax.fori_loop(0, ctx, send_part, 0)

    wide[...] = jnp.zeros_like(wide)

    def weigh(block):
        first = pl.ds(pl.multiple_of(block * BLOCK, BLOCK), BLOCK)
        sent = grad_out[first].reshape(256, CHUNK).astype(F32)
        got = back_outs[first].reshape(256, CHUNK).astype(F32)
        product = sent * got
        main = jnp.sum(product[:, 0:MAIN], axis=1, keepdims=True)
        spill = jnp.sum(product[:, MAIN:], axis=1, keepdims=True)
        ranks = dot(repeat_main, ranks_of(block))
        found = jnp.where(ranks == main_slot, main, 0.0) + jnp.where(
            ranks == spill_slot, spill, 0.0
        )
        pick_et[first, :] = jnp.sum(found.reshape(BLOCK, ROWS, tokens), axis=1)

    def take_outs(n, carry):
        bytes_of(back_outs, group, y_send, y_recv.at[n]).wait_recv()
        combine(back_outs, n)
        for b in range(group // BLOCK):
            weigh(n * (group // BLOCK) + b)
        return carry

    lax.fori_loop(0, groups, take_outs, 0)
    moe_out[...] = wide[...].astype(BF16)
    dots = pick_et[...]
    weight_grad = jnp.concatenate(
        [
            jnp.sum(
                jnp.where(expert_row == ids_t[k : k + 1, :], dots, 0.0), axis=0, keepdims=True
            )
            for k in range(ids_t.shape[0])
        ],
        axis=0,
    )
    score_grad[...] = (
        weight_grad - jnp.sum(mixing_t * weight_grad, axis=0, keepdims=True)
    ) / total_t

    def add_part(distance, total):
        part_copy(0, distance).wait_recv()
        return total + pair_in[distance].astype(F32)

    pair_sum = lax.fori_loop(1, n_ctx - ctx, add_part, pair_part[here, :].astype(F32))
    key_grad[...] = pair_sum[:, 0:PAIR].astype(BF16)
    value_grad[...] = pair_sum[:, PAIR:].astype(BF16)

    for ref, sem_s, sem_r in (
        (grad_out, g_send, g_recv.at[0]),
        (row_out, x_send, x_recv.at[0]),
        (row_in, r_send, r_recv.at[0]),
        (grad_in, y_send, y_recv.at[0]),
    ):
        bytes_of(ref, count - 1, sem_s, sem_r).wait_send()

    def sent_pair(peer, carry):
        for n in range(2):
            pair_copy(n, peer, ctx).wait_send()
        return carry

    lax.fori_loop(ctx + 1, n_ctx, sent_pair, 0)

    def sent_part(peer, carry):
        part_copy(peer, ctx - peer).wait_send()
        return carry

    lax.fori_loop(0, ctx, sent_part, 0)


def settle_kernel(*refs):
    count = (len(refs) - 2) // 3
    taken, given, held = refs[:count], refs[count : 2 * count], refs[2 * count : 3 * count]
    loads = [pltpu.make_async_copy(taken[n], held[n], refs[-2].at[n]) for n in range(count)]
    stores = [pltpu.make_async_copy(held[n], given[n], refs[-1].at[n]) for n in range(count)]
    for load in loads:
        load.start()
    for load, store in zip(loads, stores):
        load.wait()
        store.start()
    for store in stores:
        store.wait()


def settle(arrays):
    hbm = pl.BlockSpec(memory_space=pltpu.HBM)
    return pl.pallas_call(
        settle_kernel,
        out_shape=tuple(jax.ShapeDtypeStruct(a.shape, a.dtype) for a in arrays),
        in_specs=[hbm] * len(arrays),
        out_specs=[hbm] * len(arrays),
        scratch_shapes=[pltpu.VMEM(a.shape, a.dtype) for a in arrays]
        + [pltpu.SemaphoreType.DMA((len(arrays),))] * 2,
        compiler_params=pltpu.CompilerParams(vmem_limit_bytes=62 * 2**20),
        name="settle",
    )(*arrays)


def shards(
    n_dp,
    n_ctx,
    queries,
    keys,
    values,
    expert_ids,
    router_scores,
    gate_weight,
    up_weight,
    down_weight,
    out_grad,
):
    count = n_dp * n_ctx
    group = max(BLOCK, count // 4)
    groups = count // group
    tokens, width = queries.shape[1:]
    pair_width = keys.shape[2]
    top = expert_ids.shape[2]
    hidden = gate_weight.shape[2]
    length = n_ctx * tokens
    pairs = width // PAIR
    chunk_buf = pltpu.VMEM((count, ROWS, CHUNK), BF16)
    dma = pltpu.SemaphoreType.DMA
    vmem = pl.BlockSpec(memory_space=pltpu.VMEM)
    hbm = pl.BlockSpec(memory_space=pl.ANY)
    canon = pltpu.VMEM((group * 10, width), BF16)
    outs = pl.pallas_call(
        functools.partial(layer_kernel, n_dp, n_ctx, group),
        out_shape=(
            jax.ShapeDtypeStruct((tokens, width), BF16),
            jax.ShapeDtypeStruct((tokens, width), BF16),
            jax.ShapeDtypeStruct((tokens, pair_width), BF16),
            jax.ShapeDtypeStruct((tokens, pair_width), BF16),
            jax.ShapeDtypeStruct((top, tokens), F32),
        ),
        in_specs=[vmem] * 6 + [hbm] * 3,
        out_specs=[vmem] * 5,
        scratch_shapes=[
            pltpu.VMEM((width, hidden), BF16),
            pltpu.VMEM((width, hidden), BF16),
            pltpu.VMEM((hidden, width), BF16),
            chunk_buf,
            chunk_buf,
            chunk_buf,
            chunk_buf,
            chunk_buf,
            chunk_buf,
            canon,
            canon,
            pltpu.VMEM((2 * tokens, MAIN), BF16),
            pltpu.VMEM((count, tokens), F32),
            pltpu.VMEM((2 * tokens, count * ROWS), BF16),
            pltpu.VMEM((tokens, count * ROWS), BF16),
            pltpu.VMEM((length, pair_width), BF16),
            pltpu.VMEM((length, pair_width), BF16),
            pltpu.VMEM((2, length, PAIR), BF16),
            pltpu.VMEM((2, length, PAIR), BF16),
            pltpu.VMEM((2, PAIR, length), BF16),
            pltpu.VMEM((2, PAIR, length), BF16),
            pltpu.VMEM((length, 2 * tokens), F32),
            pltpu.VMEM((tokens, width), BF16),
            pltpu.VMEM((pairs, 1, 2 * tokens), F32),
            pltpu.VMEM((tokens, width), F32),
            pltpu.VMEM((count, tokens), F32),
            pltpu.VMEM((2, length, PAIR), F32),
            pltpu.VMEM((2, length, PAIR), F32),
            pltpu.VMEM((length, 2 * PAIR), BF16),
            pltpu.VMEM((n_ctx, tokens, 2 * PAIR), BF16),
            dma((3,)),
            dma((2, n_ctx)),
            dma((2, n_ctx)),
            dma,
            dma((groups,)),
            dma,
            dma((groups,)),
            dma,
            dma((groups,)),
            dma,
            dma((groups,)),
            dma((n_ctx,)),
            dma((n_ctx,)),
        ],
        compiler_params=pltpu.CompilerParams(
            collective_id=0, has_side_effects=True, vmem_limit_bytes=63 * 2**20
        ),
        name="layer",
    )(
        expert_ids[0].T,
        router_scores[0].T,
        queries[0],
        keys[0],
        values[0],
        out_grad[0],
        gate_weight[0],
        up_weight[0],
        down_weight[0],
    )
    moe_out, query_grad, key_grad, value_grad, score_grad = settle(outs)
    return (
        moe_out[None],
        query_grad[None],
        key_grad[None],
        value_grad[None],
        score_grad.T[None],
    )


def solution(mesh):
    split = P("dp", "ctx", None)
    whole = P(("dp", "ctx"), None, None)
    return jax.shard_map(
        functools.partial(shards, mesh.shape["dp"], mesh.shape["ctx"]),
        mesh=mesh,
        in_specs=(split, split, split, split, split, whole, whole, whole, split),
        out_specs=(split,) * 5,
        check_vma=False,
    )
```

```python
import functools

import jax
import jax.numpy as jnp
from jax import lax
from jax.experimental import pallas as pl
from jax.experimental.pallas import tpu as pltpu
from jax.sharding import PartitionSpec as P

HD = 64
EPSILON = 1e-06
NEGATIVE = -1e30
MESH = pl.DeviceIdType.MESH
F32 = jnp.float32
BF16 = jnp.bfloat16

ROWS = 16
MAIN = 1024
SPILL = 256
CHUNK = MAIN + SPILL
BLOCK = 16
PAIR = 128
HOLD_X, HOLD_R, HOLD_Y = 3, 3, 3


def dot(a, b):
    return lax.dot_general(a, b, (((1,), (0,)), ((), ())), preferred_element_type=F32)


def dot_nt(a, b):
    return lax.dot_general(a, b, (((1,), (1,)), ((), ())), preferred_element_type=F32)


def iota(shape, dim):
    return lax.broadcasted_iota(jnp.int32, shape, dim)


def quo(a, n):
    if a.ndim:
        return lax.shift_right_logical(a, jnp.int32(n.bit_length() - 1))
    return lax.div(a, jnp.int32(n))


def rem(a, n):
    return jnp.bitwise_and(a, n - 1) if a.ndim else lax.rem(a, jnp.int32(n))


def torus_partner(step, x, y, z, core, sign):
    inner = rem(step, 64)
    a, b, c = quo(inner, 16), rem(quo(inner, 4), 4), rem(inner, 4)
    dx = c
    dy = rem(c + b, 4)
    dz = rem(c + a + 2 * b, 4)
    tx = rem(x + sign * dx + 4, 4)
    ty = rem(y + sign * dy + 4, 4)
    tz = rem(z + sign * dz + 4, 4)
    tcore = rem(core + quo(step, 64), 2)
    return tx * 4 + rem(tz, 2) * 2 + tcore, ty * 2 + quo(tz, 2)


def partners(n_dp, n_ctx):
    dp, ctx = lax.axis_index("dp"), lax.axis_index("ctx")
    count = n_dp * n_ctx
    if (n_dp, n_ctx) == (16, 8):
        x, core = quo(dp, 4), rem(dp, 2)
        y, z = quo(ctx, 2), rem(quo(dp, 2), 2) + 2 * rem(ctx, 2)
        sign = 1 - 2 * core

        def target(step):
            step = jnp.asarray(step, jnp.int32)
            return torus_partner(step, x, y, z, core, sign)

        def source(step):
            step = jnp.asarray(step, jnp.int32)
            other = 1 - 2 * quo(step, 64)
            return torus_partner(step, x, y, z, core, -sign * other)

        return target, source
    me = dp * n_ctx + ctx

    def target(step):
        step = jnp.asarray(step, jnp.int32)
        t = rem(me + step, count)
        return quo(t, n_ctx), rem(t, n_ctx)

    def source(step):
        t = rem(me - jnp.asarray(step, jnp.int32) + count, count)
        return quo(t, n_ctx), rem(t, n_ctx)

    return target, source


def layer_kernel(
    n_dp,
    n_ctx,
    group,
    ids,
    raw,
    queries,
    keys,
    values,
    out_grad,
    gate_hbm,
    up_hbm,
    down_hbm,
    moe_out,
    query_grad,
    key_grad,
    value_grad,
    score_grad,
    w_gate,
    w_up,
    w_down,
    grad_out,
    grad_in,
    row_out,
    row_in,
    back_rows,
    back_outs,
    canon_x,
    canon_g,
    halves,
    rank_et,
    mix_main,
    mix_spill,
    all_keys,
    all_values,
    key_dup,
    value_dup,
    key_dup_t,
    value_dup_t,
    bias,
    attn,
    log_total,
    wide,
    pick_et,
    key_acc,
    value_acc,
    pair_part,
    pair_in,
    w_sem,
    kv_send,
    kv_recv,
    g_send,
    g_recv,
    x_send,
    x_recv,
    r_send,
    r_recv,
    y_send,
    y_recv,
    p_send,
    p_recv,
):
    count = n_dp * n_ctx
    groups = count // group
    tokens = queries.shape[0]
    width = queries.shape[1]
    pairs = width // PAIR
    per_kv = pairs // 2
    length = n_ctx * tokens
    dp, ctx = lax.axis_index("dp"), lax.axis_index("ctx")
    me = dp * n_ctx + ctx
    target, source = partners(n_dp, n_ctx)
    neighbour = target(1)

    weight_copies = [
        pltpu.make_async_copy(src, dst, w_sem.at[n])
        for n, (src, dst) in enumerate(((gate_hbm, w_gate), (up_hbm, w_up), (down_hbm, w_down)))
    ]
    all_keys[...] = jnp.zeros_like(all_keys)
    all_values[...] = jnp.zeros_like(all_values)

    barrier = pltpu.get_barrier_semaphore()

    def greet(step, carry):
        other = rem(me + step, count)
        where = (quo(other, n_ctx), rem(other, n_ctx))
        pl.semaphore_signal(barrier, inc=1, device_id=where, device_id_type=MESH)
        return carry

    lax.fori_loop(1, count, greet, 0)

    tdp_row, tctx_row = target(iota((count, tokens), 0))
    expert_row = (tdp_row * n_ctx + tctx_row).astype(F32)
    ids_t = ids[...].astype(F32)
    named = jnp.zeros((count, tokens), F32)
    for k in range(ids_t.shape[0]):
        named = named + jnp.where(expert_row == ids_t[k : k + 1, :], 1.0, 0.0)
    before = jnp.where(iota((tokens, tokens), 0) < iota((tokens, tokens), 1), 1.0, 0.0)
    rank = dot(named.astype(BF16), before.astype(BF16))
    rank_et[...] = jnp.where(named > 0.0, rank, -1.0)

    p_out, p_in = iota((256, 256), 0), iota((256, 256), 1)
    to_blocks = jnp.where(
        (quo(p_out, 32) == quo(rem(p_in, 16), 2))
        & (quo(rem(p_out, 32), 2) == quo(p_in, 16))
        & (rem(p_out, 2) == rem(p_in, 2)),
        1.0,
        0.0,
    ).astype(BF16)
    to_chunks = jnp.where(
        (quo(p_in, 32) == quo(rem(p_out, 16), 2))
        & (quo(rem(p_in, 32), 2) == quo(p_out, 16))
        & (rem(p_out, 2) == rem(p_in, 2)),
        1.0,
        0.0,
    ).astype(BF16)
    repeat_main = jnp.where(
        quo(iota((256, BLOCK), 0), ROWS) == iota((256, BLOCK), 1), 1.0, 0.0
    ).astype(BF16)
    repeat_spill = jnp.where(quo(iota((32, BLOCK), 0), 2) == iota((32, BLOCK), 1), 1.0, 0.0).astype(
        BF16
    )
    block_row = rem(iota((256, tokens), 0), ROWS)
    main_slot = rem(block_row, 8).astype(F32)
    spill_slot = (8 + rem(block_row, 2)).astype(F32)
    spill_row_slot = (8 + rem(iota((32, tokens), 0), 2)).astype(F32)

    def ranks_of(block):
        rows = rank_et[pl.ds(pl.multiple_of(block * BLOCK, BLOCK), BLOCK), :]
        return rows.astype(BF16)

    def pack_block(dst, block):
        ranks = ranks_of(block)
        hit = dot(repeat_main, ranks) == main_slot
        left = jnp.where(hit & (block_row < 8), 1.0, 0.0).astype(BF16)
        right = jnp.where(hit & (block_row >= 8), 1.0, 0.0).astype(BF16)
        first = pl.ds(pl.multiple_of(block * BLOCK, BLOCK), BLOCK)
        main = dot(jnp.concatenate([left, right], axis=1), halves[...])
        dst[first, :, 0:MAIN] = main.astype(BF16).reshape(BLOCK, ROWS, MAIN)
        spill_hit = jnp.where(dot(repeat_spill, ranks) == spill_row_slot, 1.0, 0.0).astype(BF16)
        rows = [
            dot(spill_hit, halves[0:tokens, :]).astype(BF16),
            dot(spill_hit, halves[tokens:, :]).astype(BF16),
        ]
        dst[first, :, MAIN:] = spill_to_chunk(rows)

    def spill_to_chunk(rows):
        stacked = jnp.concatenate(
            [part[:, c * SPILL : (c + 1) * SPILL] for part in rows for c in range(4)], axis=0
        )
        return dot(to_chunks, stacked).astype(BF16).reshape(BLOCK, ROWS, SPILL)

    def send_out(src, dst, send_sem, recv_sem, held=None):
        def send(step, carry):
            pltpu.make_async_remote_copy(
                src_ref=src.at[step],
                dst_ref=dst.at[step],
                send_sem=send_sem,
                recv_sem=recv_sem.at[quo(step, group)],
                device_id=target(step),
                device_id_type=MESH,
            ).start()
            return carry

        def body(block, carry):
            pack_block(src, block)
            if not held:
                lax.fori_loop(jnp.maximum(block * BLOCK, 1), (block + 1) * BLOCK, send, 0)
            return carry

        lax.fori_loop(0, count // BLOCK, body, 0)
        if held:
            held()
            lax.fori_loop(1, count, send, 0)
        pltpu.make_async_copy(src.at[0], dst.at[0], recv_sem.at[0]).start()

    def send_back(src, dst, send_sem, recv_sem, lo, hi):
        def body(step, carry):
            pltpu.make_async_remote_copy(
                src_ref=src.at[step],
                dst_ref=dst.at[step],
                send_sem=send_sem,
                recv_sem=recv_sem.at[quo(step, group)],
                device_id=source(step),
                device_id_type=MESH,
            ).start()
            return carry

        lax.fori_loop(lo, hi, body, 0)

    def bytes_of(ref, amount, sem_a, sem_b):
        part = ref.at[pl.ds(0, amount)]
        return pltpu.make_async_remote_copy(
            src_ref=part,
            dst_ref=part,
            send_sem=sem_a,
            recv_sem=sem_b,
            device_id=neighbour,
            device_id_type=MESH,
        )

    pl.semaphore_wait(barrier, count - 1)
    here = pl.ds(pl.multiple_of(ctx * tokens, tokens), tokens)
    pair_copies = ((keys, all_keys), (values, all_values))

    def pair_copy(n, peer, at):
        return pltpu.make_async_remote_copy(
            src_ref=pair_copies[n][0],
            dst_ref=pair_copies[n][1].at[pl.ds(pl.multiple_of(at * tokens, tokens), tokens)],
            send_sem=kv_send.at[n, peer],
            recv_sem=kv_recv.at[n, at],
            device_id=(dp, peer),
            device_id_type=MESH,
        )

    def send_pair(peer, carry):
        for n in range(2):
            pair_copy(n, peer, ctx).start()
        return carry

    lax.fori_loop(ctx + 1, n_ctx, send_pair, 0)
    halves[0:tokens, :] = out_grad[:, 0:MAIN]
    halves[tokens:, :] = out_grad[:, MAIN:]
    send_out(grad_out, grad_in, g_send, g_recv)
    for copy in weight_copies:
        copy.start()

    all_keys[here, :] = keys[...]
    all_values[here, :] = values[...]
    key_at = iota((length, 2 * tokens), 0)
    query_at = ctx * tokens + rem(iota((length, 2 * tokens), 1), tokens)
    bias[...] = jnp.where(key_at <= query_at, 0.0, NEGATIVE)

    def wait_pair(at, carry):
        for n in range(2):
            pair_copy(n, at, at).wait_recv()
        return carry

    lax.fori_loop(0, ctx, wait_pair, 0)
    for g in range(2):
        select = jnp.where(
            iota((PAIR, PAIR), 0) == g * HD + rem(iota((PAIR, PAIR), 1), HD), 1.0, 0.0
        ).astype(BF16)
        select_t = jnp.where(
            iota((PAIR, PAIR), 1) == g * HD + rem(iota((PAIR, PAIR), 0), HD), 1.0, 0.0
        ).astype(BF16)
        key_dup[g] = dot(all_keys[...], select).astype(BF16)
        value_dup[g] = dot(all_values[...], select).astype(BF16)
        key_dup_t[g] = dot_nt(select_t, all_keys[...]).astype(BF16)
        value_dup_t[g] = dot_nt(select_t, all_values[...]).astype(BF16)

    low = iota((tokens, PAIR), 1) < HD

    def two_heads(rows):
        return jnp.concatenate(
            [jnp.where(low, rows, 0.0), jnp.where(low, 0.0, rows)], axis=0
        ).astype(BF16)

    def join_heads(both_t):
        both = both_t.T
        return jnp.where(low, both[0:tokens], both[tokens:])

    def columns(p):
        return pl.ds(pl.multiple_of(p * PAIR, PAIR), PAIR)

    scale = HD**-0.5

    def forward(p, carry):
        g = p // per_kv
        query = two_heads(queries[:, columns(p)].astype(F32) * scale)
        scores = dot_nt(key_dup[g], query) + bias[...]
        top = jnp.max(scores, axis=0, keepdims=True)
        weights = jnp.exp(scores - top)
        total = jnp.sum(weights, axis=0, keepdims=True)
        out_t = dot(value_dup_t[g], weights.astype(BF16)) / total
        attn[:, columns(p)] = join_heads(out_t).astype(BF16)
        log_total[p] = top + jnp.log(total)
        return carry

    lax.fori_loop(0, pairs, forward, 0)

    attn_wide = attn[...].astype(F32)
    inv_rms = lax.rsqrt(jnp.mean(attn_wide * attn_wide, axis=1, keepdims=True) + EPSILON)
    normed = (attn_wide * inv_rms).astype(BF16)
    halves[0:tokens, :] = normed[:, 0:MAIN]
    halves[tokens:, :] = normed[:, MAIN:]

    hold_x, hold_r, hold_y = (min(h, groups) for h in (HOLD_X, HOLD_R, HOLD_Y))

    def grads_here():
        for n in range(hold_x):
            bytes_of(grad_in, group, g_send, g_recv.at[n]).wait_recv()

    send_out(row_out, row_in, x_send, x_recv, grads_here)

    scores_t = raw[...]
    total_t = jnp.sum(scores_t, axis=0, keepdims=True)
    mixing_t = scores_t / total_t
    mix_et = jnp.zeros((count, tokens), F32)
    for k in range(ids_t.shape[0]):
        mix_et = mix_et + jnp.where(expert_row == ids_t[k : k + 1, :], mixing_t[k : k + 1, :], 0.0)
    wide_shape = (count, count * ROWS)
    spread = jnp.where(iota(wide_shape, 0) == quo(iota(wide_shape, 1), ROWS), 1.0, 0.0).astype(BF16)
    lane_row = rem(iota((tokens, count * ROWS), 1), ROWS)
    rank_wide = dot(rank_et[...].T.astype(BF16), spread)
    mix_wide = dot(mix_et.T.astype(BF16), spread)
    main_mix = jnp.where(rank_wide == rem(lane_row, 8).astype(F32), mix_wide, 0.0)
    mix_main[0:tokens, :] = jnp.where(lane_row < 8, main_mix, 0.0).astype(BF16)
    mix_main[tokens:, :] = jnp.where(lane_row >= 8, main_mix, 0.0).astype(BF16)
    spill_mix = jnp.where(rank_wide == (8 + rem(lane_row, 2)).astype(F32), mix_wide, 0.0)
    mix_spill[...] = spill_mix.astype(BF16)
    for copy in weight_copies:
        copy.wait()

    main_rows = group * 8

    def unpack(buf, start, canon):
        def body(j, carry):
            both = buf[pl.ds(start + 2 * j, 2), :, 0:MAIN].astype(F32)
            at = pl.ds(pl.multiple_of(j * 16, 16), 16)
            for h in range(2):
                part = jnp.concatenate(
                    [both[0, 8 * h : 8 * h + 8], both[1, 8 * h : 8 * h + 8]], axis=0
                )
                canon[at, h * MAIN : (h + 1) * MAIN] = part.astype(BF16)
            return carry

        lax.fori_loop(0, group // 2, body, 0)
        for b in range(group // BLOCK):
            spill = buf[pl.ds(start + b * BLOCK, BLOCK), :, MAIN:].reshape(256, SPILL)
            moved = dot(to_blocks, spill).astype(BF16)
            for c in range(8):
                canon[
                    main_rows + 32 * b : main_rows + 32 * (b + 1), c * SPILL : (c + 1) * SPILL
                ] = moved[32 * c : 32 * (c + 1)]

    def repack(canon, buf, start):
        def body(j, carry):
            both = canon[pl.ds(pl.multiple_of(j * 16, 16), 16), :].astype(F32)
            for s in range(2):
                part = jnp.concatenate(
                    [both[8 * s : 8 * s + 8, 0:MAIN], both[8 * s : 8 * s + 8, MAIN:]], axis=0
                )
                buf[start + 2 * j + s, :, 0:MAIN] = part.astype(BF16)
            return carry

        lax.fori_loop(0, group // 2, body, 0)
        for b in range(group // BLOCK):
            rows = canon[main_rows + 32 * b : main_rows + 32 * (b + 1), :]
            buf[pl.ds(start + b * BLOCK, BLOCK), :, MAIN:] = spill_to_chunk(
                [rows[:, 0:MAIN], rows[:, MAIN:]]
            )

    def expert(n, carry):
        start = n * group
        bytes_of(row_in, group, x_send, x_recv.at[n]).wait_recv()

        @pl.when(n >= hold_x)
        def _():
            bytes_of(grad_in, group, g_send, g_recv.at[n]).wait_recv()

        @pl.when(n == hold_r - 1)
        def _():
            send_back(row_in, back_rows, r_send, r_recv, 1, start)

        unpack(row_in, start, canon_x)
        unpack(grad_in, start, canon_g)
        gate_act = dot(canon_x[...], w_gate[...])
        up_act = dot(canon_x[...], w_up[...])
        sigmoid = jax.nn.sigmoid(gate_act)
        silu = gate_act * sigmoid
        hidden = (silu * up_act).astype(BF16)
        hidden_grad = dot_nt(canon_g[...], w_down[...])
        gate_grad = (hidden_grad * up_act * sigmoid * (1.0 + gate_act * (1.0 - sigmoid))).astype(BF16)
        up_grad = (hidden_grad * silu).astype(BF16)
        canon_x[...] = (dot_nt(gate_grad, w_gate[...]) + dot_nt(up_grad, w_up[...])).astype(BF16)
        repack(canon_x, row_in, start)

        @pl.when(n >= hold_r - 1)
        def _():
            send_back(row_in, back_rows, r_send, r_recv, jnp.maximum(start, 1), start + group)

        canon_g[...] = dot(hidden, w_down[...]).astype(BF16)
        repack(canon_g, grad_in, start)
        return carry

    lax.fori_loop(0, groups, expert, 0)
    pltpu.make_async_copy(row_in.at[0], back_rows.at[0], r_recv.at[0]).start()

    def combine(buf, n):
        mine = pl.ds(pl.multiple_of(n * group, group), group)
        lanes = pl.ds(pl.multiple_of(n * group * ROWS, group * ROWS), group * ROWS)
        for c in range(4):
            rows = buf[mine, :, c * 256 : (c + 1) * 256].reshape(group * ROWS, 256)
            part = dot(mix_main[:, lanes], rows)
            wide[:, c * 256 : (c + 1) * 256] += part[0:tokens]
            wide[:, MAIN + c * 256 : MAIN + (c + 1) * 256] += part[tokens:]
        spill = buf[mine, :, MAIN:].reshape(group * ROWS, SPILL)
        spill_mix = mix_spill[:, lanes].astype(F32)
        column_block = quo(rem(iota((tokens, group * ROWS), 1), ROWS), 2)
        for c in range(8):
            picked = jnp.where(column_block == c, spill_mix, 0.0).astype(BF16)
            wide[:, c * SPILL : (c + 1) * SPILL] += dot(picked, spill)

    wide[...] = jnp.zeros_like(wide)

    def take_rows(n, carry):
        bytes_of(back_rows, group, r_send, r_recv.at[n]).wait_recv()

        @pl.when(n == hold_y - 1)
        def _():
            send_back(grad_in, back_outs, y_send, y_recv, 1, count)

        combine(back_rows, n)
        return carry

    lax.fori_loop(0, groups, take_rows, 0)
    pltpu.make_async_copy(grad_in.at[0], back_outs.at[0], y_recv.at[0]).start()
    normed_grad = wide[...]
    attn_again = attn[...].astype(F32)
    inv = lax.rsqrt(jnp.mean(attn_again * attn_again, axis=1, keepdims=True) + EPSILON)
    shared = jnp.mean(normed_grad * attn_again, axis=1, keepdims=True)
    wide[...] = inv * normed_grad - inv * inv * inv * attn_again * shared

    key_acc[...] = jnp.zeros_like(key_acc)
    value_acc[...] = jnp.zeros_like(value_acc)

    def backward(p, carry):
        g = p // per_kv
        query = two_heads(queries[:, columns(p)].astype(F32) * scale)
        grad = wide[:, columns(p)].astype(BF16).astype(F32)
        grads = two_heads(grad)
        product_t = (grad * attn[:, columns(p)].astype(F32)).T
        delta = jnp.concatenate(
            [
                jnp.sum(product_t[0:HD], axis=0, keepdims=True),
                jnp.sum(product_t[HD:], axis=0, keepdims=True),
            ],
            axis=1,
        )
        scores = dot_nt(key_dup[g], query) + bias[...]
        weights = jnp.exp(scores - log_total[p])
        prob_grad = dot_nt(value_dup[g], grads)
        score_grads = (weights * (prob_grad - delta)).astype(BF16)
        query_t = dot(key_dup_t[g], score_grads) * scale
        query_grad[:, columns(p)] = join_heads(query_t).astype(BF16)
        key_acc[g] += dot(score_grads, query)
        value_acc[g] += dot(weights.astype(BF16), grads)
        return carry

    lax.fori_loop(0, pairs, backward, 0)

    low_long = iota((length, PAIR), 1) < HD
    for n, acc in enumerate((key_acc, value_acc)):
        first = acc[0] + pltpu.roll(acc[0], HD, 1)
        second = acc[1] + pltpu.roll(acc[1], HD, 1)
        pair_part[:, n * PAIR : (n + 1) * PAIR] = jnp.where(low_long, first, second).astype(BF16)

    def part_copy(peer, distance):
        return pltpu.make_async_remote_copy(
            src_ref=pair_part.at[pl.ds(pl.multiple_of(peer * tokens, tokens), tokens)],
            dst_ref=pair_in.at[distance],
            send_sem=p_send.at[distance],
            recv_sem=p_recv.at[distance],
            device_id=(dp, peer),
            device_id_type=MESH,
        )

    def send_part(peer, carry):
        part_copy(peer, ctx - peer).start()
        return carry

    lax.fori_loop(0, ctx, send_part, 0)

    wide[...] = jnp.zeros_like(wide)

    def weigh(block):
        first = pl.ds(pl.multiple_of(block * BLOCK, BLOCK), BLOCK)
        sent = grad_out[first].reshape(256, CHUNK).astype(F32)
        got = back_outs[first].reshape(256, CHUNK).astype(F32)
        product = sent * got
        main = jnp.sum(product[:, 0:MAIN], axis=1, keepdims=True)
        spill = jnp.sum(product[:, MAIN:], axis=1, keepdims=True)
        ranks = dot(repeat_main, ranks_of(block))
        found = jnp.where(ranks == main_slot, main, 0.0) + jnp.where(
            ranks == spill_slot, spill, 0.0
        )
        pick_et[first, :] = jnp.sum(found.reshape(BLOCK, ROWS, tokens), axis=1)

    def take_outs(n, carry):
        bytes_of(back_outs, group, y_send, y_recv.at[n]).wait_recv()
        combine(back_outs, n)
        for b in range(group // BLOCK):
            weigh(n * (group // BLOCK) + b)
        return carry

    lax.fori_loop(0, groups, take_outs, 0)
    moe_out[...] = wide[...].astype(BF16)
    dots = pick_et[...]
    weight_grad = jnp.concatenate(
        [
            jnp.sum(
                jnp.where(expert_row == ids_t[k : k + 1, :], dots, 0.0), axis=0, keepdims=True
            )
            for k in range(ids_t.shape[0])
        ],
        axis=0,
    )
    score_grad[...] = (
        weight_grad - jnp.sum(mixing_t * weight_grad, axis=0, keepdims=True)
    ) / total_t

    def add_part(distance, total):
        part_copy(0, distance).wait_recv()
        return total + pair_in[distance].astype(F32)

    pair_sum = lax.fori_loop(1, n_ctx - ctx, add_part, pair_part[here, :].astype(F32))
    key_grad[...] = pair_sum[:, 0:PAIR].astype(BF16)
    value_grad[...] = pair_sum[:, PAIR:].astype(BF16)

    for ref, sem_s, sem_r in (
        (grad_out, g_send, g_recv.at[0]),
        (row_out, x_send, x_recv.at[0]),
        (row_in, r_send, r_recv.at[0]),
        (grad_in, y_send, y_recv.at[0]),
    ):
        bytes_of(ref, count - 1, sem_s, sem_r).wait_send()

    def sent_pair(peer, carry):
        for n in range(2):
            pair_copy(n, peer, ctx).wait_send()
        return carry

    lax.fori_loop(ctx + 1, n_ctx, sent_pair, 0)

    def sent_part(peer, carry):
        part_copy(peer, ctx - peer).wait_send()
        return carry

    lax.fori_loop(0, ctx, sent_part, 0)


def settle_kernel(*refs):
    count = (len(refs) - 2) // 3
    taken, given, held = refs[:count], refs[count : 2 * count], refs[2 * count : 3 * count]
    loads = [pltpu.make_async_copy(taken[n], held[n], refs[-2].at[n]) for n in range(count)]
    stores = [pltpu.make_async_copy(held[n], given[n], refs[-1].at[n]) for n in range(count)]
    for load in loads:
        load.start()
    for load, store in zip(loads, stores):
        load.wait()
        store.start()
    for store in stores:
        store.wait()


def settle(arrays):
    hbm = pl.BlockSpec(memory_space=pltpu.HBM)
    return pl.pallas_call(
        settle_kernel,
        out_shape=tuple(jax.ShapeDtypeStruct(a.shape, a.dtype) for a in arrays),
        in_specs=[hbm] * len(arrays),
        out_specs=[hbm] * len(arrays),
        scratch_shapes=[pltpu.VMEM(a.shape, a.dtype) for a in arrays]
        + [pltpu.SemaphoreType.DMA((len(arrays),))] * 2,
        compiler_params=pltpu.CompilerParams(vmem_limit_bytes=62 * 2**20),
        name="settle",
    )(*arrays)


def shards(
    n_dp,
    n_ctx,
    queries,
    keys,
    values,
    expert_ids,
    router_scores,
    gate_weight,
    up_weight,
    down_weight,
    out_grad,
):
    count = n_dp * n_ctx
    group = max(BLOCK, count // 4)
    groups = count // group
    tokens, width = queries.shape[1:]
    pair_width = keys.shape[2]
    top = expert_ids.shape[2]
    hidden = gate_weight.shape[2]
    length = n_ctx * tokens
    pairs = width // PAIR
    chunk_buf = pltpu.VMEM((count, ROWS, CHUNK), BF16)
    dma = pltpu.SemaphoreType.DMA
    vmem = pl.BlockSpec(memory_space=pltpu.VMEM)
    hbm = pl.BlockSpec(memory_space=pl.ANY)
    canon = pltpu.VMEM((group * 10, width), BF16)
    outs = pl.pallas_call(
        functools.partial(layer_kernel, n_dp, n_ctx, group),
        out_shape=(
            jax.ShapeDtypeStruct((tokens, width), BF16),
            jax.ShapeDtypeStruct((tokens, width), BF16),
            jax.ShapeDtypeStruct((tokens, pair_width), BF16),
            jax.ShapeDtypeStruct((tokens, pair_width), BF16),
            jax.ShapeDtypeStruct((top, tokens), F32),
        ),
        in_specs=[vmem] * 6 + [hbm] * 3,
        out_specs=[vmem] * 5,
        scratch_shapes=[
            pltpu.VMEM((width, hidden), BF16),
            pltpu.VMEM((width, hidden), BF16),
            pltpu.VMEM((hidden, width), BF16),
            chunk_buf,
            chunk_buf,
            chunk_buf,
            chunk_buf,
            chunk_buf,
            chunk_buf,
            canon,
            canon,
            pltpu.VMEM((2 * tokens, MAIN), BF16),
            pltpu.VMEM((count, tokens), F32),
            pltpu.VMEM((2 * tokens, count * ROWS), BF16),
            pltpu.VMEM((tokens, count * ROWS), BF16),
            pltpu.VMEM((length, pair_width), BF16),
            pltpu.VMEM((length, pair_width), BF16),
            pltpu.VMEM((2, length, PAIR), BF16),
            pltpu.VMEM((2, length, PAIR), BF16),
            pltpu.VMEM((2, PAIR, length), BF16),
            pltpu.VMEM((2, PAIR, length), BF16),
            pltpu.VMEM((length, 2 * tokens), F32),
            pltpu.VMEM((tokens, width), BF16),
            pltpu.VMEM((pairs, 1, 2 * tokens), F32),
            pltpu.VMEM((tokens, width), F32),
            pltpu.VMEM((count, tokens), F32),
            pltpu.VMEM((2, length, PAIR), F32),
            pltpu.VMEM((2, length, PAIR), F32),
            pltpu.VMEM((length, 2 * PAIR), BF16),
            pltpu.VMEM((n_ctx, tokens, 2 * PAIR), BF16),
            dma((3,)),
            dma((2, n_ctx)),
            dma((2, n_ctx)),
            dma,
            dma((groups,)),
            dma,
            dma((groups,)),
            dma,
            dma((groups,)),
            dma,
            dma((groups,)),
            dma((n_ctx,)),
            dma((n_ctx,)),
        ],
        compiler_params=pltpu.CompilerParams(
            collective_id=0, has_side_effects=True, vmem_limit_bytes=63 * 2**20
        ),
        name="layer",
    )(
        expert_ids[0].T,
        router_scores[0].T,
        queries[0],
        keys[0],
        values[0],
        out_grad[0],
        gate_weight[0],
        up_weight[0],
        down_weight[0],
    )
    moe_out, query_grad, key_grad, value_grad, score_grad = settle(outs)
    return (
        moe_out[None],
        query_grad[None],
        key_grad[None],
        value_grad[None],
        score_grad.T[None],
    )


def solution(mesh):
    split = P("dp", "ctx", None)
    whole = P(("dp", "ctx"), None, None)
    return jax.shard_map(
        functools.partial(shards, mesh.shape["dp"], mesh.shape["ctx"]),
        mesh=mesh,
        in_specs=(split, split, split, split, split, whole, whole, whole, split),
        out_specs=(split,) * 5,
        check_vma=False,
    )
```

```python
import functools

import jax
import jax.numpy as jnp
from jax import lax
from jax.experimental import pallas as pl
from jax.experimental.pallas import tpu as pltpu
from jax.sharding import PartitionSpec as P

HD = 64
EPSILON = 1e-06
NEGATIVE = -1e30
MESH = pl.DeviceIdType.MESH
F32 = jnp.float32
BF16 = jnp.bfloat16

ROWS = 16
MAIN = 1024
SPILL = 256
CHUNK = MAIN + SPILL
BLOCK = 16
PAIR = 128
HOLD_X, HOLD_R, HOLD_Y = 3, 3, 3


def dot(a, b):
    return lax.dot_general(a, b, (((1,), (0,)), ((), ())), preferred_element_type=F32)


def dot_nt(a, b):
    return lax.dot_general(a, b, (((1,), (1,)), ((), ())), preferred_element_type=F32)


def iota(shape, dim):
    return lax.broadcasted_iota(jnp.int32, shape, dim)


def quo(a, n):
    if a.ndim:
        return lax.shift_right_logical(a, jnp.int32(n.bit_length() - 1))
    return lax.div(a, jnp.int32(n))


def rem(a, n):
    return jnp.bitwise_and(a, n - 1) if a.ndim else lax.rem(a, jnp.int32(n))


def torus_partner(step, x, y, z, core, sign):
    inner = rem(step, 64)
    a, b, c = quo(inner, 16), rem(quo(inner, 4), 4), rem(inner, 4)
    dx = c
    dy = rem(c + b, 4)
    dz = rem(c + a + 2 * b, 4)
    tx = rem(x + sign * dx + 4, 4)
    ty = rem(y + sign * dy + 4, 4)
    tz = rem(z + sign * dz + 4, 4)
    tcore = rem(core + quo(step, 64), 2)
    return tx * 4 + rem(tz, 2) * 2 + tcore, ty * 2 + quo(tz, 2)


def partners(n_dp, n_ctx):
    dp, ctx = lax.axis_index("dp"), lax.axis_index("ctx")
    count = n_dp * n_ctx
    if (n_dp, n_ctx) == (16, 8):
        x, core = quo(dp, 4), rem(dp, 2)
        y, z = quo(ctx, 2), rem(quo(dp, 2), 2) + 2 * rem(ctx, 2)
        sign = 1 - 2 * core

        def target(step):
            step = jnp.asarray(step, jnp.int32)
            return torus_partner(step, x, y, z, core, sign)

        def source(step):
            step = jnp.asarray(step, jnp.int32)
            other = 1 - 2 * quo(step, 64)
            return torus_partner(step, x, y, z, core, -sign * other)

        return target, source
    me = dp * n_ctx + ctx

    def target(step):
        step = jnp.asarray(step, jnp.int32)
        t = rem(me + step, count)
        return quo(t, n_ctx), rem(t, n_ctx)

    def source(step):
        t = rem(me - jnp.asarray(step, jnp.int32) + count, count)
        return quo(t, n_ctx), rem(t, n_ctx)

    return target, source


def layer_kernel(
    n_dp,
    n_ctx,
    group,
    ids,
    raw,
    queries,
    keys,
    values,
    out_grad,
    gate_hbm,
    up_hbm,
    down_hbm,
    moe_out,
    query_grad,
    key_grad,
    value_grad,
    score_grad,
    w_gate,
    w_up,
    w_down,
    grad_out,
    grad_in,
    row_out,
    row_in,
    back_rows,
    back_outs,
    canon_x,
    canon_g,
    halves,
    rank_et,
    mix_main,
    mix_spill,
    all_keys,
    all_values,
    key_dup,
    value_dup,
    key_dup_t,
    value_dup_t,
    bias,
    attn,
    log_total,
    wide,
    pick_et,
    key_acc,
    value_acc,
    pair_part,
    pair_in,
    w_sem,
    kv_send,
    kv_recv,
    g_send,
    g_recv,
    x_send,
    x_recv,
    r_send,
    r_recv,
    y_send,
    y_recv,
    p_send,
    p_recv,
):
    count = n_dp * n_ctx
    groups = count // group
    tokens = queries.shape[0]
    width = queries.shape[1]
    pairs = width // PAIR
    per_kv = pairs // 2
    length = n_ctx * tokens
    dp, ctx = lax.axis_index("dp"), lax.axis_index("ctx")
    me = dp * n_ctx + ctx
    target, source = partners(n_dp, n_ctx)
    neighbour = target(1)

    weight_copies = [
        pltpu.make_async_copy(src, dst, w_sem.at[n])
        for n, (src, dst) in enumerate(((gate_hbm, w_gate), (up_hbm, w_up), (down_hbm, w_down)))
    ]
    all_keys[...] = jnp.zeros_like(all_keys)
    all_values[...] = jnp.zeros_like(all_values)

    barrier = pltpu.get_barrier_semaphore()

    def greet(step, carry):
        other = rem(me + step, count)
        where = (quo(other, n_ctx), rem(other, n_ctx))
        pl.semaphore_signal(barrier, inc=1, device_id=where, device_id_type=MESH)
        return carry

    lax.fori_loop(1, count, greet, 0)

    tdp_row, tctx_row = target(iota((count, tokens), 0))
    expert_row = (tdp_row * n_ctx + tctx_row).astype(F32)
    ids_t = ids[...].astype(F32)
    named = jnp.zeros((count, tokens), F32)
    for k in range(ids_t.shape[0]):
        named = named + jnp.where(expert_row == ids_t[k : k + 1, :], 1.0, 0.0)
    before = jnp.where(iota((tokens, tokens), 0) < iota((tokens, tokens), 1), 1.0, 0.0)
    rank = dot(named.astype(BF16), before.astype(BF16))
    rank_et[...] = jnp.where(named > 0.0, rank, -1.0)

    p_out, p_in = iota((256, 256), 0), iota((256, 256), 1)
    to_blocks = jnp.where(
        (quo(p_out, 32) == quo(rem(p_in, 16), 2))
        & (quo(rem(p_out, 32), 2) == quo(p_in, 16))
        & (rem(p_out, 2) == rem(p_in, 2)),
        1.0,
        0.0,
    ).astype(BF16)
    to_chunks = jnp.where(
        (quo(p_in, 32) == quo(rem(p_out, 16), 2))
        & (quo(rem(p_in, 32), 2) == quo(p_out, 16))
        & (rem(p_out, 2) == rem(p_in, 2)),
        1.0,
        0.0,
    ).astype(BF16)
    repeat_main = jnp.where(
        quo(iota((256, BLOCK), 0), ROWS) == iota((256, BLOCK), 1), 1.0, 0.0
    ).astype(BF16)
    repeat_spill = jnp.where(quo(iota((32, BLOCK), 0), 2) == iota((32, BLOCK), 1), 1.0, 0.0).astype(
        BF16
    )
    block_row = rem(iota((256, tokens), 0), ROWS)
    main_slot = rem(block_row, 8).astype(F32)
    spill_slot = (8 + rem(block_row, 2)).astype(F32)
    spill_row_slot = (8 + rem(iota((32, tokens), 0), 2)).astype(F32)

    def ranks_of(block):
        rows = rank_et[pl.ds(pl.multiple_of(block * BLOCK, BLOCK), BLOCK), :]
        return rows.astype(BF16)

    def pack_block(dst, block):
        ranks = ranks_of(block)
        hit = dot(repeat_main, ranks) == main_slot
        left = jnp.where(hit & (block_row < 8), 1.0, 0.0).astype(BF16)
        right = jnp.where(hit & (block_row >= 8), 1.0, 0.0).astype(BF16)
        first = pl.ds(pl.multiple_of(block * BLOCK, BLOCK), BLOCK)
        main = dot(jnp.concatenate([left, right], axis=1), halves[...])
        dst[first, :, 0:MAIN] = main.astype(BF16).reshape(BLOCK, ROWS, MAIN)
        spill_hit = jnp.where(dot(repeat_spill, ranks) == spill_row_slot, 1.0, 0.0).astype(BF16)
        rows = [
            dot(spill_hit, halves[0:tokens, :]).astype(BF16),
            dot(spill_hit, halves[tokens:, :]).astype(BF16),
        ]
        dst[first, :, MAIN:] = spill_to_chunk(rows)

    def spill_to_chunk(rows):
        stacked = jnp.concatenate(
            [part[:, c * SPILL : (c + 1) * SPILL] for part in rows for c in range(4)], axis=0
        )
        return dot(to_chunks, stacked).astype(BF16).reshape(BLOCK, ROWS, SPILL)

    def send_out(src, dst, send_sem, recv_sem, held=None):
        def send(step, carry):
            pltpu.make_async_remote_copy(
                src_ref=src.at[step],
                dst_ref=dst.at[step],
                send_sem=send_sem,
                recv_sem=recv_sem.at[quo(step, group)],
                device_id=target(step),
                device_id_type=MESH,
            ).start()
            return carry

        def body(block, carry):
            pack_block(src, block)
            if not held:
                lax.fori_loop(jnp.maximum(block * BLOCK, 1), (block + 1) * BLOCK, send, 0)
            return carry

        lax.fori_loop(0, count // BLOCK, body, 0)
        if held:
            held()
            lax.fori_loop(1, count, send, 0)
        pltpu.make_async_copy(src.at[0], dst.at[0], recv_sem.at[0]).start()

    def send_back(src, dst, send_sem, recv_sem, lo, hi, size):
        def body(step, carry):
            pltpu.make_async_remote_copy(
                src_ref=src.at[step],
                dst_ref=dst.at[step],
                send_sem=send_sem,
                recv_sem=recv_sem.at[quo(step, size)],
                device_id=source(step),
                device_id_type=MESH,
            ).start()
            return carry

        lax.fori_loop(lo, hi, body, 0)

    def bytes_of(ref, amount, sem_a, sem_b):
        part = ref.at[pl.ds(0, amount)]
        return pltpu.make_async_remote_copy(
            src_ref=part,
            dst_ref=part,
            send_sem=sem_a,
            recv_sem=sem_b,
            device_id=neighbour,
            device_id_type=MESH,
        )

    pl.semaphore_wait(barrier, count - 1)
    here = pl.ds(pl.multiple_of(ctx * tokens, tokens), tokens)
    pair_copies = ((keys, all_keys), (values, all_values))

    def pair_copy(n, peer, at):
        return pltpu.make_async_remote_copy(
            src_ref=pair_copies[n][0],
            dst_ref=pair_copies[n][1].at[pl.ds(pl.multiple_of(at * tokens, tokens), tokens)],
            send_sem=kv_send.at[n, peer],
            recv_sem=kv_recv.at[n, at],
            device_id=(dp, peer),
            device_id_type=MESH,
        )

    def send_pair(peer, carry):
        for n in range(2):
            pair_copy(n, peer, ctx).start()
        return carry

    lax.fori_loop(ctx + 1, n_ctx, send_pair, 0)
    halves[0:tokens, :] = out_grad[:, 0:MAIN]
    halves[tokens:, :] = out_grad[:, MAIN:]
    send_out(grad_out, grad_in, g_send, g_recv)
    for copy in weight_copies:
        copy.start()

    all_keys[here, :] = keys[...]
    all_values[here, :] = values[...]
    key_at = iota((length, 2 * tokens), 0)
    query_at = ctx * tokens + rem(iota((length, 2 * tokens), 1), tokens)
    bias[...] = jnp.where(key_at <= query_at, 0.0, NEGATIVE)

    def wait_pair(at, carry):
        for n in range(2):
            pair_copy(n, at, at).wait_recv()
        return carry

    lax.fori_loop(0, ctx, wait_pair, 0)
    for g in range(2):
        select = jnp.where(
            iota((PAIR, PAIR), 0) == g * HD + rem(iota((PAIR, PAIR), 1), HD), 1.0, 0.0
        ).astype(BF16)
        select_t = jnp.where(
            iota((PAIR, PAIR), 1) == g * HD + rem(iota((PAIR, PAIR), 0), HD), 1.0, 0.0
        ).astype(BF16)
        key_dup[g] = dot(all_keys[...], select).astype(BF16)
        value_dup[g] = dot(all_values[...], select).astype(BF16)
        key_dup_t[g] = dot_nt(select_t, all_keys[...]).astype(BF16)
        value_dup_t[g] = dot_nt(select_t, all_values[...]).astype(BF16)

    low = iota((tokens, PAIR), 1) < HD

    def two_heads(rows):
        return jnp.concatenate(
            [jnp.where(low, rows, 0.0), jnp.where(low, 0.0, rows)], axis=0
        ).astype(BF16)

    def join_heads(both_t):
        both = both_t.T
        return jnp.where(low, both[0:tokens], both[tokens:])

    def columns(p):
        return pl.ds(pl.multiple_of(p * PAIR, PAIR), PAIR)

    scale = HD**-0.5

    def forward(p, carry):
        g = p // per_kv
        query = two_heads(queries[:, columns(p)].astype(F32) * scale)
        scores = dot_nt(key_dup[g], query) + bias[...]
        top = jnp.max(scores, axis=0, keepdims=True)
        weights = jnp.exp(scores - top)
        total = jnp.sum(weights, axis=0, keepdims=True)
        out_t = dot(value_dup_t[g], weights.astype(BF16)) / total
        attn[:, columns(p)] = join_heads(out_t).astype(BF16)
        log_total[p] = top + jnp.log(total)
        return carry

    lax.fori_loop(0, pairs, forward, 0)

    attn_wide = attn[...].astype(F32)
    inv_rms = lax.rsqrt(jnp.mean(attn_wide * attn_wide, axis=1, keepdims=True) + EPSILON)
    normed = (attn_wide * inv_rms).astype(BF16)
    halves[0:tokens, :] = normed[:, 0:MAIN]
    halves[tokens:, :] = normed[:, MAIN:]

    hold_x, hold_r, hold_y = (min(h, groups) for h in (HOLD_X, HOLD_R, HOLD_Y))

    def grads_here():
        for n in range(hold_x):
            bytes_of(grad_in, group, g_send, g_recv.at[n]).wait_recv()

    send_out(row_out, row_in, x_send, x_recv, grads_here)

    scores_t = raw[...]
    total_t = jnp.sum(scores_t, axis=0, keepdims=True)
    mixing_t = scores_t / total_t
    mix_et = jnp.zeros((count, tokens), F32)
    for k in range(ids_t.shape[0]):
        mix_et = mix_et + jnp.where(expert_row == ids_t[k : k + 1, :], mixing_t[k : k + 1, :], 0.0)
    wide_shape = (count, count * ROWS)
    spread = jnp.where(iota(wide_shape, 0) == quo(iota(wide_shape, 1), ROWS), 1.0, 0.0).astype(BF16)
    lane_row = rem(iota((tokens, count * ROWS), 1), ROWS)
    rank_wide = dot(rank_et[...].T.astype(BF16), spread)
    mix_wide = dot(mix_et.T.astype(BF16), spread)
    main_mix = jnp.where(rank_wide == rem(lane_row, 8).astype(F32), mix_wide, 0.0)
    mix_main[0:tokens, :] = jnp.where(lane_row < 8, main_mix, 0.0).astype(BF16)
    mix_main[tokens:, :] = jnp.where(lane_row >= 8, main_mix, 0.0).astype(BF16)
    spill_mix = jnp.where(rank_wide == (8 + rem(lane_row, 2)).astype(F32), mix_wide, 0.0)
    mix_spill[...] = spill_mix.astype(BF16)
    for copy in weight_copies:
        copy.wait()

    main_rows = group * 8

    def unpack(buf, start, canon):
        def body(j, carry):
            both = buf[pl.ds(start + 2 * j, 2), :, 0:MAIN].astype(F32)
            at = pl.ds(pl.multiple_of(j * 16, 16), 16)
            for h in range(2):
                part = jnp.concatenate(
                    [both[0, 8 * h : 8 * h + 8], both[1, 8 * h : 8 * h + 8]], axis=0
                )
                canon[at, h * MAIN : (h + 1) * MAIN] = part.astype(BF16)
            return carry

        lax.fori_loop(0, group // 2, body, 0)
        for b in range(group // BLOCK):
            spill = buf[pl.ds(start + b * BLOCK, BLOCK), :, MAIN:].reshape(256, SPILL)
            moved = dot(to_blocks, spill).astype(BF16)
            for c in range(8):
                canon[
                    main_rows + 32 * b : main_rows + 32 * (b + 1), c * SPILL : (c + 1) * SPILL
                ] = moved[32 * c : 32 * (c + 1)]

    def repack(canon, buf, start):
        def body(j, carry):
            both = canon[pl.ds(pl.multiple_of(j * 16, 16), 16), :].astype(F32)
            for s in range(2):
                part = jnp.concatenate(
                    [both[8 * s : 8 * s + 8, 0:MAIN], both[8 * s : 8 * s + 8, MAIN:]], axis=0
                )
                buf[start + 2 * j + s, :, 0:MAIN] = part.astype(BF16)
            return carry

        lax.fori_loop(0, group // 2, body, 0)
        for b in range(group // BLOCK):
            rows = canon[main_rows + 32 * b : main_rows + 32 * (b + 1), :]
            buf[pl.ds(start + b * BLOCK, BLOCK), :, MAIN:] = spill_to_chunk(
                [rows[:, 0:MAIN], rows[:, MAIN:]]
            )

    def expert(n, carry):
        start = n * group
        bytes_of(row_in, group, x_send, x_recv.at[n]).wait_recv()

        @pl.when(n >= hold_x)
        def _():
            bytes_of(grad_in, group, g_send, g_recv.at[n]).wait_recv()

        @pl.when(n == hold_r - 1)
        def _():
            send_back(row_in, back_rows, r_send, r_recv, 1, start, group)

        unpack(row_in, start, canon_x)
        unpack(grad_in, start, canon_g)
        gate_act = dot(canon_x[...], w_gate[...])
        up_act = dot(canon_x[...], w_up[...])
        sigmoid = jax.nn.sigmoid(gate_act)
        silu = gate_act * sigmoid
        hidden = (silu * up_act).astype(BF16)
        hidden_grad = dot_nt(canon_g[...], w_down[...])
        gate_grad = (hidden_grad * up_act * sigmoid * (1.0 + gate_act * (1.0 - sigmoid))).astype(BF16)
        up_grad = (hidden_grad * silu).astype(BF16)
        canon_x[...] = (dot_nt(gate_grad, w_gate[...]) + dot_nt(up_grad, w_up[...])).astype(BF16)
        repack(canon_x, row_in, start)

        @pl.when(n >= hold_r - 1)
        def _():
            first = jnp.maximum(start, 1)
            send_back(row_in, back_rows, r_send, r_recv, first, start + group, group)

        canon_g[...] = dot(hidden, w_down[...]).astype(BF16)
        repack(canon_g, grad_in, start)
        return carry

    lax.fori_loop(0, groups, expert, 0)
    pltpu.make_async_copy(row_in.at[0], back_rows.at[0], r_recv.at[0]).start()

    def combine(buf, n, size):
        mine = pl.ds(pl.multiple_of(n * size, size), size)
        lanes = pl.ds(pl.multiple_of(n * size * ROWS, size * ROWS), size * ROWS)
        for c in range(4):
            rows = buf[mine, :, c * 256 : (c + 1) * 256].reshape(size * ROWS, 256)
            part = dot(mix_main[:, lanes], rows)
            wide[:, c * 256 : (c + 1) * 256] += part[0:tokens]
            wide[:, MAIN + c * 256 : MAIN + (c + 1) * 256] += part[tokens:]
        spill = buf[mine, :, MAIN:].reshape(size * ROWS, SPILL)
        spill_mix = mix_spill[:, lanes].astype(F32)
        column_block = quo(rem(iota((tokens, size * ROWS), 1), ROWS), 2)
        for c in range(8):
            picked = jnp.where(column_block == c, spill_mix, 0.0).astype(BF16)
            wide[:, c * SPILL : (c + 1) * SPILL] += dot(picked, spill)

    late = max(1, count - BLOCK)

    wide[...] = jnp.zeros_like(wide)

    def take_rows(n, carry):
        bytes_of(back_rows, group, r_send, r_recv.at[n]).wait_recv()

        @pl.when(n == hold_y - 1)
        def _():
            send_back(grad_in, back_outs, y_send, y_recv, 1, late, BLOCK)

        combine(back_rows, n, group)
        return carry

    lax.fori_loop(0, groups, take_rows, 0)
    pltpu.make_async_copy(grad_in.at[0], back_outs.at[0], y_recv.at[0]).start()
    normed_grad = wide[...]
    attn_again = attn[...].astype(F32)
    inv = lax.rsqrt(jnp.mean(attn_again * attn_again, axis=1, keepdims=True) + EPSILON)
    shared = jnp.mean(normed_grad * attn_again, axis=1, keepdims=True)
    wide[...] = inv * normed_grad - inv * inv * inv * attn_again * shared

    key_acc[...] = jnp.zeros_like(key_acc)
    value_acc[...] = jnp.zeros_like(value_acc)

    def backward(p, carry):
        g = p // per_kv
        query = two_heads(queries[:, columns(p)].astype(F32) * scale)
        grad = wide[:, columns(p)].astype(BF16).astype(F32)
        grads = two_heads(grad)
        product_t = (grad * attn[:, columns(p)].astype(F32)).T
        delta = jnp.concatenate(
            [
                jnp.sum(product_t[0:HD], axis=0, keepdims=True),
                jnp.sum(product_t[HD:], axis=0, keepdims=True),
            ],
            axis=1,
        )
        scores = dot_nt(key_dup[g], query) + bias[...]
        weights = jnp.exp(scores - log_total[p])
        prob_grad = dot_nt(value_dup[g], grads)
        score_grads = (weights * (prob_grad - delta)).astype(BF16)
        query_t = dot(key_dup_t[g], score_grads) * scale
        query_grad[:, columns(p)] = join_heads(query_t).astype(BF16)
        key_acc[g] += dot(score_grads, query)
        value_acc[g] += dot(weights.astype(BF16), grads)
        return carry

    lax.fori_loop(0, pairs, backward, 0)

    low_long = iota((length, PAIR), 1) < HD
    for n, acc in enumerate((key_acc, value_acc)):
        first = acc[0] + pltpu.roll(acc[0], HD, 1)
        second = acc[1] + pltpu.roll(acc[1], HD, 1)
        pair_part[:, n * PAIR : (n + 1) * PAIR] = jnp.where(low_long, first, second).astype(BF16)

    def part_copy(peer, distance):
        return pltpu.make_async_remote_copy(
            src_ref=pair_part.at[pl.ds(pl.multiple_of(peer * tokens, tokens), tokens)],
            dst_ref=pair_in.at[distance],
            send_sem=p_send.at[distance],
            recv_sem=p_recv.at[distance],
            device_id=(dp, peer),
            device_id_type=MESH,
        )

    def send_part(peer, carry):
        part_copy(peer, ctx - peer).start()
        return carry

    lax.fori_loop(0, ctx, send_part, 0)
    send_back(grad_in, back_outs, y_send, y_recv, late, count, BLOCK)

    wide[...] = jnp.zeros_like(wide)

    def weigh(block):
        first = pl.ds(pl.multiple_of(block * BLOCK, BLOCK), BLOCK)
        sent = grad_out[first].reshape(256, CHUNK).astype(F32)
        got = back_outs[first].reshape(256, CHUNK).astype(F32)
        product = sent * got
        main = jnp.sum(product[:, 0:MAIN], axis=1, keepdims=True)
        spill = jnp.sum(product[:, MAIN:], axis=1, keepdims=True)
        ranks = dot(repeat_main, ranks_of(block))
        found = jnp.where(ranks == main_slot, main, 0.0) + jnp.where(
            ranks == spill_slot, spill, 0.0
        )
        pick_et[first, :] = jnp.sum(found.reshape(BLOCK, ROWS, tokens), axis=1)

    def take_outs(n, carry):
        bytes_of(back_outs, BLOCK, y_send, y_recv.at[n]).wait_recv()
        combine(back_outs, n, BLOCK)
        weigh(n)
        return carry

    lax.fori_loop(0, count // BLOCK, take_outs, 0)
    moe_out[...] = wide[...].astype(BF16)
    dots = pick_et[...]
    weight_grad = jnp.concatenate(
        [
            jnp.sum(
                jnp.where(expert_row == ids_t[k : k + 1, :], dots, 0.0), axis=0, keepdims=True
            )
            for k in range(ids_t.shape[0])
        ],
        axis=0,
    )
    score_grad[...] = (
        weight_grad - jnp.sum(mixing_t * weight_grad, axis=0, keepdims=True)
    ) / total_t

    def add_part(distance, total):
        part_copy(0, distance).wait_recv()
        return total + pair_in[distance].astype(F32)

    pair_sum = lax.fori_loop(1, n_ctx - ctx, add_part, pair_part[here, :].astype(F32))
    key_grad[...] = pair_sum[:, 0:PAIR].astype(BF16)
    value_grad[...] = pair_sum[:, PAIR:].astype(BF16)

    for ref, sem_s, sem_r in (
        (grad_out, g_send, g_recv.at[0]),
        (row_out, x_send, x_recv.at[0]),
        (row_in, r_send, r_recv.at[0]),
        (grad_in, y_send, y_recv.at[0]),
    ):
        bytes_of(ref, count - 1, sem_s, sem_r).wait_send()

    def sent_pair(peer, carry):
        for n in range(2):
            pair_copy(n, peer, ctx).wait_send()
        return carry

    lax.fori_loop(ctx + 1, n_ctx, sent_pair, 0)

    def sent_part(peer, carry):
        part_copy(peer, ctx - peer).wait_send()
        return carry

    lax.fori_loop(0, ctx, sent_part, 0)


def settle_kernel(*refs):
    count = (len(refs) - 2) // 3
    taken, given, held = refs[:count], refs[count : 2 * count], refs[2 * count : 3 * count]
    loads = [pltpu.make_async_copy(taken[n], held[n], refs[-2].at[n]) for n in range(count)]
    stores = [pltpu.make_async_copy(held[n], given[n], refs[-1].at[n]) for n in range(count)]
    for load in loads:
        load.start()
    for load, store in zip(loads, stores):
        load.wait()
        store.start()
    for store in stores:
        store.wait()


def settle(arrays):
    hbm = pl.BlockSpec(memory_space=pltpu.HBM)
    return pl.pallas_call(
        settle_kernel,
        out_shape=tuple(jax.ShapeDtypeStruct(a.shape, a.dtype) for a in arrays),
        in_specs=[hbm] * len(arrays),
        out_specs=[hbm] * len(arrays),
        scratch_shapes=[pltpu.VMEM(a.shape, a.dtype) for a in arrays]
        + [pltpu.SemaphoreType.DMA((len(arrays),))] * 2,
        compiler_params=pltpu.CompilerParams(vmem_limit_bytes=62 * 2**20),
        name="settle",
    )(*arrays)


def shards(
    n_dp,
    n_ctx,
    queries,
    keys,
    values,
    expert_ids,
    router_scores,
    gate_weight,
    up_weight,
    down_weight,
    out_grad,
):
    count = n_dp * n_ctx
    group = max(BLOCK, count // 4)
    groups = count // group
    tokens, width = queries.shape[1:]
    pair_width = keys.shape[2]
    top = expert_ids.shape[2]
    hidden = gate_weight.shape[2]
    length = n_ctx * tokens
    pairs = width // PAIR
    chunk_buf = pltpu.VMEM((count, ROWS, CHUNK), BF16)
    dma = pltpu.SemaphoreType.DMA
    vmem = pl.BlockSpec(memory_space=pltpu.VMEM)
    hbm = pl.BlockSpec(memory_space=pl.ANY)
    canon = pltpu.VMEM((group * 10, width), BF16)
    outs = pl.pallas_call(
        functools.partial(layer_kernel, n_dp, n_ctx, group),
        out_shape=(
            jax.ShapeDtypeStruct((tokens, width), BF16),
            jax.ShapeDtypeStruct((tokens, width), BF16),
            jax.ShapeDtypeStruct((tokens, pair_width), BF16),
            jax.ShapeDtypeStruct((tokens, pair_width), BF16),
            jax.ShapeDtypeStruct((top, tokens), F32),
        ),
        in_specs=[vmem] * 6 + [hbm] * 3,
        out_specs=[vmem] * 5,
        scratch_shapes=[
            pltpu.VMEM((width, hidden), BF16),
            pltpu.VMEM((width, hidden), BF16),
            pltpu.VMEM((hidden, width), BF16),
            chunk_buf,
            chunk_buf,
            chunk_buf,
            chunk_buf,
            chunk_buf,
            chunk_buf,
            canon,
            canon,
            pltpu.VMEM((2 * tokens, MAIN), BF16),
            pltpu.VMEM((count, tokens), F32),
            pltpu.VMEM((2 * tokens, count * ROWS), BF16),
            pltpu.VMEM((tokens, count * ROWS), BF16),
            pltpu.VMEM((length, pair_width), BF16),
            pltpu.VMEM((length, pair_width), BF16),
            pltpu.VMEM((2, length, PAIR), BF16),
            pltpu.VMEM((2, length, PAIR), BF16),
            pltpu.VMEM((2, PAIR, length), BF16),
            pltpu.VMEM((2, PAIR, length), BF16),
            pltpu.VMEM((length, 2 * tokens), F32),
            pltpu.VMEM((tokens, width), BF16),
            pltpu.VMEM((pairs, 1, 2 * tokens), F32),
            pltpu.VMEM((tokens, width), F32),
            pltpu.VMEM((count, tokens), F32),
            pltpu.VMEM((2, length, PAIR), F32),
            pltpu.VMEM((2, length, PAIR), F32),
            pltpu.VMEM((length, 2 * PAIR), BF16),
            pltpu.VMEM((n_ctx, tokens, 2 * PAIR), BF16),
            dma((3,)),
            dma((2, n_ctx)),
            dma((2, n_ctx)),
            dma,
            dma((groups,)),
            dma,
            dma((groups,)),
            dma,
            dma((groups,)),
            dma,
            dma((count // BLOCK,)),
            dma((n_ctx,)),
            dma((n_ctx,)),
        ],
        compiler_params=pltpu.CompilerParams(
            collective_id=0, has_side_effects=True, vmem_limit_bytes=63 * 2**20
        ),
        name="layer",
    )(
        expert_ids[0].T,
        router_scores[0].T,
        queries[0],
        keys[0],
        values[0],
        out_grad[0],
        gate_weight[0],
        up_weight[0],
        down_weight[0],
    )
    moe_out, query_grad, key_grad, value_grad, score_grad = settle(outs)
    return (
        moe_out[None],
        query_grad[None],
        key_grad[None],
        value_grad[None],
        score_grad.T[None],
    )


def solution(mesh):
    split = P("dp", "ctx", None)
    whole = P(("dp", "ctx"), None, None)
    return jax.shard_map(
        functools.partial(shards, mesh.shape["dp"], mesh.shape["ctx"]),
        mesh=mesh,
        in_specs=(split, split, split, split, split, whole, whole, whole, split),
        out_specs=(split,) * 5,
        check_vma=False,
    )
```

```python
import functools

import jax
import jax.numpy as jnp
from jax import lax
from jax.experimental import pallas as pl
from jax.experimental.pallas import tpu as pltpu
from jax.sharding import PartitionSpec as P

HD = 64
EPSILON = 1e-06
NEGATIVE = -1e30
MESH = pl.DeviceIdType.MESH
F32 = jnp.float32
BF16 = jnp.bfloat16

ROWS = 16
MAIN = 1024
SPILL = 256
CHUNK = MAIN + SPILL
BLOCK = 16
PAIR = 128
HOLD_X, HOLD_R, HOLD_Y = 3, 3, 3


def dot(a, b):
    return lax.dot_general(a, b, (((1,), (0,)), ((), ())), preferred_element_type=F32)


def dot_nt(a, b):
    return lax.dot_general(a, b, (((1,), (1,)), ((), ())), preferred_element_type=F32)


def iota(shape, dim):
    return lax.broadcasted_iota(jnp.int32, shape, dim)


def quo(a, n):
    if a.ndim:
        return lax.shift_right_logical(a, jnp.int32(n.bit_length() - 1))
    return lax.div(a, jnp.int32(n))


def rem(a, n):
    return jnp.bitwise_and(a, n - 1) if a.ndim else lax.rem(a, jnp.int32(n))


def torus_partner(step, x, y, z, core, sign):
    inner = rem(step, 64)
    a, b, c = quo(inner, 16), rem(quo(inner, 4), 4), rem(inner, 4)
    dx = c
    dy = rem(c + b, 4)
    dz = rem(c + a + 2 * b, 4)
    tx = rem(x + sign * dx + 4, 4)
    ty = rem(y + sign * dy + 4, 4)
    tz = rem(z + sign * dz + 4, 4)
    tcore = rem(core + quo(step, 64), 2)
    return tx * 4 + rem(tz, 2) * 2 + tcore, ty * 2 + quo(tz, 2)


def partners(n_dp, n_ctx):
    dp, ctx = lax.axis_index("dp"), lax.axis_index("ctx")
    count = n_dp * n_ctx
    if (n_dp, n_ctx) == (16, 8):
        x, core = quo(dp, 4), rem(dp, 2)
        y, z = quo(ctx, 2), rem(quo(dp, 2), 2) + 2 * rem(ctx, 2)
        sign = 1 - 2 * core

        def target(step):
            step = jnp.asarray(step, jnp.int32)
            return torus_partner(step, x, y, z, core, sign)

        def source(step):
            step = jnp.asarray(step, jnp.int32)
            other = 1 - 2 * quo(step, 64)
            return torus_partner(step, x, y, z, core, -sign * other)

        return target, source
    me = dp * n_ctx + ctx

    def target(step):
        step = jnp.asarray(step, jnp.int32)
        t = rem(me + step, count)
        return quo(t, n_ctx), rem(t, n_ctx)

    def source(step):
        t = rem(me - jnp.asarray(step, jnp.int32) + count, count)
        return quo(t, n_ctx), rem(t, n_ctx)

    return target, source


def layer_kernel(
    n_dp,
    n_ctx,
    group,
    ids,
    raw,
    queries,
    keys,
    values,
    out_grad,
    gate_hbm,
    up_hbm,
    down_hbm,
    moe_out,
    query_grad,
    key_grad,
    value_grad,
    score_grad,
    w_gate,
    w_up,
    w_down,
    grad_out,
    grad_in,
    row_out,
    row_in,
    back_rows,
    back_outs,
    canon_x,
    canon_g,
    halves,
    rank_et,
    mix_main,
    mix_spill,
    all_keys,
    all_values,
    key_dup,
    value_dup,
    key_dup_t,
    value_dup_t,
    bias,
    attn,
    log_total,
    wide,
    pick_et,
    key_acc,
    value_acc,
    pair_part,
    pair_in,
    w_sem,
    kv_send,
    kv_recv,
    g_send,
    g_recv,
    x_send,
    x_recv,
    r_send,
    r_recv,
    y_send,
    y_recv,
    p_send,
    p_recv,
):
    count = n_dp * n_ctx
    groups = count // group
    tokens = queries.shape[0]
    width = queries.shape[1]
    pairs = width // PAIR
    per_kv = pairs // 2
    length = n_ctx * tokens
    dp, ctx = lax.axis_index("dp"), lax.axis_index("ctx")
    me = dp * n_ctx + ctx
    target, source = partners(n_dp, n_ctx)
    neighbour = target(1)

    weight_copies = [
        pltpu.make_async_copy(src, dst, w_sem.at[n])
        for n, (src, dst) in enumerate(((gate_hbm, w_gate), (up_hbm, w_up), (down_hbm, w_down)))
    ]
    all_keys[...] = jnp.zeros_like(all_keys)
    all_values[...] = jnp.zeros_like(all_values)

    barrier = pltpu.get_barrier_semaphore()

    def greet(step, carry):
        other = rem(me + step, count)
        where = (quo(other, n_ctx), rem(other, n_ctx))
        pl.semaphore_signal(barrier, inc=1, device_id=where, device_id_type=MESH)
        return carry

    lax.fori_loop(1, count, greet, 0)

    tdp_row, tctx_row = target(iota((count, tokens), 0))
    expert_row = (tdp_row * n_ctx + tctx_row).astype(F32)
    ids_t = ids[...].astype(F32)
    named = jnp.zeros((count, tokens), F32)
    for k in range(ids_t.shape[0]):
        named = named + jnp.where(expert_row == ids_t[k : k + 1, :], 1.0, 0.0)
    before = jnp.where(iota((tokens, tokens), 0) < iota((tokens, tokens), 1), 1.0, 0.0)
    rank = dot(named.astype(BF16), before.astype(BF16))
    rank_et[...] = jnp.where(named > 0.0, rank, -1.0)

    p_out, p_in = iota((256, 256), 0), iota((256, 256), 1)
    to_blocks = jnp.where(
        (quo(p_out, 32) == quo(rem(p_in, 16), 2))
        & (quo(rem(p_out, 32), 2) == quo(p_in, 16))
        & (rem(p_out, 2) == rem(p_in, 2)),
        1.0,
        0.0,
    ).astype(BF16)
    to_chunks = jnp.where(
        (quo(p_in, 32) == quo(rem(p_out, 16), 2))
        & (quo(rem(p_in, 32), 2) == quo(p_out, 16))
        & (rem(p_out, 2) == rem(p_in, 2)),
        1.0,
        0.0,
    ).astype(BF16)
    repeat_main = jnp.where(
        quo(iota((256, BLOCK), 0), ROWS) == iota((256, BLOCK), 1), 1.0, 0.0
    ).astype(BF16)
    repeat_spill = jnp.where(quo(iota((32, BLOCK), 0), 2) == iota((32, BLOCK), 1), 1.0, 0.0).astype(
        BF16
    )
    block_row = rem(iota((256, tokens), 0), ROWS)
    main_slot = rem(block_row, 8).astype(F32)
    spill_slot = (8 + rem(block_row, 2)).astype(F32)
    spill_row_slot = (8 + rem(iota((32, tokens), 0), 2)).astype(F32)

    def ranks_of(block):
        rows = rank_et[pl.ds(pl.multiple_of(block * BLOCK, BLOCK), BLOCK), :]
        return rows.astype(BF16)

    def pack_block(dst, block):
        ranks = ranks_of(block)
        hit = dot(repeat_main, ranks) == main_slot
        left = jnp.where(hit & (block_row < 8), 1.0, 0.0).astype(BF16)
        right = jnp.where(hit & (block_row >= 8), 1.0, 0.0).astype(BF16)
        first = pl.ds(pl.multiple_of(block * BLOCK, BLOCK), BLOCK)
        main = dot(jnp.concatenate([left, right], axis=1), halves[...])
        dst[first, :, 0:MAIN] = main.astype(BF16).reshape(BLOCK, ROWS, MAIN)
        spill_hit = jnp.where(dot(repeat_spill, ranks) == spill_row_slot, 1.0, 0.0).astype(BF16)
        rows = [
            dot(spill_hit, halves[0:tokens, :]).astype(BF16),
            dot(spill_hit, halves[tokens:, :]).astype(BF16),
        ]
        dst[first, :, MAIN:] = spill_to_chunk(rows)

    def spill_to_chunk(rows):
        stacked = jnp.concatenate(
            [part[:, c * SPILL : (c + 1) * SPILL] for part in rows for c in range(4)], axis=0
        )
        return dot(to_chunks, stacked).astype(BF16).reshape(BLOCK, ROWS, SPILL)

    def send_out(src, dst, send_sem, recv_sem, held=None):
        def send(step, carry):
            pltpu.make_async_remote_copy(
                src_ref=src.at[step],
                dst_ref=dst.at[step],
                send_sem=send_sem,
                recv_sem=recv_sem.at[quo(step, group)],
                device_id=target(step),
                device_id_type=MESH,
            ).start()
            return carry

        def body(block, carry):
            if held:
                pack_block(src, block)
            else:
                pl.when(block > 0)(lambda: pack_block(src, block))
                lax.fori_loop(jnp.maximum(block * BLOCK, 1), (block + 1) * BLOCK, send, 0)
            return carry

        lax.fori_loop(0, count // BLOCK, body, 0)
        if held:
            held()
            lax.fori_loop(1, count, send, 0)
        pltpu.make_async_copy(src.at[0], dst.at[0], recv_sem.at[0]).start()

    def send_back(src, dst, send_sem, recv_sem, lo, hi):
        def body(step, carry):
            pltpu.make_async_remote_copy(
                src_ref=src.at[step],
                dst_ref=dst.at[step],
                send_sem=send_sem,
                recv_sem=recv_sem.at[quo(step, group)],
                device_id=source(step),
                device_id_type=MESH,
            ).start()
            return carry

        lax.fori_loop(lo, hi, body, 0)

    def bytes_of(ref, amount, sem_a, sem_b):
        part = ref.at[pl.ds(0, amount)]
        return pltpu.make_async_remote_copy(
            src_ref=part,
            dst_ref=part,
            send_sem=sem_a,
            recv_sem=sem_b,
            device_id=neighbour,
            device_id_type=MESH,
        )

    halves[0:tokens, :] = out_grad[:, 0:MAIN]
    halves[tokens:, :] = out_grad[:, MAIN:]
    pack_block(grad_out, 0)
    pl.semaphore_wait(barrier, count - 1)
    here = pl.ds(pl.multiple_of(ctx * tokens, tokens), tokens)
    pair_copies = ((keys, all_keys), (values, all_values))

    def pair_copy(n, peer, at):
        return pltpu.make_async_remote_copy(
            src_ref=pair_copies[n][0],
            dst_ref=pair_copies[n][1].at[pl.ds(pl.multiple_of(at * tokens, tokens), tokens)],
            send_sem=kv_send.at[n, peer],
            recv_sem=kv_recv.at[n, at],
            device_id=(dp, peer),
            device_id_type=MESH,
        )

    def send_pair(peer, carry):
        for n in range(2):
            pair_copy(n, peer, ctx).start()
        return carry

    lax.fori_loop(ctx + 1, n_ctx, send_pair, 0)
    send_out(grad_out, grad_in, g_send, g_recv)
    for copy in weight_copies:
        copy.start()

    all_keys[here, :] = keys[...]
    all_values[here, :] = values[...]
    key_at = iota((length, 2 * tokens), 0)
    query_at = ctx * tokens + rem(iota((length, 2 * tokens), 1), tokens)
    bias[...] = jnp.where(key_at <= query_at, 0.0, NEGATIVE)

    def wait_pair(at, carry):
        for n in range(2):
            pair_copy(n, at, at).wait_recv()
        return carry

    lax.fori_loop(0, ctx, wait_pair, 0)
    for g in range(2):
        select = jnp.where(
            iota((PAIR, PAIR), 0) == g * HD + rem(iota((PAIR, PAIR), 1), HD), 1.0, 0.0
        ).astype(BF16)
        select_t = jnp.where(
            iota((PAIR, PAIR), 1) == g * HD + rem(iota((PAIR, PAIR), 0), HD), 1.0, 0.0
        ).astype(BF16)
        key_dup[g] = dot(all_keys[...], select).astype(BF16)
        value_dup[g] = dot(all_values[...], select).astype(BF16)
        key_dup_t[g] = dot_nt(select_t, all_keys[...]).astype(BF16)
        value_dup_t[g] = dot_nt(select_t, all_values[...]).astype(BF16)

    low = iota((tokens, PAIR), 1) < HD

    def two_heads(rows):
        return jnp.concatenate(
            [jnp.where(low, rows, 0.0), jnp.where(low, 0.0, rows)], axis=0
        ).astype(BF16)

    def join_heads(both_t):
        both = both_t.T
        return jnp.where(low, both[0:tokens], both[tokens:])

    def columns(p):
        return pl.ds(pl.multiple_of(p * PAIR, PAIR), PAIR)

    scale = HD**-0.5

    def forward(p, carry):
        g = p // per_kv
        query = two_heads(queries[:, columns(p)].astype(F32) * scale)
        scores = dot_nt(key_dup[g], query) + bias[...]
        top = jnp.max(scores, axis=0, keepdims=True)
        weights = jnp.exp(scores - top)
        total = jnp.sum(weights, axis=0, keepdims=True)
        out_t = dot(value_dup_t[g], weights.astype(BF16)) / total
        attn[:, columns(p)] = join_heads(out_t).astype(BF16)
        log_total[p] = top + jnp.log(total)
        return carry

    lax.fori_loop(0, pairs, forward, 0)

    attn_wide = attn[...].astype(F32)
    inv_rms = lax.rsqrt(jnp.mean(attn_wide * attn_wide, axis=1, keepdims=True) + EPSILON)
    normed = (attn_wide * inv_rms).astype(BF16)
    halves[0:tokens, :] = normed[:, 0:MAIN]
    halves[tokens:, :] = normed[:, MAIN:]

    hold_x, hold_r, hold_y = (min(h, groups) for h in (HOLD_X, HOLD_R, HOLD_Y))

    def grads_here():
        for n in range(hold_x):
            bytes_of(grad_in, group, g_send, g_recv.at[n]).wait_recv()

    send_out(row_out, row_in, x_send, x_recv, grads_here)

    scores_t = raw[...]
    total_t = jnp.sum(scores_t, axis=0, keepdims=True)
    mixing_t = scores_t / total_t
    mix_et = jnp.zeros((count, tokens), F32)
    for k in range(ids_t.shape[0]):
        mix_et = mix_et + jnp.where(expert_row == ids_t[k : k + 1, :], mixing_t[k : k + 1, :], 0.0)
    wide_shape = (count, count * ROWS)
    spread = jnp.where(iota(wide_shape, 0) == quo(iota(wide_shape, 1), ROWS), 1.0, 0.0).astype(BF16)
    lane_row = rem(iota((tokens, count * ROWS), 1), ROWS)
    rank_wide = dot(rank_et[...].T.astype(BF16), spread)
    mix_wide = dot(mix_et.T.astype(BF16), spread)
    main_mix = jnp.where(rank_wide == rem(lane_row, 8).astype(F32), mix_wide, 0.0)
    mix_main[0:tokens, :] = jnp.where(lane_row < 8, main_mix, 0.0).astype(BF16)
    mix_main[tokens:, :] = jnp.where(lane_row >= 8, main_mix, 0.0).astype(BF16)
    spill_mix = jnp.where(rank_wide == (8 + rem(lane_row, 2)).astype(F32), mix_wide, 0.0)
    mix_spill[...] = spill_mix.astype(BF16)
    for copy in weight_copies:
        copy.wait()

    main_rows = group * 8

    def unpack(buf, start, canon):
        def body(j, carry):
            both = buf[pl.ds(start + 2 * j, 2), :, 0:MAIN].astype(F32)
            at = pl.ds(pl.multiple_of(j * 16, 16), 16)
            for h in range(2):
                part = jnp.concatenate(
                    [both[0, 8 * h : 8 * h + 8], both[1, 8 * h : 8 * h + 8]], axis=0
                )
                canon[at, h * MAIN : (h + 1) * MAIN] = part.astype(BF16)
            return carry

        lax.fori_loop(0, group // 2, body, 0)
        for b in range(group // BLOCK):
            spill = buf[pl.ds(start + b * BLOCK, BLOCK), :, MAIN:].reshape(256, SPILL)
            moved = dot(to_blocks, spill).astype(BF16)
            for c in range(8):
                canon[
                    main_rows + 32 * b : main_rows + 32 * (b + 1), c * SPILL : (c + 1) * SPILL
                ] = moved[32 * c : 32 * (c + 1)]

    def repack(canon, buf, start):
        def body(j, carry):
            both = canon[pl.ds(pl.multiple_of(j * 16, 16), 16), :].astype(F32)
            for s in range(2):
                part = jnp.concatenate(
                    [both[8 * s : 8 * s + 8, 0:MAIN], both[8 * s : 8 * s + 8, MAIN:]], axis=0
                )
                buf[start + 2 * j + s, :, 0:MAIN] = part.astype(BF16)
            return carry

        lax.fori_loop(0, group // 2, body, 0)
        for b in range(group // BLOCK):
            rows = canon[main_rows + 32 * b : main_rows + 32 * (b + 1), :]
            buf[pl.ds(start + b * BLOCK, BLOCK), :, MAIN:] = spill_to_chunk(
                [rows[:, 0:MAIN], rows[:, MAIN:]]
            )

    def expert(n, carry):
        start = n * group
        bytes_of(row_in, group, x_send, x_recv.at[n]).wait_recv()

        @pl.when(n >= hold_x)
        def _():
            bytes_of(grad_in, group, g_send, g_recv.at[n]).wait_recv()

        @pl.when(n == hold_r - 1)
        def _():
            send_back(row_in, back_rows, r_send, r_recv, 1, start)

        unpack(row_in, start, canon_x)
        unpack(grad_in, start, canon_g)
        gate_act = dot(canon_x[...], w_gate[...])
        up_act = dot(canon_x[...], w_up[...])
        sigmoid = jax.nn.sigmoid(gate_act)
        silu = gate_act * sigmoid
        hidden = (silu * up_act).astype(BF16)
        hidden_grad = dot_nt(canon_g[...], w_down[...])
        gate_grad = (hidden_grad * up_act * sigmoid * (1.0 + gate_act * (1.0 - sigmoid))).astype(BF16)
        up_grad = (hidden_grad * silu).astype(BF16)
        canon_x[...] = (dot_nt(gate_grad, w_gate[...]) + dot_nt(up_grad, w_up[...])).astype(BF16)
        repack(canon_x, row_in, start)

        @pl.when(n >= hold_r - 1)
        def _():
            send_back(row_in, back_rows, r_send, r_recv, jnp.maximum(start, 1), start + group)

        canon_g[...] = dot(hidden, w_down[...]).astype(BF16)
        repack(canon_g, grad_in, start)
        return carry

    lax.fori_loop(0, groups, expert, 0)
    pltpu.make_async_copy(row_in.at[0], back_rows.at[0], r_recv.at[0]).start()

    def combine(buf, n):
        mine = pl.ds(pl.multiple_of(n * group, group), group)
        lanes = pl.ds(pl.multiple_of(n * group * ROWS, group * ROWS), group * ROWS)
        for c in range(4):
            rows = buf[mine, :, c * 256 : (c + 1) * 256].reshape(group * ROWS, 256)
            part = dot(mix_main[:, lanes], rows)
            wide[:, c * 256 : (c + 1) * 256] += part[0:tokens]
            wide[:, MAIN + c * 256 : MAIN + (c + 1) * 256] += part[tokens:]
        spill = buf[mine, :, MAIN:].reshape(group * ROWS, SPILL)
        spill_mix = mix_spill[:, lanes].astype(F32)
        column_block = quo(rem(iota((tokens, group * ROWS), 1), ROWS), 2)
        for c in range(8):
            picked = jnp.where(column_block == c, spill_mix, 0.0).astype(BF16)
            wide[:, c * SPILL : (c + 1) * SPILL] += dot(picked, spill)

    wide[...] = jnp.zeros_like(wide)

    def take_rows(n, carry):
        bytes_of(back_rows, group, r_send, r_recv.at[n]).wait_recv()

        @pl.when(n == hold_y - 1)
        def _():
            send_back(grad_in, back_outs, y_send, y_recv, 1, count)

        combine(back_rows, n)
        return carry

    lax.fori_loop(0, groups, take_rows, 0)
    pltpu.make_async_copy(grad_in.at[0], back_outs.at[0], y_recv.at[0]).start()
    normed_grad = wide[...]
    attn_again = attn[...].astype(F32)
    inv = lax.rsqrt(jnp.mean(attn_again * attn_again, axis=1, keepdims=True) + EPSILON)
    shared = jnp.mean(normed_grad * attn_again, axis=1, keepdims=True)
    wide[...] = inv * normed_grad - inv * inv * inv * attn_again * shared

    key_acc[...] = jnp.zeros_like(key_acc)
    value_acc[...] = jnp.zeros_like(value_acc)

    def backward(p, carry):
        g = p // per_kv
        query = two_heads(queries[:, columns(p)].astype(F32) * scale)
        grad = wide[:, columns(p)].astype(BF16).astype(F32)
        grads = two_heads(grad)
        product_t = (grad * attn[:, columns(p)].astype(F32)).T
        delta = jnp.concatenate(
            [
                jnp.sum(product_t[0:HD], axis=0, keepdims=True),
                jnp.sum(product_t[HD:], axis=0, keepdims=True),
            ],
            axis=1,
        )
        scores = dot_nt(key_dup[g], query) + bias[...]
        weights = jnp.exp(scores - log_total[p])
        prob_grad = dot_nt(value_dup[g], grads)
        score_grads = (weights * (prob_grad - delta)).astype(BF16)
        query_t = dot(key_dup_t[g], score_grads) * scale
        query_grad[:, columns(p)] = join_heads(query_t).astype(BF16)
        key_acc[g] += dot(score_grads, query)
        value_acc[g] += dot(weights.astype(BF16), grads)
        return carry

    lax.fori_loop(0, pairs, backward, 0)

    low_long = iota((length, PAIR), 1) < HD
    for n, acc in enumerate((key_acc, value_acc)):
        first = acc[0] + pltpu.roll(acc[0], HD, 1)
        second = acc[1] + pltpu.roll(acc[1], HD, 1)
        pair_part[:, n * PAIR : (n + 1) * PAIR] = jnp.where(low_long, first, second).astype(BF16)

    def part_copy(peer, distance):
        return pltpu.make_async_remote_copy(
            src_ref=pair_part.at[pl.ds(pl.multiple_of(peer * tokens, tokens), tokens)],
            dst_ref=pair_in.at[distance],
            send_sem=p_send.at[distance],
            recv_sem=p_recv.at[distance],
            device_id=(dp, peer),
            device_id_type=MESH,
        )

    def send_part(peer, carry):
        part_copy(peer, ctx - peer).start()
        return carry

    lax.fori_loop(0, ctx, send_part, 0)

    wide[...] = jnp.zeros_like(wide)

    def weigh(block):
        first = pl.ds(pl.multiple_of(block * BLOCK, BLOCK), BLOCK)
        sent = grad_out[first].reshape(256, CHUNK).astype(F32)
        got = back_outs[first].reshape(256, CHUNK).astype(F32)
        product = sent * got
        main = jnp.sum(product[:, 0:MAIN], axis=1, keepdims=True)
        spill = jnp.sum(product[:, MAIN:], axis=1, keepdims=True)
        ranks = dot(repeat_main, ranks_of(block))
        found = jnp.where(ranks == main_slot, main, 0.0) + jnp.where(
            ranks == spill_slot, spill, 0.0
        )
        pick_et[first, :] = jnp.sum(found.reshape(BLOCK, ROWS, tokens), axis=1)

    def take_outs(n, carry):
        bytes_of(back_outs, group, y_send, y_recv.at[n]).wait_recv()
        combine(back_outs, n)
        for b in range(group // BLOCK):
            weigh(n * (group // BLOCK) + b)
        return carry

    lax.fori_loop(0, groups, take_outs, 0)
    moe_out[...] = wide[...].astype(BF16)
    dots = pick_et[...]
    weight_grad = jnp.concatenate(
        [
            jnp.sum(
                jnp.where(expert_row == ids_t[k : k + 1, :], dots, 0.0), axis=0, keepdims=True
            )
            for k in range(ids_t.shape[0])
        ],
        axis=0,
    )
    score_grad[...] = (
        weight_grad - jnp.sum(mixing_t * weight_grad, axis=0, keepdims=True)
    ) / total_t

    def add_part(distance, total):
        part_copy(0, distance).wait_recv()
        return total + pair_in[distance].astype(F32)

    pair_sum = lax.fori_loop(1, n_ctx - ctx, add_part, pair_part[here, :].astype(F32))
    key_grad[...] = pair_sum[:, 0:PAIR].astype(BF16)
    value_grad[...] = pair_sum[:, PAIR:].astype(BF16)

    for ref, sem_s, sem_r in (
        (grad_out, g_send, g_recv.at[0]),
        (row_out, x_send, x_recv.at[0]),
        (row_in, r_send, r_recv.at[0]),
        (grad_in, y_send, y_recv.at[0]),
    ):
        bytes_of(ref, count - 1, sem_s, sem_r).wait_send()

    def sent_pair(peer, carry):
        for n in range(2):
            pair_copy(n, peer, ctx).wait_send()
        return carry

    lax.fori_loop(ctx + 1, n_ctx, sent_pair, 0)

    def sent_part(peer, carry):
        part_copy(peer, ctx - peer).wait_send()
        return carry

    lax.fori_loop(0, ctx, sent_part, 0)


def settle_kernel(*refs):
    count = (len(refs) - 2) // 3
    taken, given, held = refs[:count], refs[count : 2 * count], refs[2 * count : 3 * count]
    loads = [pltpu.make_async_copy(taken[n], held[n], refs[-2].at[n]) for n in range(count)]
    stores = [pltpu.make_async_copy(held[n], given[n], refs[-1].at[n]) for n in range(count)]
    for load in loads:
        load.start()
    for load, store in zip(loads, stores):
        load.wait()
        store.start()
    for store in stores:
        store.wait()


def settle(arrays):
    hbm = pl.BlockSpec(memory_space=pltpu.HBM)
    return pl.pallas_call(
        settle_kernel,
        out_shape=tuple(jax.ShapeDtypeStruct(a.shape, a.dtype) for a in arrays),
        in_specs=[hbm] * len(arrays),
        out_specs=[hbm] * len(arrays),
        scratch_shapes=[pltpu.VMEM(a.shape, a.dtype) for a in arrays]
        + [pltpu.SemaphoreType.DMA((len(arrays),))] * 2,
        compiler_params=pltpu.CompilerParams(vmem_limit_bytes=62 * 2**20),
        name="settle",
    )(*arrays)


def shards(
    n_dp,
    n_ctx,
    queries,
    keys,
    values,
    expert_ids,
    router_scores,
    gate_weight,
    up_weight,
    down_weight,
    out_grad,
):
    count = n_dp * n_ctx
    group = max(BLOCK, count // 4)
    groups = count // group
    tokens, width = queries.shape[1:]
    pair_width = keys.shape[2]
    top = expert_ids.shape[2]
    hidden = gate_weight.shape[2]
    length = n_ctx * tokens
    pairs = width // PAIR
    chunk_buf = pltpu.VMEM((count, ROWS, CHUNK), BF16)
    dma = pltpu.SemaphoreType.DMA
    vmem = pl.BlockSpec(memory_space=pltpu.VMEM)
    hbm = pl.BlockSpec(memory_space=pl.ANY)
    canon = pltpu.VMEM((group * 10, width), BF16)
    outs = pl.pallas_call(
        functools.partial(layer_kernel, n_dp, n_ctx, group),
        out_shape=(
            jax.ShapeDtypeStruct((tokens, width), BF16),
            jax.ShapeDtypeStruct((tokens, width), BF16),
            jax.ShapeDtypeStruct((tokens, pair_width), BF16),
            jax.ShapeDtypeStruct((tokens, pair_width), BF16),
            jax.ShapeDtypeStruct((top, tokens), F32),
        ),
        in_specs=[vmem] * 6 + [hbm] * 3,
        out_specs=[vmem] * 5,
        scratch_shapes=[
            pltpu.VMEM((width, hidden), BF16),
            pltpu.VMEM((width, hidden), BF16),
            pltpu.VMEM((hidden, width), BF16),
            chunk_buf,
            chunk_buf,
            chunk_buf,
            chunk_buf,
            chunk_buf,
            chunk_buf,
            canon,
            canon,
            pltpu.VMEM((2 * tokens, MAIN), BF16),
            pltpu.VMEM((count, tokens), F32),
            pltpu.VMEM((2 * tokens, count * ROWS), BF16),
            pltpu.VMEM((tokens, count * ROWS), BF16),
            pltpu.VMEM((length, pair_width), BF16),
            pltpu.VMEM((length, pair_width), BF16),
            pltpu.VMEM((2, length, PAIR), BF16),
            pltpu.VMEM((2, length, PAIR), BF16),
            pltpu.VMEM((2, PAIR, length), BF16),
            pltpu.VMEM((2, PAIR, length), BF16),
            pltpu.VMEM((length, 2 * tokens), F32),
            pltpu.VMEM((tokens, width), BF16),
            pltpu.VMEM((pairs, 1, 2 * tokens), F32),
            pltpu.VMEM((tokens, width), F32),
            pltpu.VMEM((count, tokens), F32),
            pltpu.VMEM((2, length, PAIR), F32),
            pltpu.VMEM((2, length, PAIR), F32),
            pltpu.VMEM((length, 2 * PAIR), BF16),
            pltpu.VMEM((n_ctx, tokens, 2 * PAIR), BF16),
            dma((3,)),
            dma((2, n_ctx)),
            dma((2, n_ctx)),
            dma,
            dma((groups,)),
            dma,
            dma((groups,)),
            dma,
            dma((groups,)),
            dma,
            dma((groups,)),
            dma((n_ctx,)),
            dma((n_ctx,)),
        ],
        compiler_params=pltpu.CompilerParams(
            collective_id=0, has_side_effects=True, vmem_limit_bytes=63 * 2**20
        ),
        name="layer",
    )(
        expert_ids[0].T,
        router_scores[0].T,
        queries[0],
        keys[0],
        values[0],
        out_grad[0],
        gate_weight[0],
        up_weight[0],
        down_weight[0],
    )
    moe_out, query_grad, key_grad, value_grad, score_grad = settle(outs)
    return (
        moe_out[None],
        query_grad[None],
        key_grad[None],
        value_grad[None],
        score_grad.T[None],
    )


def solution(mesh):
    split = P("dp", "ctx", None)
    whole = P(("dp", "ctx"), None, None)
    return jax.shard_map(
        functools.partial(shards, mesh.shape["dp"], mesh.shape["ctx"]),
        mesh=mesh,
        in_specs=(split, split, split, split, split, whole, whole, whole, split),
        out_specs=(split,) * 5,
        check_vma=False,
    )
```
